32 devices in a mesh: blk: 16 (over z, x, core), uly: 2 (over y).
Axes of the slice: x: 2, y: 2, z: 4, core: 2. Of those that a mesh axis runs over, the one named last changes fastest.
Arguments:
- residual: bfloat16 [384, 2048], P(('blk', 'uly')), may hold values from -24 to 24
- query_projection: bfloat16 [384, 4096], P(('blk', 'uly')), may hold values from -51 to 51
- key_projection: bfloat16 [384, 1024], P(('blk', 'uly')), may hold values from -5.1 to 5.1
- value_projection: bfloat16 [384, 1024], P(('blk', 'uly')), may hold values from -6 to 6
- gate_proj: bfloat16 [384, 4096], P(('blk', 'uly')), may hold values from -6 to 6
- positions: int32 [384], replicated, may hold values from 0 to 383, each once
- prefix_len: int32 [1], replicated, may hold values from 48 to 191
- out_weight: bfloat16 [4096, 2048], P('uly', 'blk'), may hold values from -0.375 to 0.375
- norm_gain: float32 [2048], replicated, may hold values from 0.1 to 1.9
- gate_weight: bfloat16 [2048, 6144], P('blk', 'uly'), may hold values from -0.125 to 0.125
- up_weight: bfloat16 [2048, 6144], P('blk', 'uly'), may hold values from -0.125 to 0.125
- down_weight: bfloat16 [6144, 2048], P('uly', 'blk'), may hold values from -0.078125 to 0.078125
Outputs:
- layer_out: bfloat16 [384, 2048], P(('blk', 'uly'))
The draws below stay inside these ranges and needn't reach their ends.
Inputs may be any that keep to these rules, and one draw needn't show every extreme that they name: `positions`: each of 0 to 383 appears once.
All inputs are finite; a program needn't handle non-finite values.
Results may differ from the reference program's by a relative error of at most 0.014.
Values may be sent and summed in bfloat16 or wider, within the bound.
No kernel may reach another device: no remote copies, remote signals or barrier semaphores. Data moves between devices by JAX's collectives and lax.ppermute only.
A program may use at most 128 MiB of HBM per device.

```python
import math
import jax
import jax.numpy as jnp
from jax import lax

D = 2048
QUERY_HEAD_COUNT = 32
KEY_VALUE_HEADS = 8
HEAD_SIZE = 128
FF = 6144
TOK_DEV = 12
SEQUENCE_TOKENS = 384
N_ULY = 2


def attention_parts(key):
    base_key = jax.random.fold_in(key, 4242)
    random_key_sample, query_draw = jax.random.split(base_key, 2)
    key_row_set = jnp.clip(jax.random.normal(random_key_sample, (SEQUENCE_TOKENS, KEY_VALUE_HEADS * HEAD_SIZE), jnp.float32), -3.0, 3.0) * 1.6
    query_rows = jnp.clip(jax.random.normal(query_draw, (SEQUENCE_TOKENS, QUERY_HEAD_COUNT * HEAD_SIZE), jnp.float32), -3.0, 3.0) * 1.6
    return (query_rows, key_row_set)


def draw_query_projection(key, part):
    return attention_parts(key)[0].astype(jnp.bfloat16)


def draw_key_projection(key, part):
    return attention_parts(key)[1].astype(jnp.bfloat16)


def draw_residual(key, part):
    base_key = jax.random.fold_in(key, 515)
    noise_key, row_key, col_key = jax.random.split(base_key, 3)
    row_scale = jnp.exp(jax.random.uniform(row_key, (SEQUENCE_TOKENS, 1), jnp.float32, math.log(0.2), math.log(2.0)))
    col_scale = jnp.exp(jax.random.uniform(col_key, (1, D), jnp.float32, math.log(0.3), math.log(3.0)))
    noise = jnp.clip(jax.random.normal(noise_key, (SEQUENCE_TOKENS, D), jnp.float32), -4.0, 4.0)
    return (noise * row_scale * col_scale).astype(jnp.bfloat16)


def block_levels(stream_key, dims, shards, least, high):
    def one(axis_at, parts):
        draws = jax.random.uniform(jax.random.fold_in(jax.random.fold_in(stream_key, 6), axis_at), (parts,), jnp.float32, least / len(shards), high / len(shards))
        return jnp.repeat(jnp.exp(draws), dims[axis_at] // parts).reshape((-1,) + (1,) * (len(dims) - axis_at - 1))

    level = one(*shards[0])
    for cut in shards[1:]:
        level = level * one(*cut)
    return level


def normal_values(stream_key, shape, scale, bound, cuts=(), dtype=jnp.bfloat16):
    result = scale * jax.random.normal(stream_key, shape, jnp.float32)
    if cuts:
        result = result * block_levels(stream_key, shape, cuts, -0.22, 0.18)
    return jnp.clip(result, -bound, bound).astype(dtype)


def setup_inputs(seed: int = 0) -> dict:
    arg_keys = jax.random.split(jax.random.key(seed), 13)
    return {
        "residual": draw_residual(jax.random.fold_in(arg_keys[12], 71), 0),
        "query_projection": draw_query_projection(jax.random.fold_in(arg_keys[12], 71), 0),
        "key_projection": draw_key_projection(jax.random.fold_in(arg_keys[12], 71), 0),
        "value_projection": normal_values(arg_keys[3], (SEQUENCE_TOKENS, KEY_VALUE_HEADS * HEAD_SIZE), 1.0, 6.0, ((0, 32),)),
        "gate_proj": normal_values(arg_keys[4], (SEQUENCE_TOKENS, QUERY_HEAD_COUNT * HEAD_SIZE), 1.5, 6.0, ((0, 32),)),
        "positions": jax.random.permutation(arg_keys[5], SEQUENCE_TOKENS).astype(jnp.int32),
        "prefix_len": jax.random.randint(arg_keys[6], (1,), SEQUENCE_TOKENS // 8, SEQUENCE_TOKENS // 2).astype(jnp.int32),
        "out_weight": normal_values(arg_keys[7], (QUERY_HEAD_COUNT * HEAD_SIZE, D), (QUERY_HEAD_COUNT * HEAD_SIZE // 16) ** -0.5, 0.375, ((0, 2), (1, 16))),
        "norm_gain": jnp.clip(1.0 + 0.18 * jax.random.normal(arg_keys[8], (D,), jnp.float32), 0.1, 1.9),
        "gate_weight": normal_values(arg_keys[9], (D, FF), D ** -0.5, 0.125, ((0, 16), (1, 2))),
        "up_weight": normal_values(arg_keys[10], (D, FF), D ** -0.5, 0.125, ((0, 16), (1, 2))),
        "down_weight": normal_values(arg_keys[11], (FF, D), FF ** -0.5, 0.078125, ((0, 2), (1, 16))),
    }


def rounded_parts(left, right, groups):
    width = left.shape[1] // groups
    total = jnp.zeros((left.shape[0], right.shape[1]), jnp.float32)
    for group in range(groups):
        piece = jnp.dot(left[:, group * width:(group + 1) * width], right[group * width:(group + 1) * width, :], preferred_element_type=jnp.float32)
        total = total + lax.optimization_barrier(piece.astype(jnp.bfloat16)).astype(jnp.float32)
    return total

def reference(residual, query_projection, key_projection, value_projection, gate_proj, positions, prefix_len, out_weight, norm_gain, gate_weight, up_weight, down_weight):
    heads_per_group = QUERY_HEAD_COUNT // KEY_VALUE_HEADS
    score_scale = 1.0 / math.sqrt(HEAD_SIZE)
    rows_per_block = TOK_DEV * N_ULY
    count_of_blocks = SEQUENCE_TOKENS // rows_per_block
    gathered_keys = key_projection.astype(jnp.float32).reshape(SEQUENCE_TOKENS, KEY_VALUE_HEADS, HEAD_SIZE)
    gathered_values = value_projection.astype(jnp.float32).reshape(SEQUENCE_TOKENS, KEY_VALUE_HEADS, HEAD_SIZE)
    prefix = prefix_len[0]
    query_block_list = query_projection.reshape(count_of_blocks, rows_per_block, KEY_VALUE_HEADS, heads_per_group, HEAD_SIZE)
    pos_blocks = positions.reshape(count_of_blocks, rows_per_block)

    def attend_block(pieces):
        query_part, query_pos = pieces
        scores = jnp.einsum('bkgd,skd->bkgs', query_part.astype(jnp.float32), gathered_keys) * score_scale
        visible = (positions[None, :] <= query_pos[:, None]) | (positions[None, :] < prefix)
        scores = jnp.where(visible[:, None, None, :], scores, -jnp.inf)
        row_max = lax.optimization_barrier(jnp.max(scores, axis=-1, keepdims=True))
        exp_scores = jnp.exp(scores - row_max)
        denom = lax.optimization_barrier(jnp.sum(exp_scores, axis=-1))
        probs = lax.optimization_barrier(exp_scores.astype(jnp.bfloat16)).astype(jnp.float32)
        summed = jnp.einsum('bkgs,skd->bkgd', probs, gathered_values)
        return (summed / denom[..., None]).reshape(rows_per_block, QUERY_HEAD_COUNT * HEAD_SIZE)
    attended = lax.map(attend_block, (query_block_list, pos_blocks)).reshape(SEQUENCE_TOKENS, QUERY_HEAD_COUNT * HEAD_SIZE)
    gated_out = (attended * jax.nn.sigmoid(gate_proj.astype(jnp.float32))).astype(jnp.bfloat16)
    projected = rounded_parts(gated_out, out_weight, N_ULY)
    hidden_sum = (residual.astype(jnp.float32) + projected).astype(jnp.bfloat16)
    hidden_f = hidden_sum.astype(jnp.float32)
    mean_sq = lax.optimization_barrier(jnp.mean(hidden_f * hidden_f, axis=-1, keepdims=True))
    normed = (hidden_f * lax.rsqrt(mean_sq + 1e-06) * norm_gain.astype(jnp.float32)).astype(jnp.bfloat16)
    gate_sum = jnp.dot(normed, gate_weight, preferred_element_type=jnp.float32)
    up_sum = jnp.dot(normed, up_weight, preferred_element_type=jnp.float32)
    activated = (jax.nn.silu(gate_sum) * up_sum).astype(jnp.bfloat16)
    ffn_out = rounded_parts(activated, down_weight, N_ULY)
    return (hidden_f + ffn_out).astype(jnp.bfloat16)
```

```python
import functools
import math

import jax
import jax.numpy as jnp
import numpy as np
from jax import lax
from jax.experimental import pallas as pl
from jax.experimental.pallas import tpu as pltpu
from jax.sharding import PartitionSpec as P

HEAD_SIZE = 128
ROW_TILE = 16
HIDE = -1e30
NO_POSITION = np.iinfo(np.int32).max
F32 = jnp.float32
BF16 = jnp.bfloat16
VMEM = pl.BlockSpec(memory_space=pltpu.VMEM)
SMEM = pl.BlockSpec(memory_space=pltpu.SMEM)
NT = (((1,), (1,)), ((), ()))


def move_weights(
    residual,
    query_projection,
    key_projection,
    value_projection,
    gate_proj,
    positions,
    prefix_len,
    out_weight,
    norm_gain,
    gate_weight,
    up_weight,
    down_weight,
):
    q_loc, k_loc, v_loc, g_loc = (
        lax.all_to_all(query_projection, "uly", split_axis=1, concat_axis=0, tiled=True),
        lax.all_to_all(key_projection, "uly", split_axis=1, concat_axis=0, tiled=True),
        lax.all_to_all(value_projection, "uly", split_axis=1, concat_axis=0, tiled=True),
        lax.all_to_all(gate_proj, "uly", split_axis=1, concat_axis=0, tiled=True),
    )
    row_count = q_loc.shape[0]
    kv_heads = k_loc.shape[1] // HEAD_SIZE
    q_heads = q_loc.shape[1] // HEAD_SIZE
    heads_per_group = q_heads // kv_heads
    score_scale = 1.0 / math.sqrt(HEAD_SIZE)
    blk_index = lax.axis_index("blk")
    query_pos = lax.dynamic_slice_in_dim(positions, blk_index * row_count, row_count)
    prefix = prefix_len[0]
    query_heads = q_loc.reshape(row_count, kv_heads, heads_per_group, HEAD_SIZE)
    wo_full, wg_full, wu_full, wd_full = (
        lax.all_gather(out_weight, "blk", axis=1, tiled=True),
        lax.all_gather(gate_weight, "blk", axis=0, tiled=True),
        lax.all_gather(up_weight, "blk", axis=0, tiled=True),
        lax.all_gather(down_weight, "blk", axis=1, tiled=True),
    )
    key_part = lax.all_gather(k_loc, "blk", axis=0, tiled=True)
    value_part = lax.all_gather(v_loc, "blk", axis=0, tiled=True)
    key_count = key_part.shape[0]
    scores = (
        jnp.einsum(
            "bkgd,skd->bkgs",
            query_heads,
            key_part.reshape(key_count, kv_heads, HEAD_SIZE),
            preferred_element_type=F32,
        )
        * score_scale
    )
    visible = (positions[None, :] <= query_pos[:, None]) | (positions[None, :] < prefix)
    scores = jnp.where(visible[:, None, None, :], scores, -jnp.inf)
    row_max = jnp.max(scores, axis=-1)
    exp_scores = jnp.exp(scores - row_max[..., None])
    denom = jnp.sum(exp_scores, axis=-1)
    probs = exp_scores.astype(BF16)
    weighted = jnp.einsum(
        "bkgs,skd->bkgd",
        probs,
        value_part.reshape(key_count, kv_heads, HEAD_SIZE),
        preferred_element_type=F32,
    )
    attended = (weighted / denom[..., None]).reshape(row_count, q_heads * HEAD_SIZE)
    gated_out = (attended * jax.nn.sigmoid(g_loc.astype(F32))).astype(BF16)
    head_partial = jnp.dot(gated_out, wo_full, preferred_element_type=F32)
    projected = lax.psum_scatter(
        head_partial.astype(BF16), "uly", scatter_dimension=0, tiled=True
    ).astype(F32)
    hidden_f = (residual.astype(F32) + projected).astype(BF16).astype(F32)
    mean_sq = jnp.mean(hidden_f * hidden_f, axis=-1, keepdims=True)
    normed = (hidden_f * lax.rsqrt(mean_sq + 1e-06) * norm_gain).astype(BF16)
    group_rows = lax.all_gather(normed, "uly", axis=0, tiled=True)
    gate_sum = jnp.dot(group_rows, wg_full, preferred_element_type=F32)
    up_sum = jnp.dot(group_rows, wu_full, preferred_element_type=F32)
    activated = (jax.nn.silu(gate_sum) * up_sum).astype(BF16)
    ffn_partial = jnp.dot(activated, wd_full, preferred_element_type=F32)
    ffn_out = lax.psum_scatter(
        ffn_partial.astype(BF16), "uly", scatter_dimension=0, tiled=True
    ).astype(F32)
    return (hidden_f + ffn_out).astype(BF16)


def dot(a, b):
    return jnp.dot(a, b, preferred_element_type=F32)


def attention_kernel(heads, planes, idx, qg, *refs):
    kvs, bias, pick, out = refs[:planes], refs[planes], refs[planes + 1], refs[planes + 2]
    group, rows, _ = qg.shape
    r = idx[1]
    keys = jnp.concatenate([kv[:, :, :HEAD_SIZE].reshape(group * rows, HEAD_SIZE) for kv in kvs])
    values = jnp.concatenate([kv[:, :, HEAD_SIZE:].reshape(group * rows, HEAD_SIZE) for kv in kvs])
    scale = 1.0 / math.sqrt(HEAD_SIZE)
    done = []
    for h in range(heads):
        at = slice(h * HEAD_SIZE, (h + 1) * HEAD_SIZE)
        gate_at = slice((heads + h) * HEAD_SIZE, (heads + h + 1) * HEAD_SIZE)
        q = jnp.concatenate([qg[b ^ r, :, at] for b in range(group)])
        gate = jnp.concatenate([qg[b ^ r, :, gate_at] for b in range(group)]).astype(F32)
        s = lax.dot_general(q, keys, NT, preferred_element_type=F32) * scale + bias[...]
        e = jnp.exp(s - jnp.max(s, axis=-1, keepdims=True))
        denom = jnp.sum(e, axis=-1, keepdims=True)
        attended = dot(e.astype(BF16), values) / denom
        done.append((attended / (1.0 + jnp.exp(-gate))).astype(BF16))
    out[...] = dot(pick[...], jnp.concatenate(done, axis=1)).astype(BF16)


def project_kernel(planes, idx, *refs):
    parts = refs[:planes]
    weight, pick, keep, send, held = refs[planes:]
    z = idx[0]
    for k in range(planes):
        held[z ^ k] = parts[k][...]
    rows, width = parts[0].shape
    x = dot(pick[...], held[...].reshape(planes * rows, width)).astype(BF16)
    w = jnp.concatenate([weight[c] for c in range(weight.shape[0])], axis=1)
    y = dot(x, w).astype(BF16)
    half = y.shape[0] // 2
    keep[...] = y[:half]
    send[...] = y[half:]


def core_sum_kernel(keep, got, *outs):
    rows = outs[0].shape[0]
    for i, out in enumerate(outs):
        at = slice(i * rows, (i + 1) * rows)
        out[...] = (keep[at].astype(F32) + got[at].astype(F32)).astype(out.dtype)


def sum_kernel(*refs):
    *parts, out = refs
    total = parts[0][...].astype(F32)
    for part in parts[1:]:
        total = total + part[...].astype(F32)
    out[...] = total.astype(out.dtype)


def norm_kernel(planes, idx, *refs):
    parts, gain, out = refs[:planes], refs[planes], refs[planes + 1]
    z = idx[0]
    width = parts[0].shape[1]
    held = [p[...].astype(F32) for p in parts]
    square = sum(jnp.sum(h * h, axis=-1, keepdims=True) for h in held)
    factor = lax.rsqrt(square / (width * planes) + 1e-06)
    for k in range(planes):
        out[z ^ k] = (held[k] * factor * gain[z ^ k]).astype(BF16)


def ffn_kernel(blocks, *refs):
    parts, (gate_up, down, keep, send) = refs[:blocks], refs[blocks:]
    planes = parts[0].shape[0]
    sources, both, _ = gate_up.shape
    units = both // 2
    per = sources // planes
    gate = up = 0.0
    for p in range(planes):
        x = jnp.concatenate([part[p] for part in parts])
        w = jnp.concatenate([gate_up[p * per + i] for i in range(per)], axis=1)
        gate = gate + lax.dot_general(x, w[:units], NT, preferred_element_type=F32)
        up = up + lax.dot_general(x, w[units:], NT, preferred_element_type=F32)
    activated = (gate / (1.0 + jnp.exp(-gate)) * up).astype(BF16)
    half = activated.shape[0] // 2
    width = per * down.shape[2]
    for p in range(planes):
        w = jnp.concatenate([down[p * per + i] for i in range(per)], axis=1)
        y = dot(activated, w).astype(BF16)
        keep[:, p * width:(p + 1) * width] = y[:half]
        send[:, p * width:(p + 1) * width] = y[half:]


def row_of(z, k, tokens, rows, total):
    i = lax.broadcasted_iota(jnp.int32, (rows, total), 0)
    j = lax.broadcasted_iota(jnp.int32, (rows, total), 1)
    return jnp.where((j == i + (z ^ k) * tokens) & (i < tokens), 1.0, 0.0).astype(BF16)


def plane_sum_kernel(planes, tokens, idx, *refs):
    parts, outs = refs[:-planes], refs[-planes:]
    total = parts[0][...].astype(F32)
    for part in parts[1:]:
        total = total + part[...].astype(F32)
    total = total.astype(BF16)
    for k, out in enumerate(outs):
        pick = row_of(idx[0], k, tokens, out.shape[0], total.shape[0])
        out[...] = dot(pick, total).astype(BF16)


def last_kernel(planes, tokens, idx, *refs):
    parts, hidden, out = refs[:planes], refs[planes:-1], refs[-1]
    total = parts[0][...].astype(F32)
    for part in parts[1:]:
        total = total + part[...].astype(F32)
    z = idx[0]
    pick = row_of(z, 0, tokens, total.shape[0], hidden[0].shape[0])
    held = jnp.concatenate([dot(pick, h[...]) for h in hidden], axis=1)
    width = hidden[0].shape[1]
    whole = jnp.zeros_like(total)
    for k in range(planes):
        at = pl.ds(pl.multiple_of((z ^ k) * width, width), width)
        out[:, at] = held[:tokens, k * width:(k + 1) * width].astype(BF16)
    out[...] = (out[...].astype(F32) + total[:tokens]).astype(BF16)


def call(kernel, outs, *args, scratch=()):
    single = not isinstance(outs, list)
    shapes = [outs] if single else outs
    got = pl.pallas_call(
        kernel,
        out_shape=shapes,
        in_specs=[SMEM if a.dtype == jnp.int32 else VMEM for a in args],
        out_specs=[VMEM] * len(shapes),
        scratch_shapes=list(scratch),
        compiler_params=pltpu.CompilerParams(vmem_limit_bytes=40 * 2**20),
    )(*args)
    return got[0] if single else got


def like(*shape, dtype=BF16):
    return jax.ShapeDtypeStruct(shape, dtype)


def move_tokens(
    n_blk,
    n_uly,
    residual,
    query_projection,
    key_projection,
    value_projection,
    gate_proj,
    positions,
    prefix_len,
    out_weight,
    norm_gain,
    gate_weight,
    up_weight,
    down_weight,
):
    axes = ("blk", "uly")
    kv_heads = key_projection.shape[1] // HEAD_SIZE
    heads = query_projection.shape[1] // key_projection.shape[1]
    tokens, features = residual.shape
    rows = -(-tokens // ROW_TILE) * ROW_TILE
    group = kv_heads
    per = group // n_uly
    planes = n_blk // per
    devices = n_blk * n_uly
    me = lax.axis_index("blk") * n_uly + lax.axis_index("uly")
    z, r = me // group, me % group
    idx = jnp.stack([z, r]).astype(jnp.int32)
    core = n_uly
    near = [b for b in range(group) if not b & core]
    order = near + [b ^ core for b in near]
    steps = near[1:]

    def swap(x, mask):
        return lax.ppermute(x, axes, [(i, i ^ mask) for i in range(devices)])

    def swap_planes(x):
        return [swap(x, k * group) for k in range(1, planes)]

    def by_head(x):
        x = x.reshape(tokens, n_uly, per, x.shape[1] // group)
        return x.transpose(2, 1, 0, 3).reshape(group, tokens, x.shape[3])

    def packed(*xs):
        x = jnp.concatenate([by_head(x) for x in xs], axis=2)
        return jnp.pad(x, ((0, 0), (0, rows - tokens), (0, 0)))

    plane_groups = [[p * group + i for i in range(group)] for p in range(planes)]

    def plane_exchange(x):
        return lax.all_to_all(x, axes, 0, 0, axis_index_groups=plane_groups, tiled=True)

    kv = plane_exchange(packed(key_projection, value_projection))
    qg = plane_exchange(packed(query_projection, gate_proj))

    wo = lax.all_to_all(
        out_weight.reshape(per, out_weight.shape[0] // per, out_weight.shape[1]),
        "blk", 0, 0,
        axis_index_groups=[[p * per + i for i in range(per)] for p in range(planes)],
        tiled=True,
    )
    units = gate_weight.shape[1] // n_blk

    def by_unit(w):
        return w.reshape(w.shape[0], n_blk, units).transpose(1, 2, 0)

    gate_up = lax.all_to_all(
        jnp.concatenate([by_unit(gate_weight), by_unit(up_weight)], axis=1), "blk", 0, 0, tiled=True
    )
    down = lax.all_to_all(
        down_weight.reshape(n_blk, units, down_weight.shape[1]), "blk", 0, 0, tiled=True
    )
    width = features // planes
    resid = lax.all_to_all(
        residual.reshape(tokens, planes, width).transpose(1, 0, 2),
        "blk", 0, 0,
        axis_index_groups=[[p * per + i for p in range(planes)] for i in range(per)],
        tiled=True,
    ).reshape(planes * tokens, width)

    spots = jnp.pad(
        positions.reshape(planes, group, tokens),
        ((0, 0), (0, 0), (0, rows - tokens)),
        constant_values=NO_POSITION,
    )
    key_spot = spots[z ^ jnp.arange(planes)].reshape(1, -1)
    query_spot = spots[z][r ^ jnp.arange(group)].reshape(-1, 1)
    visible = (key_spot <= query_spot) | (key_spot < prefix_len[0])
    bias = jnp.where(visible, 0.0, HIDE).astype(F32)

    pick = np.zeros((group, tokens, group, rows), np.float32)
    for b in range(group):
        for t in range(tokens):
            pick[b, t, b, t] = 1
    pick = jnp.asarray(pick.reshape(group * tokens, group * rows), BF16)
    gated = call(
        functools.partial(attention_kernel, heads, planes),
        like(group * tokens, heads * HEAD_SIZE),
        idx, qg, kv, *swap_planes(kv), bias, pick,
    )

    turn = np.zeros((group, planes, tokens, planes, group, tokens), np.float32)
    for i, b in enumerate(order):
        for p in range(planes):
            for t in range(tokens):
                turn[i, p, t, p, b, t] = 1
    total = devices * tokens
    turn = jnp.asarray(turn.reshape(total, total), BF16)
    keep, send = call(
        functools.partial(project_kernel, planes),
        [like(total // 2, width)] * 2,
        idx, gated, *swap_planes(gated), wo, turn,
        scratch=[pltpu.VMEM((planes,) + gated.shape, BF16)],
    )
    share = total // group
    own, *rest = call(
        core_sum_kernel,
        [like(share, width, dtype=F32)] + [like(share, width)] * len(steps),
        keep, swap(send, core),
    )
    hidden = call(
        sum_kernel, like(share, width), own, resid, *[swap(x, b) for x, b in zip(rest, steps)]
    )
    hiddens = [hidden] + swap_planes(hidden)
    normed = call(
        functools.partial(norm_kernel, planes),
        like(planes, share, width),
        idx, *hiddens, norm_gain.reshape(planes, 1, width),
    )
    blocks = [normed] + [swap(normed, b) for b in steps]
    blocks = blocks + [swap(x, core) for x in blocks]
    keep, send = call(
        functools.partial(ffn_kernel, group),
        [like(total // 2, features)] * 2,
        *blocks, gate_up, down,
    )
    own, *rest = call(
        core_sum_kernel,
        [like(share, features, dtype=F32)] + [like(share, features)] * len(steps),
        keep, swap(send, core),
    )
    parts = call(
        functools.partial(plane_sum_kernel, planes, tokens),
        [like(rows, features)] * planes,
        idx, own, *[swap(x, b) for x, b in zip(rest, steps)],
    )
    return call(
        functools.partial(last_kernel, planes, tokens),
        like(tokens, features),
        idx, parts[0], *[swap(x, k * group) for k, x in enumerate(parts) if k], *hiddens,
    )


def tokens_can_travel(n_blk, n_uly, kv_heads, token_count, unit_count):
    def power(n):
        return n > 0 and not n & (n - 1)

    per = kv_heads // n_uly
    return (
        power(n_blk)
        and power(n_uly)
        and power(kv_heads)
        and per > 1
        and n_blk % per == 0
        and token_count < unit_count // n_uly
    )


def solution(mesh):
    n_blk, n_uly = mesh.shape["blk"], mesh.shape["uly"]

    def per_device(*args):
        residual, key_projection, gate_weight = args[0], args[2], args[9]
        travel = tokens_can_travel(
            n_blk,
            n_uly,
            key_projection.shape[1] // HEAD_SIZE,
            residual.shape[0] * n_blk * n_uly,
            gate_weight.shape[1] * n_uly,
        )
        if travel:
            return move_tokens(n_blk, n_uly, *args)
        return move_weights(*args)

    return jax.shard_map(
        per_device,
        mesh=mesh,
        in_specs=(
            P(("blk", "uly"), None),
            P(("blk", "uly"), None),
            P(("blk", "uly"), None),
            P(("blk", "uly"), None),
            P(("blk", "uly"), None),
            P(),
            P(),
            P("uly", "blk"),
            P(),
            P("blk", "uly"),
            P("blk", "uly"),
            P("uly", "blk"),
        ),
        out_specs=P(("blk", "uly"), None),
        check_vma=False,
    )
```

```python
import functools
import math

import jax
import jax.numpy as jnp
import numpy as np
from jax import lax
from jax.experimental import pallas as pl
from jax.experimental.pallas import tpu as pltpu
from jax.sharding import PartitionSpec as P

HEAD_SIZE = 128
ROW_TILE = 16
HIDE = -1e30
NO_POSITION = float(2**30)
F32 = jnp.float32
BF16 = jnp.bfloat16
VMEM = pl.BlockSpec(memory_space=pltpu.VMEM)
SMEM = pl.BlockSpec(memory_space=pltpu.SMEM)
NT = (((1,), (1,)), ((), ()))


def move_weights(
    residual,
    query_projection,
    key_projection,
    value_projection,
    gate_proj,
    positions,
    prefix_len,
    out_weight,
    norm_gain,
    gate_weight,
    up_weight,
    down_weight,
):
    q_loc, k_loc, v_loc, g_loc = (
        lax.all_to_all(query_projection, "uly", split_axis=1, concat_axis=0, tiled=True),
        lax.all_to_all(key_projection, "uly", split_axis=1, concat_axis=0, tiled=True),
        lax.all_to_all(value_projection, "uly", split_axis=1, concat_axis=0, tiled=True),
        lax.all_to_all(gate_proj, "uly", split_axis=1, concat_axis=0, tiled=True),
    )
    row_count = q_loc.shape[0]
    kv_heads = k_loc.shape[1] // HEAD_SIZE
    q_heads = q_loc.shape[1] // HEAD_SIZE
    heads_per_group = q_heads // kv_heads
    score_scale = 1.0 / math.sqrt(HEAD_SIZE)
    blk_index = lax.axis_index("blk")
    query_pos = lax.dynamic_slice_in_dim(positions, blk_index * row_count, row_count)
    prefix = prefix_len[0]
    query_heads = q_loc.reshape(row_count, kv_heads, heads_per_group, HEAD_SIZE)
    wo_full, wg_full, wu_full, wd_full = (
        lax.all_gather(out_weight, "blk", axis=1, tiled=True),
        lax.all_gather(gate_weight, "blk", axis=0, tiled=True),
        lax.all_gather(up_weight, "blk", axis=0, tiled=True),
        lax.all_gather(down_weight, "blk", axis=1, tiled=True),
    )
    key_part = lax.all_gather(k_loc, "blk", axis=0, tiled=True)
    value_part = lax.all_gather(v_loc, "blk", axis=0, tiled=True)
    key_count = key_part.shape[0]
    scores = (
        jnp.einsum(
            "bkgd,skd->bkgs",
            query_heads,
            key_part.reshape(key_count, kv_heads, HEAD_SIZE),
            preferred_element_type=F32,
        )
        * score_scale
    )
    visible = (positions[None, :] <= query_pos[:, None]) | (positions[None, :] < prefix)
    scores = jnp.where(visible[:, None, None, :], scores, -jnp.inf)
    row_max = jnp.max(scores, axis=-1)
    exp_scores = jnp.exp(scores - row_max[..., None])
    denom = jnp.sum(exp_scores, axis=-1)
    probs = exp_scores.astype(BF16)
    weighted = jnp.einsum(
        "bkgs,skd->bkgd",
        probs,
        value_part.reshape(key_count, kv_heads, HEAD_SIZE),
        preferred_element_type=F32,
    )
    attended = (weighted / denom[..., None]).reshape(row_count, q_heads * HEAD_SIZE)
    gated_out = (attended * jax.nn.sigmoid(g_loc.astype(F32))).astype(BF16)
    head_partial = jnp.dot(gated_out, wo_full, preferred_element_type=F32)
    projected = lax.psum_scatter(
        head_partial.astype(BF16), "uly", scatter_dimension=0, tiled=True
    ).astype(F32)
    hidden_f = (residual.astype(F32) + projected).astype(BF16).astype(F32)
    mean_sq = jnp.mean(hidden_f * hidden_f, axis=-1, keepdims=True)
    normed = (hidden_f * lax.rsqrt(mean_sq + 1e-06) * norm_gain).astype(BF16)
    group_rows = lax.all_gather(normed, "uly", axis=0, tiled=True)
    gate_sum = jnp.dot(group_rows, wg_full, preferred_element_type=F32)
    up_sum = jnp.dot(group_rows, wu_full, preferred_element_type=F32)
    activated = (jax.nn.silu(gate_sum) * up_sum).astype(BF16)
    ffn_partial = jnp.dot(activated, wd_full, preferred_element_type=F32)
    ffn_out = lax.psum_scatter(
        ffn_partial.astype(BF16), "uly", scatter_dimension=0, tiled=True
    ).astype(F32)
    return (hidden_f + ffn_out).astype(BF16)


def dot(a, b):
    return jnp.dot(a, b, preferred_element_type=F32)


def pack_heads_kernel(head_of, *refs):
    *parts, out = refs
    tokens = parts[0].shape[0]
    out[...] = jnp.zeros_like(out)
    for r, j in enumerate(head_of):
        start = 0
        for part in parts:
            width = part.shape[1] // len(head_of)
            out[r, :tokens, start:start + width] = part[:, j * width:(j + 1) * width]
            start += width


def message_kernel(planes, idx, heads, residual, *outs):
    group, rows, whole = heads.shape
    tokens, features = residual.shape
    pair = 2 * HEAD_SIZE
    lot = group * rows
    width = features // planes
    z = idx[0]
    keys = heads[:, :, whole - pair:].reshape(lot, pair)
    for k, out in enumerate(outs):
        out[:lot] = keys
        out[lot:] = jnp.zeros((out.shape[0] - lot, pair), BF16)
        for c in range(width // pair):
            at = pl.ds(pl.multiple_of((z ^ k) * width + c * pair, pair), pair)
            out[lot + c * rows:lot + c * rows + tokens] = residual[:, at]


def attention_kernel(heads, planes, idx, prefix, qg, *refs):
    messages, (spots, pick, out) = refs[:planes], refs[planes:]
    group, rows, _ = qg.shape
    z, r = idx[0], idx[1]
    lot = group * rows
    keys, values, key_spot = [], [], []
    for k in range(planes):
        keys.append(messages[k][:lot, :HEAD_SIZE])
        values.append(messages[k][:lot, HEAD_SIZE:])
        key_spot.append(spots[z ^ k])
    keys, values = jnp.concatenate(keys), jnp.concatenate(values)
    key_spot = jnp.concatenate(key_spot, axis=1)
    i = lax.broadcasted_iota(jnp.int32, (lot, lot), 0)
    j = lax.broadcasted_iota(jnp.int32, (lot, lot), 1)
    own = jnp.where((i ^ (r * rows)) == j, spots[z], 0.0)
    query_spot = jnp.sum(own, axis=1, keepdims=True)
    visible = (key_spot <= query_spot) | (key_spot < prefix[0].astype(F32))
    bias = jnp.where(visible, 0.0, HIDE)
    scale = 1.0 / math.sqrt(HEAD_SIZE)
    done = []
    for h in range(heads):
        at = slice(h * HEAD_SIZE, (h + 1) * HEAD_SIZE)
        gate_at = slice((heads + h) * HEAD_SIZE, (heads + h + 1) * HEAD_SIZE)
        q = jnp.concatenate([qg[b ^ r, :, at] for b in range(group)])
        gate = jnp.concatenate([qg[b ^ r, :, gate_at] for b in range(group)]).astype(F32)
        s = lax.dot_general(q, keys, NT, preferred_element_type=F32) * scale + bias
        e = jnp.exp(s - jnp.max(s, axis=-1, keepdims=True))
        denom = jnp.sum(e, axis=-1, keepdims=True)
        attended = dot(e.astype(BF16), values) / denom
        done.append((attended / (1.0 + jnp.exp(-gate))).astype(BF16))
    out[...] = dot(pick[...], jnp.concatenate(done, axis=1)).astype(BF16)


def project_kernel(planes, idx, *refs):
    parts = refs[:planes]
    weights, (pick, keep, send, held, wide) = refs[planes:-5], refs[-5:]
    z, q = idx[0], idx[2]
    for k in range(planes):
        held[z ^ k] = parts[k][...]
    rows, width = parts[0].shape
    x = dot(pick[...], held[...].reshape(planes * rows, width)).astype(BF16)
    lanes = weights[0].shape[1]
    for c, weight in enumerate(weights):
        wide[:, pl.ds(pl.multiple_of((q ^ c) * lanes, lanes), lanes)] = weight[...]
    y = dot(x, wide[...]).astype(BF16)
    half = y.shape[0] // 2
    keep[...] = y[:half]
    send[...] = y[half:]


def core_sum_kernel(keep, got, *outs):
    rows = outs[0].shape[0]
    for i, out in enumerate(outs):
        at = slice(i * rows, (i + 1) * rows)
        out[...] = (keep[at].astype(F32) + got[at].astype(F32)).astype(out.dtype)


def hidden_kernel(planes, tokens, idx, *refs):
    parts, messages, out = refs[:-planes - 1], refs[-planes - 1:-1], refs[-1]
    total = parts[0][...]
    for part in parts[1:]:
        total = total + part[...].astype(F32)
    width = out.shape[1]
    pair = messages[0].shape[1]
    pieces = width // pair
    rows = -(-tokens // ROW_TILE) * ROW_TILE
    for k, message in enumerate(messages):
        i = lax.broadcasted_iota(jnp.int32, (out.shape[0], rows), 0)
        j = lax.broadcasted_iota(jnp.int32, (out.shape[0], rows), 1)
        place = jnp.where((i == j + (idx[0] ^ k) * tokens) & (j < tokens), 1.0, 0.0).astype(BF16)
        lot = message.shape[0] - pieces * rows
        held = [message[lot + c * rows:lot + (c + 1) * rows] for c in range(pieces)]
        total = total + dot(place, jnp.concatenate(held, axis=1))
    out[...] = total.astype(BF16)


def stack_kernel(*refs):
    *parts, out = refs
    for k, part in enumerate(parts):
        out[k] = part[...]


def split_gate_up_kernel(planes, sides, idx, gate, up, *outs):
    half = planes // 2
    units = outs[0].shape[1] // 4
    side, near, far = idx[3], idx[0] % half, idx[0] // half
    for k in range(half):
        for c in range(sides):
            chip = (near ^ k) * sides + (side ^ c)
            for i in range(2):
                start = pl.multiple_of((chip * 2 + (far ^ i)) * units, units)
                out = outs[k * sides + c]
                out[:, 2 * i * units:(2 * i + 1) * units] = gate[:, pl.ds(start, units)]
                out[:, (2 * i + 1) * units:(2 * i + 2) * units] = up[:, pl.ds(start, units)]


def split_down_kernel(planes, idx, weight, *outs):
    half = planes // 2
    sides = len(outs)
    units = outs[0].shape[1]
    for k in range(planes):
        z = idx[0] ^ k
        for c, out in enumerate(outs):
            chip = (z % half) * sides + (idx[3] ^ c)
            start = pl.multiple_of((chip * 2 + z // half) * units, units)
            out[k] = weight[pl.ds(start, units), :]


def regroup_kernel(*refs):
    many = refs[-1].shape[0]
    parts, outs = refs[:many], refs[many:]
    for k, out in enumerate(outs):
        for c, part in enumerate(parts):
            out[c] = part[k]


def gate_up_kernel(blocks, per, idx, *refs):
    parts, pieces = refs[:blocks], refs[blocks:-4]
    gain, keep, send, held = refs[-4:]
    half, share, width = parts[0].shape
    lanes = width // per
    z, q = idx[0], idx[2]
    total = square = 0.0
    for k in range(half):
        x = jnp.concatenate([part[k] for part in parts]).astype(F32)
        square = square + jnp.sum(x * x, axis=1, keepdims=True)
        held[k] = (x * gain[z ^ k]).astype(BF16)
        x = [held[k, :, pl.ds(pl.multiple_of((q ^ c) * lanes, lanes), lanes)] for c in range(per)]
        w = jnp.concatenate([pieces[k * per + c][...] for c in range(per)])
        total = total + dot(jnp.concatenate(x, axis=1), w)
    columns = total.shape[1] // 2
    lane = lax.broadcasted_iota(jnp.int32, (blocks * share, HEAD_SIZE), 1)
    keep[:, :columns] = total[:, :columns]
    keep[:, columns:] = jnp.where(lane == 0, square, 0.0)
    send[:, :columns] = total[:, columns:].astype(BF16)
    high = square.astype(BF16).astype(F32)
    low = square - high
    send[:, columns:] = jnp.where(lane == 0, high, jnp.where(lane == 1, low, 0.0)).astype(BF16)


def down_kernel(planes, per, features, idx, keep, got, *refs):
    pieces, own, sends = refs[:planes * 2], refs[planes * 2], refs[planes * 2 + 1:]
    total = keep[...] + got[...].astype(F32)
    units = (total.shape[1] - HEAD_SIZE) // 2
    square = jnp.sum(total[:, 2 * units:], axis=1, keepdims=True)
    factor = lax.rsqrt(square / features + 1e-06)
    gate, up = total[:, :units] * factor, total[:, units:2 * units] * factor
    activated = (gate / (1.0 + jnp.exp(-gate)) * up).astype(BF16)
    z, q = idx[0], idx[2]
    rows = own.shape[1]
    sides = per // 2
    for k in range(planes):
        w = [pieces[(c % 2) * planes + k][c // 2] for c in range(per)]
        y = dot(activated, jnp.concatenate(w, axis=1))
        lanes = w[0].shape[1]
        for c in range(per):
            at = pl.ds(pl.multiple_of((q ^ c) * lanes, lanes), lanes)
            block = y[:, c * lanes:(c + 1) * lanes]
            own[z ^ k, :, at] = block[:rows]
            for i, send in enumerate(sends):
                send[z ^ k, :, at] = block[(i + 1) * rows:(i + 2) * rows].astype(BF16)


def head_rows_kernel(idx, weight, *outs):
    rows = outs[0].shape[0]
    for c, out in enumerate(outs):
        out[...] = weight[pl.ds(pl.multiple_of((idx[2] ^ c) * rows, rows), rows), :]


def split_kernel(planes, wide, nearest, idx, weight, *outs):
    sides = len(outs) if not nearest else outs[0].shape[0]
    units = outs[0].shape[2 if wide else 1]
    for k in range(planes):
        for c in range(sides):
            chip = (idx[0] ^ k) * sides + (idx[3] ^ c)
            at = pl.ds(pl.multiple_of(chip * units, units), units)
            block = weight[:, at] if wide else weight[at, :]
            if nearest:
                outs[k][c] = block
            else:
                outs[c][k] = block


def regroup_kernel(*refs):
    many = refs[-1].shape[0]
    parts, outs = refs[:many], refs[many:]
    for k, out in enumerate(outs):
        for c, part in enumerate(parts):
            out[c] = part[k]


def ffn_kernel(blocks, planes, idx, *refs):
    parts, refs = refs[:blocks], refs[blocks:]
    held = refs[-1]
    own, *sends = refs[-1 - blocks:-1]
    per = held.shape[2] // HEAD_SIZE
    lanes = held.shape[2] // per
    pieces = refs[:-1 - blocks]
    near = per // 2 * 2
    far = planes * 2
    starts = (0, near, near + far, near + 2 * far)
    z, q = idx[0], idx[2]
    gate = up = 0.0

    def piece(which, k, c):
        got = pieces[starts[which]:starts[which + 1]]
        side, core = c // 2, c % 2
        sides = per // 2
        if which:
            return got[core * planes + k][side]
        return got[core * sides + side][k]

    for k in range(planes):
        x = jnp.concatenate([part[z ^ k] for part in parts])
        held[k] = x
        x = [held[k, :, pl.ds(pl.multiple_of((q ^ c) * lanes, lanes), lanes)] for c in range(per)]
        x = jnp.concatenate(x, axis=1)
        w = jnp.concatenate([piece(0, k, c) for c in range(per)])
        gate = gate + dot(x, w)
        w = jnp.concatenate([piece(1, k, c) for c in range(per)])
        up = up + dot(x, w)
    activated = (gate / (1.0 + jnp.exp(-gate)) * up).astype(BF16)
    rows = own.shape[1]
    for k in range(planes):
        y = dot(activated, jnp.concatenate([piece(2, k, c) for c in range(per)], axis=1))
        for c in range(per):
            at = pl.ds(pl.multiple_of((q ^ c) * lanes, lanes), lanes)
            block = y[:, c * lanes:(c + 1) * lanes]
            own[z ^ k, :, at] = block[:rows]
            for i, send in enumerate(sends):
                send[z ^ k, :, at] = block[(i + 1) * rows:(i + 2) * rows].astype(BF16)


def head_rows_kernel(idx, weight, *outs):
    rows = outs[0].shape[0]
    for c, out in enumerate(outs):
        out[...] = weight[pl.ds(pl.multiple_of((idx[2] ^ c) * rows, rows), rows), :]


def row_of(z, k, tokens, rows, total):
    i = lax.broadcasted_iota(jnp.int32, (rows, total), 0)
    j = lax.broadcasted_iota(jnp.int32, (rows, total), 1)
    return jnp.where((j == i + (z ^ k) * tokens) & (i < tokens), 1.0, 0.0).astype(BF16)


def plane_sum_kernel(planes, tokens, idx, hidden, *refs):
    parts, outs = refs[:-planes], refs[-planes:]
    total = parts[0][...]
    for part in parts[1:]:
        total = total + part[...].astype(F32)
    total = total.astype(BF16)
    for k, out in enumerate(outs):
        pick = row_of(idx[0], k, tokens, out.shape[1], total.shape[1])
        for p in range(planes):
            out[p] = dot(pick, total[p]).astype(BF16)
        out[planes] = dot(pick, hidden[...]).astype(BF16)


def last_kernel(planes, tokens, idx, *refs):
    *parts, out, held = refs
    width = parts[0].shape[2]
    total = parts[0][:planes].astype(F32)
    for part in parts[1:]:
        total = total + part[:planes].astype(F32)
    for k, part in enumerate(parts):
        held[idx[0] ^ k] = part[planes].astype(F32)
    for p in range(planes):
        value = held[p] + total[p]
        out[:, p * width:(p + 1) * width] = value[:tokens].astype(BF16)


def call(kernel, outs, *args, scratch=()):
    single = not isinstance(outs, list)
    shapes = [outs] if single else outs
    got = pl.pallas_call(
        kernel,
        out_shape=shapes,
        in_specs=[SMEM if a.dtype == jnp.int32 else VMEM for a in args],
        out_specs=[VMEM] * len(shapes),
        scratch_shapes=list(scratch),
        compiler_params=pltpu.CompilerParams(vmem_limit_bytes=16 * 2**20),
    )(*args)
    return got[0] if single else list(got)


def like(*shape, dtype=BF16):
    return jax.ShapeDtypeStruct(shape, dtype)


def move_tokens(
    n_blk,
    n_uly,
    residual,
    query_projection,
    key_projection,
    value_projection,
    gate_proj,
    positions,
    prefix_len,
    out_weight,
    norm_gain,
    gate_weight,
    up_weight,
    down_weight,
):
    axes = ("blk", "uly")
    kv_heads = key_projection.shape[1] // HEAD_SIZE
    heads = query_projection.shape[1] // key_projection.shape[1]
    tokens, features = residual.shape
    rows = -(-tokens // ROW_TILE) * ROW_TILE
    group = kv_heads
    per = group // n_uly
    planes = n_blk // per
    devices = n_blk * n_uly
    me = lax.axis_index("blk") * n_uly + lax.axis_index("uly")
    z, r = me // group, me % group
    idx = jnp.stack([z, r, r // n_uly, r // (2 * n_uly)]).astype(jnp.int32)
    core = n_uly
    near = [b for b in range(group) if not b & core]
    order = near + [b ^ core for b in near]
    steps = near[1:]

    def swap(x, mask):
        return lax.ppermute(x, axes, [(i, i ^ mask) for i in range(devices)])

    def swap_planes(x):
        return [swap(x, k * group) for k in range(1, planes)]

    head_of = [(i % n_uly) * per + i // n_uly for i in range(group)]
    plane_groups = [[p * group + i for i in range(group)] for p in range(planes)]

    def plane_exchange(x):
        return lax.all_to_all(x, axes, 0, 0, axis_index_groups=plane_groups, tiled=True)

    def after(xs, later):
        return lax.optimization_barrier((xs, later))

    width = features // planes
    sides = per // 2
    units = gate_weight.shape[1] // (planes * sides)

    def within_plane(parts):
        return [x if not c else swap(x, c * n_uly) for c, x in enumerate(parts)]

    def across_planes(parts):
        return [x if not k else swap(x, k * group) for k, x in enumerate(parts)]

    def regroup(parts):
        shape = (len(parts),) + parts[0].shape[1:]
        return call(regroup_kernel, [like(*shape)] * parts[0].shape[0], *parts)

    half = planes // 2
    lot = group * rows
    pair = 2 * HEAD_SIZE
    head_groups = call(
        functools.partial(pack_heads_kernel, head_of),
        like(group, rows, 2 * heads * HEAD_SIZE + pair),
        query_projection, gate_proj, key_projection, value_projection,
    )
    masks = [k * group + c * 2 * n_uly for k in range(half) for c in range(sides)]
    head_groups, (gate_weight, up_weight, down_weight, out_weight, positions) = after(
        head_groups, (gate_weight, up_weight, down_weight, out_weight, positions)
    )
    gate_up = call(
        functools.partial(split_gate_up_kernel, planes, sides),
        [like(gate_weight.shape[0], 4 * units)] * len(masks),
        idx, gate_weight, up_weight,
    )
    head_rows = call(
        head_rows_kernel,
        [like(out_weight.shape[0] // per, out_weight.shape[1])] * per,
        idx, out_weight,
    )
    down_parts = call(
        functools.partial(split_down_kernel, planes),
        [like(planes, units, down_weight.shape[1])] * sides,
        idx, down_weight,
    )
    spots = jnp.pad(
        positions.reshape(planes, group, tokens).astype(F32),
        ((0, 0), (0, 0), (0, rows - tokens)),
        constant_values=NO_POSITION,
    ).reshape(planes, 1, group * rows)
    own_heads = plane_exchange(head_groups)
    gate_up[sides] = swap(gate_up[sides], masks[sides])
    own_heads, (gate_up, head_rows, down_parts, spots) = after(
        own_heads, (gate_up, head_rows, down_parts, spots)
    )
    messages = across_planes(
        call(
            functools.partial(message_kernel, planes),
            [like(lot + rows * width // pair, pair)] * planes,
            idx, own_heads, residual,
        )
    )
    wo = within_plane(head_rows)
    down_parts[1] = swap(down_parts[1], masks[1])
    gate_up[1] = swap(gate_up[1], masks[1])
    pick = np.zeros((group, tokens, group, rows), np.float32)
    for b in range(group):
        for t in range(tokens):
            pick[b, t, b, t] = 1
    pick = jnp.asarray(pick.reshape(group * tokens, group * rows), BF16)
    gated = call(
        functools.partial(attention_kernel, heads, planes),
        like(group * tokens, heads * HEAD_SIZE),
        idx, prefix_len, own_heads, *messages, spots, pick,
    )
    gated, (wo, down_parts, gate_up[3]) = after(gated, (wo, down_parts, gate_up[3]))
    gateds = [gated] + swap_planes(gated)
    gate_up[3] = swap(gate_up[3], masks[3])
    gateds, (gate_up[1], down_parts) = after(gateds, (gate_up[1], regroup(down_parts)))
    down_parts = across_planes(down_parts)

    turn = np.zeros((group, planes, tokens, planes, group, tokens), np.float32)
    for i, b in enumerate(order):
        for p in range(planes):
            for t in range(tokens):
                turn[i, p, t, p, b, t] = 1
    total = devices * tokens
    turn = jnp.asarray(turn.reshape(total, total), BF16)
    keep, send = call(
        functools.partial(project_kernel, planes),
        [like(total // 2, width)] * 2,
        idx, *gateds, *wo, turn,
        scratch=[
            pltpu.VMEM((planes,) + gated.shape, BF16),
            pltpu.VMEM((wo[0].shape[0], width), BF16),
        ],
    )
    share = total // group
    own, *rest = call(
        core_sum_kernel,
        [like(share, width, dtype=F32)] + [like(share, width)] * len(steps),
        keep, swap(send, core),
    )
    hidden = call(
        functools.partial(hidden_kernel, planes, tokens),
        like(share, width),
        idx, own, *[swap(x, b) for x, b in zip(rest, steps)], *messages,
    )
    hidden, gate_up[3] = after(hidden, gate_up[3])
    near_hidden = [hidden] + [swap(hidden, k * group) for k in range(1, half)]
    gate_up = [x for both in zip(gate_up, [swap(x, core) for x in gate_up]) for x in both]
    block = call(stack_kernel, like(half, share, width), *near_hidden)
    blocks = [block] + [swap(block, b) for b in steps]
    keep, send = call(
        functools.partial(gate_up_kernel, len(blocks), per),
        [
            like(len(blocks) * share, 2 * units + HEAD_SIZE, dtype=F32),
            like(len(blocks) * share, 2 * units + HEAD_SIZE),
        ],
        idx, *blocks, *gate_up, norm_gain.reshape(planes, 1, width),
        scratch=[pltpu.VMEM((half, len(blocks) * share, width), BF16)],
    )
    send, down_parts = after(send, down_parts)
    got = swap(send, half * group)
    down_share = down_parts + [swap(x, core) for x in down_parts]
    own, *rest = call(
        functools.partial(down_kernel, planes, per, features),
        [like(planes, share, width, dtype=F32)] + [like(planes, share, width)] * len(steps),
        idx, keep, got, *down_share,
    )
    parts = call(
        functools.partial(plane_sum_kernel, planes, tokens),
        [like(planes + 1, rows, width)] * planes,
        idx, hidden, own, *[swap(x, b) for x, b in zip(rest, steps)],
    )
    return call(
        functools.partial(last_kernel, planes, tokens),
        like(tokens, features),
        idx, *across_planes(parts),
        scratch=[pltpu.VMEM((planes, rows, width), F32)],
    )


def tokens_can_travel(n_blk, n_uly, kv_heads, token_count, unit_count):
    def power(n):
        return n > 0 and not n & (n - 1)

    per = kv_heads // n_uly
    return (
        power(n_blk)
        and power(n_uly)
        and power(kv_heads)
        and per > 1
        and n_blk % per == 0
        and token_count < unit_count // n_uly
    )


def solution(mesh):
    n_blk, n_uly = mesh.shape["blk"], mesh.shape["uly"]

    def per_device(*args):
        residual, key_projection, gate_weight = args[0], args[2], args[9]
        travel = tokens_can_travel(
            n_blk,
            n_uly,
            key_projection.shape[1] // HEAD_SIZE,
            residual.shape[0] * n_blk * n_uly,
            gate_weight.shape[1] * n_uly,
        )
        if travel:
            return move_tokens(n_blk, n_uly, *args)
        return move_weights(*args)

    return jax.shard_map(
        per_device,
        mesh=mesh,
        in_specs=(
            P(("blk", "uly"), None),
            P(("blk", "uly"), None),
            P(("blk", "uly"), None),
            P(("blk", "uly"), None),
            P(("blk", "uly"), None),
            P(),
            P(),
            P("uly", "blk"),
            P(),
            P("blk", "uly"),
            P("blk", "uly"),
            P("uly", "blk"),
        ),
        out_specs=P(("blk", "uly"), None),
        check_vma=False,
    )
```

```python
import functools
import math

import jax
import jax.numpy as jnp
import numpy as np
from jax import lax
from jax.experimental import pallas as pl
from jax.experimental.pallas import tpu as pltpu
from jax.sharding import PartitionSpec as P

HEAD_SIZE = 128
ROW_TILE = 16
HIDE = -1e30
NO_POSITION = float(2**30)
F32 = jnp.float32
BF16 = jnp.bfloat16
VMEM = pl.BlockSpec(memory_space=pltpu.VMEM)
SMEM = pl.BlockSpec(memory_space=pltpu.SMEM)
NT = (((1,), (1,)), ((), ()))


def move_weights(
    residual,
    query_projection,
    key_projection,
    value_projection,
    gate_proj,
    positions,
    prefix_len,
    out_weight,
    norm_gain,
    gate_weight,
    up_weight,
    down_weight,
):
    q_loc, k_loc, v_loc, g_loc = (
        lax.all_to_all(query_projection, "uly", split_axis=1, concat_axis=0, tiled=True),
        lax.all_to_all(key_projection, "uly", split_axis=1, concat_axis=0, tiled=True),
        lax.all_to_all(value_projection, "uly", split_axis=1, concat_axis=0, tiled=True),
        lax.all_to_all(gate_proj, "uly", split_axis=1, concat_axis=0, tiled=True),
    )
    row_count = q_loc.shape[0]
    kv_heads = k_loc.shape[1] // HEAD_SIZE
    q_heads = q_loc.shape[1] // HEAD_SIZE
    heads_per_group = q_heads // kv_heads
    score_scale = 1.0 / math.sqrt(HEAD_SIZE)
    blk_index = lax.axis_index("blk")
    query_pos = lax.dynamic_slice_in_dim(positions, blk_index * row_count, row_count)
    prefix = prefix_len[0]
    query_heads = q_loc.reshape(row_count, kv_heads, heads_per_group, HEAD_SIZE)
    wo_full, wg_full, wu_full, wd_full = (
        lax.all_gather(out_weight, "blk", axis=1, tiled=True),
        lax.all_gather(gate_weight, "blk", axis=0, tiled=True),
        lax.all_gather(up_weight, "blk", axis=0, tiled=True),
        lax.all_gather(down_weight, "blk", axis=1, tiled=True),
    )
    key_part = lax.all_gather(k_loc, "blk", axis=0, tiled=True)
    value_part = lax.all_gather(v_loc, "blk", axis=0, tiled=True)
    key_count = key_part.shape[0]
    scores = (
        jnp.einsum(
            "bkgd,skd->bkgs",
            query_heads,
            key_part.reshape(key_count, kv_heads, HEAD_SIZE),
            preferred_element_type=F32,
        )
        * score_scale
    )
    visible = (positions[None, :] <= query_pos[:, None]) | (positions[None, :] < prefix)
    scores = jnp.where(visible[:, None, None, :], scores, -jnp.inf)
    row_max = jnp.max(scores, axis=-1)
    exp_scores = jnp.exp(scores - row_max[..., None])
    denom = jnp.sum(exp_scores, axis=-1)
    probs = exp_scores.astype(BF16)
    weighted = jnp.einsum(
        "bkgs,skd->bkgd",
        probs,
        value_part.reshape(key_count, kv_heads, HEAD_SIZE),
        preferred_element_type=F32,
    )
    attended = (weighted / denom[..., None]).reshape(row_count, q_heads * HEAD_SIZE)
    gated_out = (attended * jax.nn.sigmoid(g_loc.astype(F32))).astype(BF16)
    head_partial = jnp.dot(gated_out, wo_full, preferred_element_type=F32)
    projected = lax.psum_scatter(
        head_partial.astype(BF16), "uly", scatter_dimension=0, tiled=True
    ).astype(F32)
    hidden_f = (residual.astype(F32) + projected).astype(BF16).astype(F32)
    mean_sq = jnp.mean(hidden_f * hidden_f, axis=-1, keepdims=True)
    normed = (hidden_f * lax.rsqrt(mean_sq + 1e-06) * norm_gain).astype(BF16)
    group_rows = lax.all_gather(normed, "uly", axis=0, tiled=True)
    gate_sum = jnp.dot(group_rows, wg_full, preferred_element_type=F32)
    up_sum = jnp.dot(group_rows, wu_full, preferred_element_type=F32)
    activated = (jax.nn.silu(gate_sum) * up_sum).astype(BF16)
    ffn_partial = jnp.dot(activated, wd_full, preferred_element_type=F32)
    ffn_out = lax.psum_scatter(
        ffn_partial.astype(BF16), "uly", scatter_dimension=0, tiled=True
    ).astype(F32)
    return (hidden_f + ffn_out).astype(BF16)


def dot(a, b):
    return jnp.dot(a, b, preferred_element_type=F32)


def pack_heads_kernel(head_of, *refs):
    *parts, out = refs
    tokens = parts[0].shape[0]
    out[...] = jnp.zeros_like(out)
    for r, j in enumerate(head_of):
        start = 0
        for part in parts:
            width = part.shape[1] // len(head_of)
            out[r, :tokens, start:start + width] = part[:, j * width:(j + 1) * width]
            start += width


def message_kernel(planes, idx, heads, residual, *outs):
    group, rows, whole = heads.shape
    tokens, features = residual.shape
    pair = 2 * HEAD_SIZE
    lot = group * rows
    width = features // planes
    z = idx[0]
    keys = heads[:, :, whole - pair:].reshape(lot, pair)
    for k, out in enumerate(outs):
        out[:lot] = keys
        out[lot:] = jnp.zeros((out.shape[0] - lot, pair), BF16)
        for c in range(width // pair):
            at = pl.ds(pl.multiple_of((z ^ k) * width + c * pair, pair), pair)
            out[lot + c * rows:lot + c * rows + tokens] = residual[:, at]


def attention_kernel(heads, planes, idx, prefix, qg, *refs):
    messages, (spots, pick, out) = refs[:planes], refs[planes:]
    group, rows, _ = qg.shape
    z, r = idx[0], idx[1]
    lot = group * rows
    keys, values, key_spot = [], [], []
    for k in range(planes):
        keys.append(messages[k][:lot, :HEAD_SIZE])
        values.append(messages[k][:lot, HEAD_SIZE:])
        key_spot.append(spots[z ^ k])
    keys, values = jnp.concatenate(keys), jnp.concatenate(values)
    key_spot = jnp.concatenate(key_spot, axis=1)
    i = lax.broadcasted_iota(jnp.int32, (lot, lot), 0)
    j = lax.broadcasted_iota(jnp.int32, (lot, lot), 1)
    own = jnp.where((i ^ (r * rows)) == j, spots[z], 0.0)
    query_spot = jnp.sum(own, axis=1, keepdims=True)
    visible = (key_spot <= query_spot) | (key_spot < prefix[0].astype(F32))
    bias = jnp.where(visible, 0.0, HIDE)
    scale = 1.0 / math.sqrt(HEAD_SIZE)
    done = []
    for h in range(heads):
        at = slice(h * HEAD_SIZE, (h + 1) * HEAD_SIZE)
        gate_at = slice((heads + h) * HEAD_SIZE, (heads + h + 1) * HEAD_SIZE)
        q = jnp.concatenate([qg[b ^ r, :, at] for b in range(group)])
        gate = jnp.concatenate([qg[b ^ r, :, gate_at] for b in range(group)]).astype(F32)
        s = lax.dot_general(q, keys, NT, preferred_element_type=F32) * scale + bias
        e = jnp.exp(s - jnp.max(s, axis=-1, keepdims=True))
        denom = jnp.sum(e, axis=-1, keepdims=True)
        attended = dot(e.astype(BF16), values) / denom
        done.append((attended / (1.0 + jnp.exp(-gate))).astype(BF16))
    out[...] = dot(pick[...], jnp.concatenate(done, axis=1)).astype(BF16)


def project_kernel(planes, idx, *refs):
    parts = refs[:planes]
    weights, (pick, keep, send, held, wide) = refs[planes:-5], refs[-5:]
    z, q = idx[0], idx[2]
    for k in range(planes):
        held[z ^ k] = parts[k][...]
    rows, width = parts[0].shape
    x = dot(pick[...], held[...].reshape(planes * rows, width)).astype(BF16)
    lanes = weights[0].shape[1]
    for c, weight in enumerate(weights):
        wide[:, pl.ds(pl.multiple_of((q ^ c) * lanes, lanes), lanes)] = weight[...]
    y = dot(x, wide[...]).astype(BF16)
    half = y.shape[0] // 2
    keep[...] = y[:half]
    send[...] = y[half:]


def core_sum_kernel(keep, got, *outs):
    rows = outs[0].shape[0]
    for i, out in enumerate(outs):
        at = slice(i * rows, (i + 1) * rows)
        out[...] = (keep[at].astype(F32) + got[at].astype(F32)).astype(out.dtype)


def hidden_kernel(planes, tokens, idx, *refs):
    parts, messages, out = refs[:-planes - 1], refs[-planes - 1:-1], refs[-1]
    total = parts[0][...]
    for part in parts[1:]:
        total = total + part[...].astype(F32)
    width = out.shape[1]
    pair = messages[0].shape[1]
    pieces = width // pair
    rows = -(-tokens // ROW_TILE) * ROW_TILE
    for k, message in enumerate(messages):
        i = lax.broadcasted_iota(jnp.int32, (out.shape[0], rows), 0)
        j = lax.broadcasted_iota(jnp.int32, (out.shape[0], rows), 1)
        place = jnp.where((i == j + (idx[0] ^ k) * tokens) & (j < tokens), 1.0, 0.0).astype(BF16)
        lot = message.shape[0] - pieces * rows
        held = [message[lot + c * rows:lot + (c + 1) * rows] for c in range(pieces)]
        total = total + dot(place, jnp.concatenate(held, axis=1))
    out[...] = total.astype(BF16)


def split_gate_up_kernel(planes, sides, idx, gate, up, *outs):
    units = outs[0].shape[1] // (2 * planes)
    for c, out in enumerate(outs):
        for k in range(planes):
            chip = (idx[0] ^ k) * sides + (idx[3] ^ c)
            at = pl.ds(pl.multiple_of(chip * units, units), units)
            out[:, 2 * k * units:(2 * k + 1) * units] = gate[:, at]
            out[:, (2 * k + 1) * units:(2 * k + 2) * units] = up[:, at]


def split_rows_kernel(planes, per, idx, down, heads, message, own, own_heads, core_heads):
    sides = per // 2
    units, head_rows = own.shape[1], own_heads.shape[0]
    for k in range(planes):
        for c in range(sides):
            chip = (idx[0] ^ k) * sides + (idx[3] ^ c)
            start = pl.multiple_of(chip * units, units)
            rows = down[pl.ds(start, units), :]
            if c:
                message[k * units:(k + 1) * units] = rows
            else:
                own[k] = rows
    for c in range(per):
        rows = heads[pl.ds(pl.multiple_of((idx[2] ^ c) * head_rows, head_rows), head_rows), :]
        if c == 0:
            own_heads[...] = rows
        elif c == 1:
            core_heads[...] = rows
        else:
            start = planes * units + (c - 2) * head_rows
            message[start:start + head_rows] = rows


def regroup_kernel(own, message, *outs):
    *downs, near_heads, far_heads = outs
    units, head_rows = own.shape[1], near_heads.shape[0]
    for k, out in enumerate(downs):
        out[0] = own[k]
        out[1] = message[k * units:(k + 1) * units]
    start = len(downs) * units
    near_heads[...] = message[start:start + head_rows]
    far_heads[...] = message[start + head_rows:start + 2 * head_rows]


def gate_up_kernel(blocks, per, planes, idx, *refs):
    parts, pieces = refs[:blocks], refs[blocks:blocks + per]
    gain, same, *outs, held = refs[blocks + per:]
    x = jnp.concatenate([part[...] for part in parts]).astype(F32)
    rows, width = x.shape
    lanes = width // per
    square = jnp.sum(x * x, axis=1, keepdims=True)
    held[...] = (x * gain[idx[0]]).astype(BF16)
    x = [held[:, pl.ds(pl.multiple_of((idx[2] ^ c) * lanes, lanes), lanes)] for c in range(per)]
    x = jnp.concatenate(x, axis=1)
    columns = pieces[0].shape[1] // planes
    lane = lax.broadcasted_iota(jnp.int32, (rows, HEAD_SIZE), 1)
    high = square.astype(BF16).astype(F32)
    terms = jnp.where(lane == 0, high, jnp.where(lane == 1, square - high, 0.0)).astype(BF16)
    terms = lax.dot_general(terms, same[...], (((0,), (0,)), ((), ())), preferred_element_type=F32)
    for k, out in enumerate(outs):
        at = slice(k * columns, (k + 1) * columns)
        total = dot(x, jnp.concatenate([piece[:, at] for piece in pieces]))
        out[:rows] = total.astype(out.dtype)
        out[rows:] = jnp.zeros((out.shape[0] - rows, columns), out.dtype)
        out[rows:, :rows] = terms[:out.shape[0] - rows].astype(out.dtype)


def down_kernel(planes, per, features, idx, *refs):
    totals, pieces, same = refs[:planes], refs[planes:3 * planes], refs[3 * planes]
    own, *sends = refs[3 * planes + 1:]
    many = same.shape[0]
    total = totals[0][:many]
    terms = totals[0][many:, :many]
    for part in totals[1:]:
        total = total + part[:many].astype(F32)
        terms = jnp.concatenate([terms, part[many:, :many].astype(F32)])
    units = total.shape[1] // 2
    square = lax.dot_general(same[...], terms.astype(BF16), NT, preferred_element_type=F32)
    square = jnp.sum(square, axis=1, keepdims=True)
    factor = lax.rsqrt(square / features + 1e-06)
    gate, up = total[:, :units] * factor, total[:, units:] * factor
    activated = (gate / (1.0 + jnp.exp(-gate)) * up).astype(BF16)
    z, q = idx[0], idx[2]
    rows = own.shape[1]
    for k in range(planes):
        w = [pieces[(c % 2) * planes + k][c // 2] for c in range(per)]
        y = dot(activated, jnp.concatenate(w, axis=1))
        lanes = w[0].shape[1]
        for c in range(per):
            at = pl.ds(pl.multiple_of((q ^ c) * lanes, lanes), lanes)
            block = y[:, c * lanes:(c + 1) * lanes]
            own[z ^ k, :, at] = block[:rows]
            for i, send in enumerate(sends):
                send[z ^ k, :, at] = block[(i + 1) * rows:(i + 2) * rows].astype(BF16)


def row_of(z, k, tokens, rows, total):
    i = lax.broadcasted_iota(jnp.int32, (rows, total), 0)
    j = lax.broadcasted_iota(jnp.int32, (rows, total), 1)
    return jnp.where((j == i + (z ^ k) * tokens) & (i < tokens), 1.0, 0.0).astype(BF16)


def plane_sum_kernel(planes, tokens, idx, hidden, *refs):
    parts, outs = refs[:-planes], refs[-planes:]
    total = parts[0][...]
    for part in parts[1:]:
        total = total + part[...].astype(F32)
    total = total.astype(BF16)
    for k, out in enumerate(outs):
        pick = row_of(idx[0], k, tokens, out.shape[1], total.shape[1])
        for p in range(planes):
            out[p] = dot(pick, total[p]).astype(BF16)
        out[planes] = dot(pick, hidden[...]).astype(BF16)


def last_kernel(planes, tokens, idx, *refs):
    *parts, out, held = refs
    width = parts[0].shape[2]
    total = parts[0][:planes].astype(F32)
    for part in parts[1:]:
        total = total + part[:planes].astype(F32)
    for k, part in enumerate(parts):
        held[idx[0] ^ k] = part[planes].astype(F32)
    for p in range(planes):
        value = held[p] + total[p]
        out[:, p * width:(p + 1) * width] = value[:tokens].astype(BF16)


def call(kernel, outs, *args, scratch=()):
    single = not isinstance(outs, list)
    shapes = [outs] if single else outs
    got = pl.pallas_call(
        kernel,
        out_shape=shapes,
        in_specs=[SMEM if a.dtype == jnp.int32 else VMEM for a in args],
        out_specs=[VMEM] * len(shapes),
        scratch_shapes=list(scratch),
        compiler_params=pltpu.CompilerParams(vmem_limit_bytes=16 * 2**20),
    )(*args)
    return got[0] if single else list(got)


def like(*shape, dtype=BF16):
    return jax.ShapeDtypeStruct(shape, dtype)


def move_tokens(
    n_blk,
    n_uly,
    residual,
    query_projection,
    key_projection,
    value_projection,
    gate_proj,
    positions,
    prefix_len,
    out_weight,
    norm_gain,
    gate_weight,
    up_weight,
    down_weight,
):
    axes = ("blk", "uly")
    kv_heads = key_projection.shape[1] // HEAD_SIZE
    heads = query_projection.shape[1] // key_projection.shape[1]
    tokens, features = residual.shape
    rows = -(-tokens // ROW_TILE) * ROW_TILE
    group = kv_heads
    per = group // n_uly
    planes = n_blk // per
    devices = n_blk * n_uly
    me = lax.axis_index("blk") * n_uly + lax.axis_index("uly")
    z, r = me // group, me % group
    idx = jnp.stack([z, r, r // n_uly, r // (2 * n_uly)]).astype(jnp.int32)
    core = n_uly
    near = [b for b in range(group) if not b & core]
    order = near + [b ^ core for b in near]
    steps = near[1:]

    def swap(x, mask):
        return lax.ppermute(x, axes, [(i, i ^ mask) for i in range(devices)])

    def swap_planes(x):
        return [swap(x, k * group) for k in range(1, planes)]

    head_of = [(i % n_uly) * per + i // n_uly for i in range(group)]
    plane_groups = [[p * group + i for i in range(group)] for p in range(planes)]

    def plane_exchange(x):
        return lax.all_to_all(x, axes, 0, 0, axis_index_groups=plane_groups, tiled=True)

    def after(*xs):
        return lax.optimization_barrier(xs)

    width = features // planes
    sides = per // 2
    units = gate_weight.shape[1] // (planes * sides)

    def across_planes(parts):
        return [x if not k else swap(x, k * group) for k, x in enumerate(parts)]

    lot = group * rows
    pair = 2 * HEAD_SIZE
    head_groups = call(
        functools.partial(pack_heads_kernel, head_of),
        like(group, rows, 2 * heads * HEAD_SIZE + pair),
        query_projection, gate_proj, key_projection, value_projection,
    )
    head_groups, gate_weight, up_weight, down_weight, out_weight, positions = after(
        head_groups, gate_weight, up_weight, down_weight, out_weight, positions
    )
    side = 2 * n_uly
    gate_up = call(
        functools.partial(split_gate_up_kernel, planes, sides),
        [like(gate_weight.shape[0], 2 * planes * units)] * sides,
        idx, gate_weight, up_weight,
    )
    head_rows = out_weight.shape[0] // per
    lanes = out_weight.shape[1]
    message, own_down, wo_own, wo_core = call(
        functools.partial(split_rows_kernel, planes, per),
        [
            like(planes * units + 2 * head_rows, lanes),
            like(planes, units, lanes),
            like(head_rows, lanes),
            like(head_rows, lanes),
        ],
        idx, down_weight, out_weight,
    )
    spots = jnp.pad(
        positions.reshape(planes, group, tokens).astype(F32),
        ((0, 0), (0, 0), (0, rows - tokens)),
        constant_values=NO_POSITION,
    ).reshape(planes, 1, group * rows)
    own_heads = plane_exchange(head_groups)
    wo_core = swap(wo_core, core)
    own_heads, message, gate_up, wo_core, spots = after(
        own_heads, message, gate_up, wo_core, spots
    )
    messages = across_planes(
        call(
            functools.partial(message_kernel, planes),
            [like(lot + rows * width // pair, pair)] * planes,
            idx, own_heads, residual,
        )
    )
    message = swap(message, side)
    *messages, gate_up[1] = after(*messages, gate_up[1])
    gate_up[1] = swap(gate_up[1], side)
    pick = np.zeros((group, tokens, group, rows), np.float32)
    for b in range(group):
        for t in range(tokens):
            pick[b, t, b, t] = 1
    pick = jnp.asarray(pick.reshape(group * tokens, group * rows), BF16)
    gated = call(
        functools.partial(attention_kernel, heads, planes),
        like(group * tokens, heads * HEAD_SIZE),
        idx, prefix_len, own_heads, *messages, spots, pick,
    )
    gated, message, own_gate_up = after(gated, message, gate_up[0])
    *down_parts, wo_near, wo_far = call(
        regroup_kernel,
        [like(sides, units, lanes)] * planes + [like(head_rows, lanes)] * 2,
        own_down, message,
    )
    gateds = [gated] + swap_planes(gated)
    wo = [wo_own, wo_core, wo_near, swap(wo_far, core)]
    twin = [swap(own_gate_up, core), None]
    gateds, wo, down_parts, twin[0] = after(gateds, wo, down_parts, twin[0])
    down_parts[2] = swap(down_parts[2], 2 * group)

    turn = np.zeros((group, planes, tokens, planes, group, tokens), np.float32)
    for i, b in enumerate(order):
        for p in range(planes):
            for t in range(tokens):
                turn[i, p, t, p, b, t] = 1
    total = devices * tokens
    turn = jnp.asarray(turn.reshape(total, total), BF16)
    keep, send = call(
        functools.partial(project_kernel, planes),
        [like(total // 2, width)] * 2,
        idx, *gateds, *wo, turn,
        scratch=[
            pltpu.VMEM((planes,) + gated.shape, BF16),
            pltpu.VMEM((wo[0].shape[0], width), BF16),
        ],
    )
    share = total // group
    own, *rest = call(
        core_sum_kernel,
        [like(share, width, dtype=F32)] + [like(share, width)] * len(steps),
        keep, swap(send, core),
    )
    rest, gate_up[1] = after(rest, gate_up[1])
    twin[1] = swap(gate_up[1], core)
    hidden = call(
        functools.partial(hidden_kernel, planes, tokens),
        like(share, width),
        idx, own, *[swap(x, b) for x, b in zip(rest, steps)], *messages,
    )
    hidden, twin[1], down_parts[3] = after(hidden, twin[1], down_parts[3])
    blocks = [hidden] + [swap(hidden, b) for b in steps]
    same = jnp.eye(len(blocks) * share, dtype=BF16)
    down_parts[3] = swap(down_parts[3], 3 * group)
    pieces = [x for both in zip(gate_up, twin) for x in both]
    many = len(blocks) * share
    keep, *sends = call(
        functools.partial(gate_up_kernel, len(blocks), per, planes),
        [like(many + ROW_TILE, 2 * units, dtype=F32)]
        + [like(many + ROW_TILE, 2 * units)] * (planes - 1),
        idx, *blocks, *pieces, norm_gain.reshape(planes, 1, width), same,
        scratch=[pltpu.VMEM((many, width), BF16)],
    )
    sends, down_parts[2:3], down_parts[1] = after(sends, down_parts[2:3], down_parts[1])
    totals = across_planes([keep] + sends)
    down_parts[1] = swap(down_parts[1], group)
    down_share = down_parts + [swap(x, core) for x in down_parts]
    own, *rest = call(
        functools.partial(down_kernel, planes, per, features),
        [like(planes, share, width, dtype=F32)] + [like(planes, share, width)] * len(steps),
        idx, *totals, *down_share, same,
    )
    parts = call(
        functools.partial(plane_sum_kernel, planes, tokens),
        [like(planes + 1, rows, width)] * planes,
        idx, hidden, own, *[swap(x, b) for x, b in zip(rest, steps)],
    )
    return call(
        functools.partial(last_kernel, planes, tokens),
        like(tokens, features),
        idx, *across_planes(parts),
        scratch=[pltpu.VMEM((planes, rows, width), F32)],
    )


def tokens_can_travel(n_blk, n_uly, kv_heads, token_count, unit_count):
    def power(n):
        return n > 0 and not n & (n - 1)

    per = kv_heads // n_uly
    return (
        power(n_blk)
        and power(n_uly)
        and power(kv_heads)
        and per > 1
        and n_blk % per == 0
        and token_count < unit_count // n_uly
    )


def solution(mesh):
    n_blk, n_uly = mesh.shape["blk"], mesh.shape["uly"]

    def per_device(*args):
        residual, key_projection, gate_weight = args[0], args[2], args[9]
        travel = tokens_can_travel(
            n_blk,
            n_uly,
            key_projection.shape[1] // HEAD_SIZE,
            residual.shape[0] * n_blk * n_uly,
            gate_weight.shape[1] * n_uly,
        )
        if travel:
            return move_tokens(n_blk, n_uly, *args)
        return move_weights(*args)

    return jax.shard_map(
        per_device,
        mesh=mesh,
        in_specs=(
            P(("blk", "uly"), None),
            P(("blk", "uly"), None),
            P(("blk", "uly"), None),
            P(("blk", "uly"), None),
            P(("blk", "uly"), None),
            P(),
            P(),
            P("uly", "blk"),
            P(),
            P("blk", "uly"),
            P("blk", "uly"),
            P("uly", "blk"),
        ),
        out_specs=P(("blk", "uly"), None),
        check_vma=False,
    )
```

```python
import functools
import math

import jax
import jax.numpy as jnp
import numpy as np
from jax import lax
from jax.experimental import pallas as pl
from jax.experimental.pallas import tpu as pltpu
from jax.sharding import PartitionSpec as P

HEAD_SIZE = 128
ROW_TILE = 16
HIDE = -1e30
F32 = jnp.float32
BF16 = jnp.bfloat16
VMEM = pl.BlockSpec(memory_space=pltpu.VMEM)
SMEM = pl.BlockSpec(memory_space=pltpu.SMEM)
NT = (((1,), (1,)), ((), ()))


def move_weights(
    residual,
    query_projection,
    key_projection,
    value_projection,
    gate_proj,
    positions,
    prefix_len,
    out_weight,
    norm_gain,
    gate_weight,
    up_weight,
    down_weight,
):
    q_loc, k_loc, v_loc, g_loc = (
        lax.all_to_all(query_projection, "uly", split_axis=1, concat_axis=0, tiled=True),
        lax.all_to_all(key_projection, "uly", split_axis=1, concat_axis=0, tiled=True),
        lax.all_to_all(value_projection, "uly", split_axis=1, concat_axis=0, tiled=True),
        lax.all_to_all(gate_proj, "uly", split_axis=1, concat_axis=0, tiled=True),
    )
    row_count = q_loc.shape[0]
    kv_heads = k_loc.shape[1] // HEAD_SIZE
    q_heads = q_loc.shape[1] // HEAD_SIZE
    heads_per_group = q_heads // kv_heads
    score_scale = 1.0 / math.sqrt(HEAD_SIZE)
    blk_index = lax.axis_index("blk")
    query_pos = lax.dynamic_slice_in_dim(positions, blk_index * row_count, row_count)
    prefix = prefix_len[0]
    query_heads = q_loc.reshape(row_count, kv_heads, heads_per_group, HEAD_SIZE)
    wo_full, wg_full, wu_full, wd_full = (
        lax.all_gather(out_weight, "blk", axis=1, tiled=True),
        lax.all_gather(gate_weight, "blk", axis=0, tiled=True),
        lax.all_gather(up_weight, "blk", axis=0, tiled=True),
        lax.all_gather(down_weight, "blk", axis=1, tiled=True),
    )
    key_part = lax.all_gather(k_loc, "blk", axis=0, tiled=True)
    value_part = lax.all_gather(v_loc, "blk", axis=0, tiled=True)
    key_count = key_part.shape[0]
    scores = (
        jnp.einsum(
            "bkgd,skd->bkgs",
            query_heads,
            key_part.reshape(key_count, kv_heads, HEAD_SIZE),
            preferred_element_type=F32,
        )
        * score_scale
    )
    visible = (positions[None, :] <= query_pos[:, None]) | (positions[None, :] < prefix)
    scores = jnp.where(visible[:, None, None, :], scores, -jnp.inf)
    row_max = jnp.max(scores, axis=-1)
    exp_scores = jnp.exp(scores - row_max[..., None])
    denom = jnp.sum(exp_scores, axis=-1)
    probs = exp_scores.astype(BF16)
    weighted = jnp.einsum(
        "bkgs,skd->bkgd",
        probs,
        value_part.reshape(key_count, kv_heads, HEAD_SIZE),
        preferred_element_type=F32,
    )
    attended = (weighted / denom[..., None]).reshape(row_count, q_heads * HEAD_SIZE)
    gated_out = (attended * jax.nn.sigmoid(g_loc.astype(F32))).astype(BF16)
    head_partial = jnp.dot(gated_out, wo_full, preferred_element_type=F32)
    projected = lax.psum_scatter(
        head_partial.astype(BF16), "uly", scatter_dimension=0, tiled=True
    ).astype(F32)
    hidden_f = (residual.astype(F32) + projected).astype(BF16).astype(F32)
    mean_sq = jnp.mean(hidden_f * hidden_f, axis=-1, keepdims=True)
    normed = (hidden_f * lax.rsqrt(mean_sq + 1e-06) * norm_gain).astype(BF16)
    group_rows = lax.all_gather(normed, "uly", axis=0, tiled=True)
    gate_sum = jnp.dot(group_rows, wg_full, preferred_element_type=F32)
    up_sum = jnp.dot(group_rows, wu_full, preferred_element_type=F32)
    activated = (jax.nn.silu(gate_sum) * up_sum).astype(BF16)
    ffn_partial = jnp.dot(activated, wd_full, preferred_element_type=F32)
    ffn_out = lax.psum_scatter(
        ffn_partial.astype(BF16), "uly", scatter_dimension=0, tiled=True
    ).astype(F32)
    return (hidden_f + ffn_out).astype(BF16)


def dot(a, b):
    return jnp.dot(a, b, preferred_element_type=F32)


def pack_heads_kernel(head_of, *refs):
    many = (len(refs) - 2) // 2
    parts, out, held, sems = refs[:many], refs[many], refs[many + 1:-1], refs[-1]
    copies = [
        pltpu.make_async_copy(part, spot, sems.at[i])
        for i, (part, spot) in enumerate(zip(parts, held))
    ]
    for copy in copies:
        copy.start()
    out[...] = jnp.zeros_like(out)
    tokens = parts[0].shape[0]
    start = 0
    for copy, spot in zip(copies, held):
        copy.wait()
        width = spot.shape[1] // len(head_of)
        for r, j in enumerate(head_of):
            out[r, :tokens, start:start + width] = spot[:, j * width:(j + 1) * width]
        start += width


def message_kernel(planes, idx, heads, residual, pick, *outs):
    group, rows, _ = heads.shape
    tokens, features = residual.shape
    pair = 2 * HEAD_SIZE
    width = features // planes
    z = idx[0]
    keys = dot(pick[...], heads[:, :, :pair].reshape(group * rows, pair)).astype(BF16)
    lot = keys.shape[0]
    for k, out in enumerate(outs):
        out[:lot] = keys
        out[lot:] = jnp.zeros((out.shape[0] - lot, pair), BF16)
        for c in range(width // pair):
            at = pl.ds(pl.multiple_of((z ^ k) * width + c * pair, pair), pair)
            out[lot + c * rows:lot + c * rows + tokens] = residual[:, at]


def attention_kernel(heads, planes, idx, prefix, qg, *refs):
    messages, (spots, pick, out) = refs[:planes], refs[planes:]
    group, rows, _ = qg.shape
    z, r = idx[0], idx[1]
    lot, held = group * rows, pick.shape[0]
    tokens = held // group
    keys, values, key_spot = [], [], []
    for k in range(planes):
        keys.append(messages[k][:held, :HEAD_SIZE])
        values.append(messages[k][:held, HEAD_SIZE:])
        key_spot.append(spots[z ^ k])
    keys, values = jnp.concatenate(keys), jnp.concatenate(values)
    key_spot = jnp.concatenate(key_spot, axis=1)
    i = lax.broadcasted_iota(jnp.int32, (lot, held), 0) ^ (r * rows)
    j = lax.broadcasted_iota(jnp.int32, (lot, held), 1)
    source = i // rows * tokens + jnp.minimum(i % rows, tokens - 1)
    query_spot = jnp.sum(jnp.where(source == j, spots[z], 0.0), axis=1, keepdims=True)
    visible = (key_spot <= query_spot) | (key_spot < prefix[0].astype(F32))
    bias = jnp.where(visible, 0.0, HIDE)
    scale = 1.0 / math.sqrt(HEAD_SIZE)
    done = []
    for h in range(heads):
        at = slice((h + 2) * HEAD_SIZE, (h + 3) * HEAD_SIZE)
        gate_at = slice((heads + h + 2) * HEAD_SIZE, (heads + h + 3) * HEAD_SIZE)
        q = jnp.concatenate([qg[b ^ r, :, at] for b in range(group)])
        gate = jnp.concatenate([qg[b ^ r, :, gate_at] for b in range(group)]).astype(F32)
        s = lax.dot_general(q, keys, NT, preferred_element_type=F32) * scale + bias
        e = jnp.exp(s - jnp.max(s, axis=-1, keepdims=True))
        denom = jnp.sum(e, axis=-1, keepdims=True)
        attended = dot(e.astype(BF16), values) / denom
        done.append((attended / (1.0 + jnp.exp(-gate))).astype(BF16))
    out[...] = dot(pick[...], jnp.concatenate(done, axis=1)).astype(BF16)


def project_kernel(planes, idx, *refs):
    parts = refs[:planes]
    weights, (pick, keep, send, held, wide) = refs[planes:-5], refs[-5:]
    z, q = idx[0], idx[2]
    for k in range(planes):
        held[z ^ k] = parts[k][...]
    rows, width = parts[0].shape
    x = dot(pick[...], held[...].reshape(planes * rows, width)).astype(BF16)
    lanes = weights[0].shape[1]
    for c, weight in enumerate(weights):
        wide[:, pl.ds(pl.multiple_of((q ^ c) * lanes, lanes), lanes)] = weight[...]
    y = dot(x, wide[...]).astype(BF16)
    half = y.shape[0] // 2
    keep[...] = y[:half]
    send[...] = y[half:]


def core_sum_kernel(keep, got, *outs):
    rows = outs[0].shape[0]
    for i, out in enumerate(outs):
        at = slice(i * rows, (i + 1) * rows)
        out[...] = (keep[at].astype(F32) + got[at].astype(F32)).astype(out.dtype)


def hidden_kernel(planes, tokens, idx, *refs):
    parts, messages, out = refs[:-planes - 1], refs[-planes - 1:-1], refs[-1]
    total = parts[0][...]
    for part in parts[1:]:
        total = total + part[...].astype(F32)
    width = out.shape[1]
    pair = messages[0].shape[1]
    pieces = width // pair
    rows = -(-tokens // ROW_TILE) * ROW_TILE
    for k, message in enumerate(messages):
        i = lax.broadcasted_iota(jnp.int32, (out.shape[0], rows), 0)
        j = lax.broadcasted_iota(jnp.int32, (out.shape[0], rows), 1)
        place = jnp.where((i == j + (idx[0] ^ k) * tokens) & (j < tokens), 1.0, 0.0).astype(BF16)
        lot = message.shape[0] - pieces * rows
        held = [message[lot + c * rows:lot + (c + 1) * rows] for c in range(pieces)]
        total = total + dot(place, jnp.concatenate(held, axis=1))
    out[...] = total.astype(BF16)


def stack_kernel(*refs):
    *parts, out = refs
    for k, part in enumerate(parts):
        out[k] = part[...]


def split_gate_up_kernel(planes, sides, idx, gate, up, *outs):
    units = outs[0].shape[1] // (2 * planes)
    for c, out in enumerate(outs):
        for k in range(planes):
            chip = (idx[0] ^ k) * sides + (idx[3] ^ c)
            at = pl.ds(pl.multiple_of(chip * units, units), units)
            out[:, 2 * k * units:(2 * k + 1) * units] = gate[:, at]
            out[:, (2 * k + 1) * units:(2 * k + 2) * units] = up[:, at]


def split_rows_kernel(planes, per, idx, down, heads, message, own, own_heads, core_heads):
    sides = per // 2
    units, head_rows = own.shape[1], own_heads.shape[0]
    for k in range(planes):
        for c in range(sides):
            chip = (idx[0] ^ k) * sides + (idx[3] ^ c)
            start = pl.multiple_of(chip * units, units)
            rows = down[pl.ds(start, units), :]
            if c:
                message[k * units:(k + 1) * units] = rows
            else:
                own[k] = rows
    for c in range(per):
        rows = heads[pl.ds(pl.multiple_of((idx[2] ^ c) * head_rows, head_rows), head_rows), :]
        if c == 0:
            own_heads[...] = rows
        elif c == 1:
            core_heads[...] = rows
        else:
            start = planes * units + (c - 2) * head_rows
            message[start:start + head_rows] = rows


def regroup_kernel(own, message, *outs):
    *downs, near_heads, far_heads = outs
    units, head_rows = own.shape[1], near_heads.shape[0]
    for k, out in enumerate(downs):
        out[0] = own[k]
        out[1] = message[k * units:(k + 1) * units]
    start = len(downs) * units
    near_heads[...] = message[start:start + head_rows]
    far_heads[...] = message[start + head_rows:start + 2 * head_rows]


def gate_up_kernel(blocks, per, planes, idx, *refs):
    parts, pieces = refs[:blocks], refs[blocks:blocks + per]
    gain, same, *outs, held = refs[blocks + per:]
    x = jnp.concatenate([part[...] for part in parts]).astype(F32)
    rows, width = x.shape
    lanes = width // per
    square = jnp.sum(x * x, axis=1, keepdims=True)
    held[...] = (x * gain[idx[0]]).astype(BF16)
    x = [held[:, pl.ds(pl.multiple_of((idx[2] ^ c) * lanes, lanes), lanes)] for c in range(per)]
    x = jnp.concatenate(x, axis=1)
    columns = pieces[0].shape[1] // planes
    lane = lax.broadcasted_iota(jnp.int32, (rows, HEAD_SIZE), 1)
    high = square.astype(BF16).astype(F32)
    terms = jnp.where(lane == 0, high, jnp.where(lane == 1, square - high, 0.0)).astype(BF16)
    terms = lax.dot_general(terms, same[...], (((0,), (0,)), ((), ())), preferred_element_type=F32)
    for k, out in enumerate(outs):
        at = slice(k * columns, (k + 1) * columns)
        total = dot(x, jnp.concatenate([piece[:, at] for piece in pieces]))
        out[:rows] = total.astype(out.dtype)
        out[rows:] = jnp.zeros((out.shape[0] - rows, columns), out.dtype)
        out[rows:, :rows] = terms[:out.shape[0] - rows].astype(out.dtype)


def down_kernel(planes, per, features, idx, *refs):
    totals, (near, far, same, own, *sends) = refs[:planes], refs[planes:]
    many = same.shape[0]
    total = totals[0][:many]
    terms = totals[0][many:, :many]
    for part in totals[1:]:
        total = total + part[:many].astype(F32)
        terms = jnp.concatenate([terms, part[many:, :many].astype(F32)])
    units = total.shape[1] // 2
    square = lax.dot_general(same[...], terms.astype(BF16), NT, preferred_element_type=F32)
    square = jnp.sum(square, axis=1, keepdims=True)
    factor = lax.rsqrt(square / features + 1e-06)
    gate, up = total[:, :units] * factor, total[:, units:] * factor
    activated = (gate / (1.0 + jnp.exp(-gate)) * up).astype(BF16)
    z, q = idx[0], idx[2]
    rows = own.shape[1]
    for k in range(planes):
        w = [(far if c % 2 else near)[k, c // 2] for c in range(per)]
        y = dot(activated, jnp.concatenate(w, axis=1))
        lanes = w[0].shape[1]
        for c in range(per):
            at = pl.ds(pl.multiple_of((q ^ c) * lanes, lanes), lanes)
            block = y[:, c * lanes:(c + 1) * lanes]
            own[z ^ k, :, at] = block[:rows]
            for i, send in enumerate(sends):
                send[z ^ k, :, at] = block[(i + 1) * rows:(i + 2) * rows].astype(BF16)


def row_of(z, k, tokens, rows, total):
    i = lax.broadcasted_iota(jnp.int32, (rows, total), 0)
    j = lax.broadcasted_iota(jnp.int32, (rows, total), 1)
    return jnp.where((j == i + (z ^ k) * tokens) & (i < tokens), 1.0, 0.0).astype(BF16)


def plane_sum_kernel(planes, tokens, idx, hidden, *refs):
    parts, outs = refs[:-planes], refs[-planes:]
    total = parts[0][...]
    for part in parts[1:]:
        total = total + part[...].astype(F32)
    total = total.astype(BF16)
    for k, out in enumerate(outs):
        pick = row_of(idx[0], k, tokens, out.shape[1], total.shape[1])
        for p in range(planes):
            out[p] = dot(pick, total[p]).astype(BF16)
        out[planes] = dot(pick, hidden[...]).astype(BF16)


def last_kernel(planes, tokens, idx, *refs):
    *parts, out, held = refs
    width = parts[0].shape[2]
    total = parts[0][:planes].astype(F32)
    for part in parts[1:]:
        total = total + part[:planes].astype(F32)
    for k, part in enumerate(parts):
        held[idx[0] ^ k] = part[planes].astype(F32)
    for p in range(planes):
        value = held[p] + total[p]
        out[:, p * width:(p + 1) * width] = value[:tokens].astype(BF16)


def call(kernel, outs, *args, scratch=(), place=VMEM, limit=16):
    single = not isinstance(outs, list)
    shapes = [outs] if single else outs
    got = pl.pallas_call(
        kernel,
        out_shape=shapes,
        in_specs=[SMEM if a.dtype == jnp.int32 else place for a in args],
        out_specs=[VMEM] * len(shapes),
        scratch_shapes=list(scratch),
        compiler_params=pltpu.CompilerParams(vmem_limit_bytes=limit * 2**20),
    )(*args)
    return got[0] if single else list(got)


def like(*shape, dtype=BF16):
    return jax.ShapeDtypeStruct(shape, dtype)


def move_tokens(
    n_blk,
    n_uly,
    residual,
    query_projection,
    key_projection,
    value_projection,
    gate_proj,
    positions,
    prefix_len,
    out_weight,
    norm_gain,
    gate_weight,
    up_weight,
    down_weight,
):
    axes = ("blk", "uly")
    kv_heads = key_projection.shape[1] // HEAD_SIZE
    heads = query_projection.shape[1] // key_projection.shape[1]
    tokens, features = residual.shape
    rows = -(-tokens // ROW_TILE) * ROW_TILE
    group = kv_heads
    per = group // n_uly
    planes = n_blk // per
    devices = n_blk * n_uly
    me = lax.axis_index("blk") * n_uly + lax.axis_index("uly")
    z, r = me // group, me % group
    idx = jnp.stack([z, r, r // n_uly, r // (2 * n_uly)]).astype(jnp.int32)
    core = n_uly
    near = [b for b in range(group) if not b & core]
    order = near + [b ^ core for b in near]
    steps = near[1:]

    def swap(x, mask):
        return lax.ppermute(x, axes, [(i, i ^ mask) for i in range(devices)])

    def swap_planes(x):
        return [swap(x, k * group) for k in range(1, planes)]

    head_of = [(i % n_uly) * per + i // n_uly for i in range(group)]
    plane_groups = [[p * group + i for i in range(group)] for p in range(planes)]

    def plane_exchange(x):
        return lax.all_to_all(x, axes, 0, 0, axis_index_groups=plane_groups, tiled=True)

    def after(*xs):
        return lax.optimization_barrier(xs)

    width = features // planes
    sides = per // 2
    units = gate_weight.shape[1] // (planes * sides)

    def across_planes(parts):
        return [x if not k else swap(x, k * group) for k, x in enumerate(parts)]

    pair = 2 * HEAD_SIZE
    tokens_in = (key_projection, value_projection, query_projection, gate_proj)
    head_groups = call(
        functools.partial(pack_heads_kernel, head_of),
        like(group, rows, 2 * heads * HEAD_SIZE + pair),
        *tokens_in,
        scratch=[pltpu.VMEM(x.shape, x.dtype) for x in tokens_in]
        + [pltpu.SemaphoreType.DMA((len(tokens_in),))],
        place=pl.BlockSpec(memory_space=pl.ANY),
        limit=60,
    )
    head_groups, gate_weight, up_weight, down_weight, out_weight, positions = after(
        head_groups, gate_weight, up_weight, down_weight, out_weight, positions
    )
    side = 2 * n_uly
    gate_up = call(
        functools.partial(split_gate_up_kernel, planes, sides),
        [like(gate_weight.shape[0], 2 * planes * units)] * sides,
        idx, gate_weight, up_weight,
    )
    head_rows = out_weight.shape[0] // per
    lanes = out_weight.shape[1]
    message, own_down, wo_own, wo_core = call(
        functools.partial(split_rows_kernel, planes, per),
        [
            like(planes * units + 2 * head_rows, lanes),
            like(planes, units, lanes),
            like(head_rows, lanes),
            like(head_rows, lanes),
        ],
        idx, down_weight, out_weight,
    )
    spots = positions.astype(F32).reshape(planes, 1, group * tokens)
    own_heads = plane_exchange(head_groups)
    wo_core = swap(wo_core, core)
    own_heads, message, gate_up, wo_core, spots = after(
        own_heads, message, gate_up, wo_core, spots
    )
    pick = np.zeros((group, tokens, group, rows), np.float32)
    for b in range(group):
        for t in range(tokens):
            pick[b, t, b, t] = 1
    pick = jnp.asarray(pick.reshape(group * tokens, group * rows), BF16)
    messages = across_planes(
        call(
            functools.partial(message_kernel, planes),
            [like(group * tokens + rows * width // pair, pair)] * planes,
            idx, own_heads, residual, pick,
        )
    )
    message = swap(message, side)
    twin = [swap(gate_up[0], core), None]
    *messages, gate_up[1], twin[0] = after(*messages, gate_up[1], twin[0])
    gate_up[1] = swap(gate_up[1], side)
    gated = call(
        functools.partial(attention_kernel, heads, planes),
        like(group * tokens, heads * HEAD_SIZE),
        idx, prefix_len, own_heads, *messages, spots, pick,
    )
    gated, message = after(gated, message)
    *down_parts, wo_near, wo_far = call(
        regroup_kernel,
        [like(sides, units, lanes)] * planes + [like(head_rows, lanes)] * 2,
        own_down, message,
    )
    gateds = [gated] + swap_planes(gated)
    wo = [wo_own, wo_core, wo_near, swap(wo_far, core)]
    down_parts[1] = swap(down_parts[1], group)
    gateds, wo, down_parts = after(gateds, wo, down_parts)
    for k in (2, 3):
        down_parts[k] = swap(down_parts[k], k * group)

    turn = np.zeros((group, planes, tokens, planes, group, tokens), np.float32)
    for i, b in enumerate(order):
        for p in range(planes):
            for t in range(tokens):
                turn[i, p, t, p, b, t] = 1
    total = devices * tokens
    turn = jnp.asarray(turn.reshape(total, total), BF16)
    keep, send = call(
        functools.partial(project_kernel, planes),
        [like(total // 2, width)] * 2,
        idx, *gateds, *wo, turn,
        scratch=[
            pltpu.VMEM((planes,) + gated.shape, BF16),
            pltpu.VMEM((wo[0].shape[0], width), BF16),
        ],
    )
    share = total // group
    own, *rest = call(
        core_sum_kernel,
        [like(share, width, dtype=F32)] + [like(share, width)] * len(steps),
        keep, swap(send, core),
    )
    rest, gate_up[1] = after(rest, gate_up[1])
    hidden = call(
        functools.partial(hidden_kernel, planes, tokens),
        like(share, width),
        idx, own, *[swap(x, b) for x, b in zip(rest, steps)], *messages,
    )
    hidden, gate_up[1], down_parts[2] = after(hidden, gate_up[1], down_parts[2])
    twin[1] = swap(gate_up[1], core)
    blocks = [hidden] + [swap(hidden, b) for b in steps]
    same = jnp.eye(len(blocks) * share, dtype=BF16)
    pieces = [x for both in zip(gate_up, twin) for x in both]
    many = len(blocks) * share
    keep, *sends = call(
        functools.partial(gate_up_kernel, len(blocks), per, planes),
        [like(many + ROW_TILE, 2 * units, dtype=F32)]
        + [like(many + ROW_TILE, 2 * units)] * (planes - 1),
        idx, *blocks, *pieces, norm_gain.reshape(planes, 1, width), same,
        scratch=[pltpu.VMEM((many, width), BF16)],
    )
    sends, down_parts = after(sends, down_parts)
    totals = across_planes([keep] + sends)
    downs = call(stack_kernel, like(planes, *down_parts[0].shape), *down_parts)
    own, *rest = call(
        functools.partial(down_kernel, planes, per, features),
        [like(planes, share, width, dtype=F32)] + [like(planes, share, width)] * len(steps),
        idx, *totals, downs, swap(downs, core), same,
    )
    parts = call(
        functools.partial(plane_sum_kernel, planes, tokens),
        [like(planes + 1, rows, width)] * planes,
        idx, hidden, own, *[swap(x, b) for x, b in zip(rest, steps)],
    )
    return call(
        functools.partial(last_kernel, planes, tokens),
        like(tokens, features),
        idx, *across_planes(parts),
        scratch=[pltpu.VMEM((planes, rows, width), F32)],
    )


def tokens_can_travel(n_blk, n_uly, kv_heads, token_count, unit_count):
    def power(n):
        return n > 0 and not n & (n - 1)

    per = kv_heads // n_uly
    return (
        power(n_blk)
        and power(n_uly)
        and power(kv_heads)
        and per > 1
        and n_blk % per == 0
        and token_count < unit_count // n_uly
    )


def solution(mesh):
    n_blk, n_uly = mesh.shape["blk"], mesh.shape["uly"]

    def per_device(*args):
        residual, key_projection, gate_weight = args[0], args[2], args[9]
        travel = tokens_can_travel(
            n_blk,
            n_uly,
            key_projection.shape[1] // HEAD_SIZE,
            residual.shape[0] * n_blk * n_uly,
            gate_weight.shape[1] * n_uly,
        )
        if travel:
            return move_tokens(n_blk, n_uly, *args)
        return move_weights(*args)

    return jax.shard_map(
        per_device,
        mesh=mesh,
        in_specs=(
            P(("blk", "uly"), None),
            P(("blk", "uly"), None),
            P(("blk", "uly"), None),
            P(("blk", "uly"), None),
            P(("blk", "uly"), None),
            P(),
            P(),
            P("uly", "blk"),
            P(),
            P("blk", "uly"),
            P("blk", "uly"),
            P("uly", "blk"),
        ),
        out_specs=P(("blk", "uly"), None),
        check_vma=False,
    )
```

```python
import functools
import math

import jax
import jax.numpy as jnp
import numpy as np
from jax import lax
from jax.experimental import pallas as pl
from jax.experimental.pallas import tpu as pltpu
from jax.sharding import PartitionSpec as P

HEAD_SIZE = 128
ROW_TILE = 16
HIDE = -1e30
F32 = jnp.float32
BF16 = jnp.bfloat16
VMEM = pl.BlockSpec(memory_space=pltpu.VMEM)
SMEM = pl.BlockSpec(memory_space=pltpu.SMEM)
NT = (((1,), (1,)), ((), ()))


def move_weights(
    residual,
    query_projection,
    key_projection,
    value_projection,
    gate_proj,
    positions,
    prefix_len,
    out_weight,
    norm_gain,
    gate_weight,
    up_weight,
    down_weight,
):
    q_loc, k_loc, v_loc, g_loc = (
        lax.all_to_all(query_projection, "uly", split_axis=1, concat_axis=0, tiled=True),
        lax.all_to_all(key_projection, "uly", split_axis=1, concat_axis=0, tiled=True),
        lax.all_to_all(value_projection, "uly", split_axis=1, concat_axis=0, tiled=True),
        lax.all_to_all(gate_proj, "uly", split_axis=1, concat_axis=0, tiled=True),
    )
    row_count = q_loc.shape[0]
    kv_heads = k_loc.shape[1] // HEAD_SIZE
    q_heads = q_loc.shape[1] // HEAD_SIZE
    heads_per_group = q_heads // kv_heads
    score_scale = 1.0 / math.sqrt(HEAD_SIZE)
    blk_index = lax.axis_index("blk")
    query_pos = lax.dynamic_slice_in_dim(positions, blk_index * row_count, row_count)
    prefix = prefix_len[0]
    query_heads = q_loc.reshape(row_count, kv_heads, heads_per_group, HEAD_SIZE)
    wo_full, wg_full, wu_full, wd_full = (
        lax.all_gather(out_weight, "blk", axis=1, tiled=True),
        lax.all_gather(gate_weight, "blk", axis=0, tiled=True),
        lax.all_gather(up_weight, "blk", axis=0, tiled=True),
        lax.all_gather(down_weight, "blk", axis=1, tiled=True),
    )
    key_part = lax.all_gather(k_loc, "blk", axis=0, tiled=True)
    value_part = lax.all_gather(v_loc, "blk", axis=0, tiled=True)
    key_count = key_part.shape[0]
    scores = (
        jnp.einsum(
            "bkgd,skd->bkgs",
            query_heads,
            key_part.reshape(key_count, kv_heads, HEAD_SIZE),
            preferred_element_type=F32,
        )
        * score_scale
    )
    visible = (positions[None, :] <= query_pos[:, None]) | (positions[None, :] < prefix)
    scores = jnp.where(visible[:, None, None, :], scores, -jnp.inf)
    row_max = jnp.max(scores, axis=-1)
    exp_scores = jnp.exp(scores - row_max[..., None])
    denom = jnp.sum(exp_scores, axis=-1)
    probs = exp_scores.astype(BF16)
    weighted = jnp.einsum(
        "bkgs,skd->bkgd",
        probs,
        value_part.reshape(key_count, kv_heads, HEAD_SIZE),
        preferred_element_type=F32,
    )
    attended = (weighted / denom[..., None]).reshape(row_count, q_heads * HEAD_SIZE)
    gated_out = (attended * jax.nn.sigmoid(g_loc.astype(F32))).astype(BF16)
    head_partial = jnp.dot(gated_out, wo_full, preferred_element_type=F32)
    projected = lax.psum_scatter(
        head_partial.astype(BF16), "uly", scatter_dimension=0, tiled=True
    ).astype(F32)
    hidden_f = (residual.astype(F32) + projected).astype(BF16).astype(F32)
    mean_sq = jnp.mean(hidden_f * hidden_f, axis=-1, keepdims=True)
    normed = (hidden_f * lax.rsqrt(mean_sq + 1e-06) * norm_gain).astype(BF16)
    group_rows = lax.all_gather(normed, "uly", axis=0, tiled=True)
    gate_sum = jnp.dot(group_rows, wg_full, preferred_element_type=F32)
    up_sum = jnp.dot(group_rows, wu_full, preferred_element_type=F32)
    activated = (jax.nn.silu(gate_sum) * up_sum).astype(BF16)
    ffn_partial = jnp.dot(activated, wd_full, preferred_element_type=F32)
    ffn_out = lax.psum_scatter(
        ffn_partial.astype(BF16), "uly", scatter_dimension=0, tiled=True
    ).astype(F32)
    return (hidden_f + ffn_out).astype(BF16)


def dot(a, b):
    return jnp.dot(a, b, preferred_element_type=F32)


def pack_heads_kernel(head_of, *refs):
    many = (len(refs) - 2) // 2
    parts, out, held, sems = refs[:many], refs[many], refs[many + 1:-1], refs[-1]
    copies = [
        pltpu.make_async_copy(part, spot, sems.at[i])
        for i, (part, spot) in enumerate(zip(parts, held))
    ]
    for copy in copies:
        copy.start()
    out[...] = jnp.zeros_like(out)
    tokens = parts[0].shape[0]
    start = 0
    for copy, spot in zip(copies, held):
        copy.wait()
        width = spot.shape[1] // len(head_of)
        for r, j in enumerate(head_of):
            out[r, :tokens, start:start + width] = spot[:, j * width:(j + 1) * width]
        start += width


def message_kernel(planes, idx, heads, residual, pick, *outs):
    group, rows, _ = heads.shape
    tokens, features = residual.shape
    pair = 2 * HEAD_SIZE
    width = features // planes
    z = idx[0]
    keys = dot(pick[...], heads[:, :, :pair].reshape(group * rows, pair)).astype(BF16)
    lot = keys.shape[0]
    for k, out in enumerate(outs):
        out[:lot] = keys
        out[lot:] = jnp.zeros((out.shape[0] - lot, pair), BF16)
        for c in range(width // pair):
            at = pl.ds(pl.multiple_of((z ^ k) * width + c * pair, pair), pair)
            out[lot + c * rows:lot + c * rows + tokens] = residual[:, at]


def attention_kernel(heads, planes, idx, prefix, qg, *refs):
    messages, (spots, pick, out) = refs[:planes], refs[planes:]
    group, rows, _ = qg.shape
    z, r = idx[0], idx[1]
    lot, held = group * rows, pick.shape[0]
    tokens = held // group
    keys, values, key_spot = [], [], []
    for k in range(planes):
        keys.append(messages[k][:held, :HEAD_SIZE])
        values.append(messages[k][:held, HEAD_SIZE:])
        key_spot.append(spots[z ^ k])
    keys, values = jnp.concatenate(keys), jnp.concatenate(values)
    key_spot = jnp.concatenate(key_spot, axis=1)
    i = lax.broadcasted_iota(jnp.int32, (lot, held), 0) ^ (r * rows)
    j = lax.broadcasted_iota(jnp.int32, (lot, held), 1)
    source = i // rows * tokens + jnp.minimum(i % rows, tokens - 1)
    query_spot = jnp.sum(jnp.where(source == j, spots[z], 0.0), axis=1, keepdims=True)
    visible = (key_spot <= query_spot) | (key_spot < prefix[0].astype(F32))
    bias = jnp.where(visible, 0.0, HIDE)
    scale = 1.0 / math.sqrt(HEAD_SIZE)
    done = []
    for h in range(heads):
        at = slice((h + 2) * HEAD_SIZE, (h + 3) * HEAD_SIZE)
        gate_at = slice((heads + h + 2) * HEAD_SIZE, (heads + h + 3) * HEAD_SIZE)
        q = jnp.concatenate([qg[b ^ r, :, at] for b in range(group)])
        gate = jnp.concatenate([qg[b ^ r, :, gate_at] for b in range(group)]).astype(F32)
        s = lax.dot_general(q, keys, NT, preferred_element_type=F32) * scale + bias
        e = jnp.exp(s - jnp.max(s, axis=-1, keepdims=True))
        denom = jnp.sum(e, axis=-1, keepdims=True)
        attended = dot(e.astype(BF16), values) / denom
        done.append((attended / (1.0 + jnp.exp(-gate))).astype(BF16))
    out[...] = dot(pick[...], jnp.concatenate(done, axis=1)).astype(BF16)


def project_kernel(planes, idx, *refs):
    parts = refs[:planes]
    weights, (pick, keep, send, held, wide) = refs[planes:-5], refs[-5:]
    z, q = idx[0], idx[2]
    for k in range(planes):
        held[z ^ k] = parts[k][...]
    rows, width = parts[0].shape
    x = dot(pick[...], held[...].reshape(planes * rows, width)).astype(BF16)
    lanes = weights[0].shape[1]
    for c, weight in enumerate(weights):
        wide[:, pl.ds(pl.multiple_of((q ^ c) * lanes, lanes), lanes)] = weight[...]
    y = dot(x, wide[...]).astype(BF16)
    half = y.shape[0] // 2
    keep[...] = y[:half]
    send[...] = y[half:]


def core_sum_kernel(keep, got, *outs):
    rows = outs[0].shape[0]
    for i, out in enumerate(outs):
        at = slice(i * rows, (i + 1) * rows)
        out[...] = (keep[at].astype(F32) + got[at].astype(F32)).astype(out.dtype)


def hidden_kernel(planes, tokens, idx, *refs):
    parts, messages, out = refs[:-planes - 1], refs[-planes - 1:-1], refs[-1]
    total = parts[0][...]
    for part in parts[1:]:
        total = total + part[...].astype(F32)
    width = out.shape[1]
    pair = messages[0].shape[1]
    pieces = width // pair
    rows = -(-tokens // ROW_TILE) * ROW_TILE
    for k, message in enumerate(messages):
        i = lax.broadcasted_iota(jnp.int32, (out.shape[0], rows), 0)
        j = lax.broadcasted_iota(jnp.int32, (out.shape[0], rows), 1)
        place = jnp.where((i == j + (idx[0] ^ k) * tokens) & (j < tokens), 1.0, 0.0).astype(BF16)
        lot = message.shape[0] - pieces * rows
        held = [message[lot + c * rows:lot + (c + 1) * rows] for c in range(pieces)]
        total = total + dot(place, jnp.concatenate(held, axis=1))
    out[...] = total.astype(BF16)


def stack_kernel(*refs):
    *parts, out = refs
    for k, part in enumerate(parts):
        out[k] = part[...]


def split_gate_up_kernel(planes, sides, idx, gate, up, *outs):
    units = outs[0].shape[1] // (2 * planes)
    for c, out in enumerate(outs):
        for k in range(planes):
            chip = (idx[0] ^ k) * sides + (idx[3] ^ c)
            at = pl.ds(pl.multiple_of(chip * units, units), units)
            out[:, 2 * k * units:(2 * k + 1) * units] = gate[:, at]
            out[:, (2 * k + 1) * units:(2 * k + 2) * units] = up[:, at]


def split_rows_kernel(planes, per, idx, down, heads, message, own, own_heads, core_heads):
    sides = per // 2
    units, head_rows = own.shape[1], own_heads.shape[0]
    for k in range(planes):
        for c in range(sides):
            chip = (idx[0] ^ k) * sides + (idx[3] ^ c)
            start = pl.multiple_of(chip * units, units)
            rows = down[pl.ds(start, units), :]
            if c:
                message[k * units:(k + 1) * units] = rows
            else:
                own[k] = rows
    for c in range(per):
        rows = heads[pl.ds(pl.multiple_of((idx[2] ^ c) * head_rows, head_rows), head_rows), :]
        if c == 0:
            own_heads[...] = rows
        elif c == 1:
            core_heads[...] = rows
        else:
            start = planes * units + (c - 2) * head_rows
            message[start:start + head_rows] = rows


def regroup_kernel(own, message, *outs):
    *downs, near_heads, far_heads = outs
    units, head_rows = own.shape[1], near_heads.shape[0]
    for k, out in enumerate(downs):
        out[0] = own[k]
        out[1] = message[k * units:(k + 1) * units]
    start = len(downs) * units
    near_heads[...] = message[start:start + head_rows]
    far_heads[...] = message[start + head_rows:start + 2 * head_rows]


def gate_up_kernel(blocks, per, planes, idx, *refs):
    parts, pieces = refs[:blocks], refs[blocks:blocks + per]
    gain, same, *outs, held = refs[blocks + per:]
    x = jnp.concatenate([part[...] for part in parts]).astype(F32)
    rows, width = x.shape
    lanes = width // per
    square = jnp.sum(x * x, axis=1, keepdims=True)
    held[...] = (x * gain[idx[0]]).astype(BF16)
    x = [held[:, pl.ds(pl.multiple_of((idx[2] ^ c) * lanes, lanes), lanes)] for c in range(per)]
    x = jnp.concatenate(x, axis=1)
    columns = pieces[0].shape[1] // planes
    lane = lax.broadcasted_iota(jnp.int32, (rows, HEAD_SIZE), 1)
    high = square.astype(BF16).astype(F32)
    terms = jnp.where(lane == 0, high, jnp.where(lane == 1, square - high, 0.0)).astype(BF16)
    terms = lax.dot_general(terms, same[...], (((0,), (0,)), ((), ())), preferred_element_type=F32)
    keep, near, *fars = outs
    terms = terms[:ROW_TILE]
    split = rows // 2
    for k in range(planes):
        at = slice(k * columns, (k + 1) * columns)
        total = dot(x, jnp.concatenate([piece[:, at] for piece in pieces]))
        if k < 2:
            places = [(outs[k], 0, rows)]
        else:
            places = [(fars[2 * k - 4], split, rows), (fars[2 * k - 3], 0, split)]
        for out, start, end in places:
            many = end - start
            out[:many] = total[start:end].astype(out.dtype)
            if out.shape[0] > many:
                out[many:] = jnp.zeros((ROW_TILE, columns), out.dtype)
                out[many:, :rows] = terms.astype(out.dtype)


def far_sum_kernel(rows, kept, got, out):
    total = kept[...] + got[...].astype(F32)
    out[:rows] = total[:rows].astype(BF16)
    if out.shape[0] > rows:
        square = jnp.sum(total[rows:], axis=0, keepdims=True)
        high = square.astype(BF16).astype(F32)
        row = lax.broadcasted_iota(jnp.int32, (out.shape[0] - rows, total.shape[1]), 0)
        terms = jnp.where(row == 0, high, jnp.where(row == 1, square - high, 0.0))
        out[rows:] = terms.astype(BF16)


def down_kernel(start, planes, per, features, idx, keep, got, far_head, far_part, near, far, same, *outs):
    many = same.shape[0]
    half = many // 2
    at = slice(start, start + half)
    total = keep[at] + got[at].astype(F32) + far_part[:half].astype(F32)
    terms = [keep[many:, :many], got[many:, :many].astype(F32), far_head[half:, :many].astype(F32)]
    units = total.shape[1] // 2
    square = jnp.concatenate(terms).astype(BF16)
    square = lax.dot_general(same[at], square, NT, preferred_element_type=F32)
    square = jnp.sum(square, axis=1, keepdims=True)
    factor = lax.rsqrt(square / features + 1e-06)
    gate, up = total[:, :units] * factor, total[:, units:] * factor
    activated = (gate / (1.0 + jnp.exp(-gate)) * up).astype(BF16)
    z, q = idx[0], idx[2]
    rows = outs[0].shape[1]
    for k in range(planes):
        w = [(far if c % 2 else near)[k, c // 2] for c in range(per)]
        y = dot(activated, jnp.concatenate(w, axis=1))
        lanes = w[0].shape[1]
        for c in range(per):
            at = pl.ds(pl.multiple_of((q ^ c) * lanes, lanes), lanes)
            block = y[:, c * lanes:(c + 1) * lanes]
            for i, out in enumerate(outs):
                out[z ^ k, :, at] = block[i * rows:(i + 1) * rows].astype(out.dtype)


def row_of(z, k, tokens, rows, total):
    i = lax.broadcasted_iota(jnp.int32, (rows, total), 0)
    j = lax.broadcasted_iota(jnp.int32, (rows, total), 1)
    return jnp.where((j == i + (z ^ k) * tokens) & (i < tokens), 1.0, 0.0).astype(BF16)


def plane_sum_kernel(planes, tokens, idx, hidden, *refs):
    parts, outs = refs[:-planes], refs[-planes:]
    total = parts[0][...]
    for part in parts[1:]:
        total = total + part[...].astype(F32)
    total = total.astype(BF16)
    for k, out in enumerate(outs):
        pick = row_of(idx[0], k, tokens, out.shape[1], total.shape[1])
        for p in range(planes):
            out[p] = dot(pick, total[p]).astype(BF16)
        out[planes] = dot(pick, hidden[...]).astype(BF16)


def last_kernel(planes, tokens, idx, *refs):
    *parts, out, held = refs
    width = parts[0].shape[2]
    total = parts[0][:planes].astype(F32)
    for part in parts[1:]:
        total = total + part[:planes].astype(F32)
    for k, part in enumerate(parts):
        held[idx[0] ^ k] = part[planes].astype(F32)
    for p in range(planes):
        value = held[p] + total[p]
        out[:, p * width:(p + 1) * width] = value[:tokens].astype(BF16)


def call(kernel, outs, *args, scratch=(), place=VMEM, limit=16):
    single = not isinstance(outs, list)
    shapes = [outs] if single else outs
    got = pl.pallas_call(
        kernel,
        out_shape=shapes,
        in_specs=[SMEM if a.dtype == jnp.int32 else place for a in args],
        out_specs=[VMEM] * len(shapes),
        scratch_shapes=list(scratch),
        compiler_params=pltpu.CompilerParams(vmem_limit_bytes=limit * 2**20),
    )(*args)
    return got[0] if single else list(got)


def like(*shape, dtype=BF16):
    return jax.ShapeDtypeStruct(shape, dtype)


def move_tokens(
    n_blk,
    n_uly,
    residual,
    query_projection,
    key_projection,
    value_projection,
    gate_proj,
    positions,
    prefix_len,
    out_weight,
    norm_gain,
    gate_weight,
    up_weight,
    down_weight,
):
    axes = ("blk", "uly")
    kv_heads = key_projection.shape[1] // HEAD_SIZE
    heads = query_projection.shape[1] // key_projection.shape[1]
    tokens, features = residual.shape
    rows = -(-tokens // ROW_TILE) * ROW_TILE
    group = kv_heads
    per = group // n_uly
    planes = n_blk // per
    devices = n_blk * n_uly
    me = lax.axis_index("blk") * n_uly + lax.axis_index("uly")
    z, r = me // group, me % group
    idx = jnp.stack([z, r, r // n_uly, r // (2 * n_uly)]).astype(jnp.int32)
    core = n_uly
    near = [b for b in range(group) if not b & core]
    order = near + [b ^ core for b in near]
    steps = near[1:]

    def swap(x, mask):
        return lax.ppermute(x, axes, [(i, i ^ mask) for i in range(devices)])

    def swap_planes(x):
        return [swap(x, k * group) for k in range(1, planes)]

    head_of = [(i % n_uly) * per + i // n_uly for i in range(group)]
    plane_groups = [[p * group + i for i in range(group)] for p in range(planes)]

    def plane_exchange(x):
        return lax.all_to_all(x, axes, 0, 0, axis_index_groups=plane_groups, tiled=True)

    def after(*xs):
        return lax.optimization_barrier(xs)

    width = features // planes
    sides = per // 2
    units = gate_weight.shape[1] // (planes * sides)

    def across_planes(parts):
        return [x if not k else swap(x, k * group) for k, x in enumerate(parts)]

    pair = 2 * HEAD_SIZE
    tokens_in = (key_projection, value_projection, query_projection, gate_proj)
    head_groups = call(
        functools.partial(pack_heads_kernel, head_of),
        like(group, rows, 2 * heads * HEAD_SIZE + pair),
        *tokens_in,
        scratch=[pltpu.VMEM(x.shape, x.dtype) for x in tokens_in]
        + [pltpu.SemaphoreType.DMA((len(tokens_in),))],
        place=pl.BlockSpec(memory_space=pl.ANY),
        limit=60,
    )
    head_groups, gate_weight, up_weight, down_weight, out_weight, positions = after(
        head_groups, gate_weight, up_weight, down_weight, out_weight, positions
    )
    side = 2 * n_uly
    gate_up = call(
        functools.partial(split_gate_up_kernel, planes, sides),
        [like(gate_weight.shape[0], 2 * planes * units)] * sides,
        idx, gate_weight, up_weight,
    )
    head_rows = out_weight.shape[0] // per
    lanes = out_weight.shape[1]
    message, own_down, wo_own, wo_core = call(
        functools.partial(split_rows_kernel, planes, per),
        [
            like(planes * units + 2 * head_rows, lanes),
            like(planes, units, lanes),
            like(head_rows, lanes),
            like(head_rows, lanes),
        ],
        idx, down_weight, out_weight,
    )
    spots = positions.astype(F32).reshape(planes, 1, group * tokens)
    own_heads = plane_exchange(head_groups)
    wo_core = swap(wo_core, core)
    own_heads, message, gate_up, wo_core, spots = after(
        own_heads, message, gate_up, wo_core, spots
    )
    pick = np.zeros((group, tokens, group, rows), np.float32)
    for b in range(group):
        for t in range(tokens):
            pick[b, t, b, t] = 1
    pick = jnp.asarray(pick.reshape(group * tokens, group * rows), BF16)
    messages = across_planes(
        call(
            functools.partial(message_kernel, planes),
            [like(group * tokens + rows * width // pair, pair)] * planes,
            idx, own_heads, residual, pick,
        )
    )
    message = swap(message, side)
    twin = [swap(gate_up[0], core), None]
    *messages, gate_up[1], twin[0] = after(*messages, gate_up[1], twin[0])
    gate_up[1] = swap(gate_up[1], side)
    gated = call(
        functools.partial(attention_kernel, heads, planes),
        like(group * tokens, heads * HEAD_SIZE),
        idx, prefix_len, own_heads, *messages, spots, pick,
    )
    gated, message = after(gated, message)
    *down_parts, wo_near, wo_far = call(
        regroup_kernel,
        [like(sides, units, lanes)] * planes + [like(head_rows, lanes)] * 2,
        own_down, message,
    )
    gateds = [gated] + swap_planes(gated)
    wo = [wo_own, wo_core, wo_near, swap(wo_far, core)]
    down_parts[1] = swap(down_parts[1], group)
    gateds, wo, down_parts = after(gateds, wo, down_parts)
    for k in (2, 3):
        down_parts[k] = swap(down_parts[k], k * group)

    turn = np.zeros((group, planes, tokens, planes, group, tokens), np.float32)
    for i, b in enumerate(order):
        for p in range(planes):
            for t in range(tokens):
                turn[i, p, t, p, b, t] = 1
    total = devices * tokens
    turn = jnp.asarray(turn.reshape(total, total), BF16)
    keep, send = call(
        functools.partial(project_kernel, planes),
        [like(total // 2, width)] * 2,
        idx, *gateds, *wo, turn,
        scratch=[
            pltpu.VMEM((planes,) + gated.shape, BF16),
            pltpu.VMEM((wo[0].shape[0], width), BF16),
        ],
    )
    share = total // group
    own, *rest = call(
        core_sum_kernel,
        [like(share, width, dtype=F32)] + [like(share, width)] * len(steps),
        keep, swap(send, core),
    )
    rest, gate_up[1] = after(rest, gate_up[1])
    hidden = call(
        functools.partial(hidden_kernel, planes, tokens),
        like(share, width),
        idx, own, *[swap(x, b) for x, b in zip(rest, steps)], *messages,
    )
    hidden, gate_up[1], down_parts[2] = after(hidden, gate_up[1], down_parts[2])
    twin[1] = swap(gate_up[1], core)
    blocks = [hidden] + [swap(hidden, b) for b in steps]
    same = jnp.eye(len(blocks) * share, dtype=BF16)
    pieces = [x for both in zip(gate_up, twin) for x in both]
    many = len(blocks) * share
    group_far = planes // 2 * group
    split = many // 2
    ends = (split + ROW_TILE, split)
    keep, near_send, *fars = call(
        functools.partial(gate_up_kernel, len(blocks), per, planes),
        [like(many + ROW_TILE, 2 * units, dtype=F32), like(many + ROW_TILE, 2 * units)]
        + [like(rows_, 2 * units, dtype=F32) for rows_ in ends]
        + [like(rows_, 2 * units) for rows_ in ends],
        idx, *blocks, *pieces, norm_gain.reshape(planes, 1, width), same,
        scratch=[pltpu.VMEM((many, width), BF16)],
    )
    far_keeps, far_sends = fars[:2], fars[2:]
    far_sends[0], down_parts = after(far_sends[0], down_parts)

    def far_sum(i, got):
        return call(
            functools.partial(far_sum_kernel, split), like(ends[i], 2 * units), far_keeps[i], got
        )

    got = swap(far_sends[0], group)
    got, far_sends[1] = after(got, far_sends[1])
    far_head = swap(far_sum(0, got), group_far)
    got, near_send = after(swap(far_sends[1], group), near_send)
    far_rest = swap(far_sum(1, got), group_far)
    near_got = swap(near_send, group)
    downs = call(stack_kernel, like(planes, *down_parts[0].shape), *down_parts)
    weights = [downs, swap(downs, core), same]

    def ffn_out(start, part, dtypes):
        return call(
            functools.partial(down_kernel, start, planes, per, features),
            [like(planes, share, width, dtype=dtype) for dtype in dtypes],
            idx, keep, near_got, far_head, part, *weights,
        )

    late = ffn_out(split, far_head, [BF16, BF16])
    own, early = ffn_out(0, far_rest, [F32, BF16])
    rest = [early] + late
    parts = call(
        functools.partial(plane_sum_kernel, planes, tokens),
        [like(planes + 1, rows, width)] * planes,
        idx, hidden, own, *[swap(x, b) for x, b in zip(rest, steps)],
    )
    return call(
        functools.partial(last_kernel, planes, tokens),
        like(tokens, features),
        idx, *across_planes(parts),
        scratch=[pltpu.VMEM((planes, rows, width), F32)],
    )


def tokens_can_travel(n_blk, n_uly, kv_heads, token_count, unit_count):
    def power(n):
        return n > 0 and not n & (n - 1)

    per = kv_heads // n_uly
    return (
        power(n_blk)
        and power(n_uly)
        and power(kv_heads)
        and per > 1
        and n_blk == 4 * per
        and token_count < unit_count // n_uly
    )


def solution(mesh):
    n_blk, n_uly = mesh.shape["blk"], mesh.shape["uly"]

    def per_device(*args):
        residual, key_projection, gate_weight = args[0], args[2], args[9]
        travel = tokens_can_travel(
            n_blk,
            n_uly,
            key_projection.shape[1] // HEAD_SIZE,
            residual.shape[0] * n_blk * n_uly,
            gate_weight.shape[1] * n_uly,
        )
        if travel:
            return move_tokens(n_blk, n_uly, *args)
        return move_weights(*args)

    return jax.shard_map(
        per_device,
        mesh=mesh,
        in_specs=(
            P(("blk", "uly"), None),
            P(("blk", "uly"), None),
            P(("blk", "uly"), None),
            P(("blk", "uly"), None),
            P(("blk", "uly"), None),
            P(),
            P(),
            P("uly", "blk"),
            P(),
            P("blk", "uly"),
            P("blk", "uly"),
            P("uly", "blk"),
        ),
        out_specs=P(("blk", "uly"), None),
        check_vma=False,
    )
```

```python
import functools
import math

import jax
import jax.numpy as jnp
import numpy as np
from jax import lax
from jax.experimental import pallas as pl
from jax.experimental.pallas import tpu as pltpu
from jax.sharding import PartitionSpec as P

HEAD_SIZE = 128
ROW_TILE = 16
HIDE = -1e30
F32 = jnp.float32
BF16 = jnp.bfloat16
VMEM = pl.BlockSpec(memory_space=pltpu.VMEM)
SMEM = pl.BlockSpec(memory_space=pltpu.SMEM)
NT = (((1,), (1,)), ((), ()))


def move_weights(
    residual,
    query_projection,
    key_projection,
    value_projection,
    gate_proj,
    positions,
    prefix_len,
    out_weight,
    norm_gain,
    gate_weight,
    up_weight,
    down_weight,
):
    q_loc, k_loc, v_loc, g_loc = (
        lax.all_to_all(query_projection, "uly", split_axis=1, concat_axis=0, tiled=True),
        lax.all_to_all(key_projection, "uly", split_axis=1, concat_axis=0, tiled=True),
        lax.all_to_all(value_projection, "uly", split_axis=1, concat_axis=0, tiled=True),
        lax.all_to_all(gate_proj, "uly", split_axis=1, concat_axis=0, tiled=True),
    )
    row_count = q_loc.shape[0]
    kv_heads = k_loc.shape[1] // HEAD_SIZE
    q_heads = q_loc.shape[1] // HEAD_SIZE
    heads_per_group = q_heads // kv_heads
    score_scale = 1.0 / math.sqrt(HEAD_SIZE)
    blk_index = lax.axis_index("blk")
    query_pos = lax.dynamic_slice_in_dim(positions, blk_index * row_count, row_count)
    prefix = prefix_len[0]
    query_heads = q_loc.reshape(row_count, kv_heads, heads_per_group, HEAD_SIZE)
    wo_full, wg_full, wu_full, wd_full = (
        lax.all_gather(out_weight, "blk", axis=1, tiled=True),
        lax.all_gather(gate_weight, "blk", axis=0, tiled=True),
        lax.all_gather(up_weight, "blk", axis=0, tiled=True),
        lax.all_gather(down_weight, "blk", axis=1, tiled=True),
    )
    key_part = lax.all_gather(k_loc, "blk", axis=0, tiled=True)
    value_part = lax.all_gather(v_loc, "blk", axis=0, tiled=True)
    key_count = key_part.shape[0]
    scores = (
        jnp.einsum(
            "bkgd,skd->bkgs",
            query_heads,
            key_part.reshape(key_count, kv_heads, HEAD_SIZE),
            preferred_element_type=F32,
        )
        * score_scale
    )
    visible = (positions[None, :] <= query_pos[:, None]) | (positions[None, :] < prefix)
    scores = jnp.where(visible[:, None, None, :], scores, -jnp.inf)
    row_max = jnp.max(scores, axis=-1)
    exp_scores = jnp.exp(scores - row_max[..., None])
    denom = jnp.sum(exp_scores, axis=-1)
    probs = exp_scores.astype(BF16)
    weighted = jnp.einsum(
        "bkgs,skd->bkgd",
        probs,
        value_part.reshape(key_count, kv_heads, HEAD_SIZE),
        preferred_element_type=F32,
    )
    attended = (weighted / denom[..., None]).reshape(row_count, q_heads * HEAD_SIZE)
    gated_out = (attended * jax.nn.sigmoid(g_loc.astype(F32))).astype(BF16)
    head_partial = jnp.dot(gated_out, wo_full, preferred_element_type=F32)
    projected = lax.psum_scatter(
        head_partial.astype(BF16), "uly", scatter_dimension=0, tiled=True
    ).astype(F32)
    hidden_f = (residual.astype(F32) + projected).astype(BF16).astype(F32)
    mean_sq = jnp.mean(hidden_f * hidden_f, axis=-1, keepdims=True)
    normed = (hidden_f * lax.rsqrt(mean_sq + 1e-06) * norm_gain).astype(BF16)
    group_rows = lax.all_gather(normed, "uly", axis=0, tiled=True)
    gate_sum = jnp.dot(group_rows, wg_full, preferred_element_type=F32)
    up_sum = jnp.dot(group_rows, wu_full, preferred_element_type=F32)
    activated = (jax.nn.silu(gate_sum) * up_sum).astype(BF16)
    ffn_partial = jnp.dot(activated, wd_full, preferred_element_type=F32)
    ffn_out = lax.psum_scatter(
        ffn_partial.astype(BF16), "uly", scatter_dimension=0, tiled=True
    ).astype(F32)
    return (hidden_f + ffn_out).astype(BF16)


def dot(a, b):
    return jnp.dot(a, b, preferred_element_type=F32)


def pack_heads_kernel(head_of, *refs):
    many = (len(refs) - 2) // 2
    parts, out, held, sems = refs[:many], refs[many], refs[many + 1:-1], refs[-1]
    copies = [
        pltpu.make_async_copy(part, spot, sems.at[i])
        for i, (part, spot) in enumerate(zip(parts, held))
    ]
    for copy in copies:
        copy.start()
    out[...] = jnp.zeros_like(out)
    tokens = parts[0].shape[0]
    start = 0
    for copy, spot in zip(copies, held):
        copy.wait()
        width = spot.shape[1] // len(head_of)
        for r, j in enumerate(head_of):
            out[r, :tokens, start:start + width] = spot[:, j * width:(j + 1) * width]
        start += width


def message_kernel(planes, idx, heads, residual, pick, *outs):
    group, rows, _ = heads.shape
    tokens, features = residual.shape
    pair = 2 * HEAD_SIZE
    width = features // planes
    z = idx[0]
    keys = dot(pick[...], heads[:, :, :pair].reshape(group * rows, pair)).astype(BF16)
    lot = keys.shape[0]
    for k, out in enumerate(outs):
        out[:lot] = keys
        out[lot:] = jnp.zeros((out.shape[0] - lot, pair), BF16)
        for c in range(width // pair):
            at = pl.ds(pl.multiple_of((z ^ k) * width + c * pair, pair), pair)
            out[lot + c * rows:lot + c * rows + tokens] = residual[:, at]


def attention_kernel(heads, planes, idx, prefix, qg, *refs):
    messages, (spots, pick, out) = refs[:planes], refs[planes:]
    group, rows, _ = qg.shape
    z, r = idx[0], idx[1]
    lot, held = group * rows, pick.shape[0]
    tokens = held // group
    keys, values, key_spot = [], [], []
    for k in range(planes):
        keys.append(messages[k][:held, :HEAD_SIZE])
        values.append(messages[k][:held, HEAD_SIZE:])
        key_spot.append(spots[z ^ k])
    keys, values = jnp.concatenate(keys), jnp.concatenate(values)
    key_spot = jnp.concatenate(key_spot, axis=1)
    i = lax.broadcasted_iota(jnp.int32, (lot, held), 0) ^ (r * rows)
    j = lax.broadcasted_iota(jnp.int32, (lot, held), 1)
    source = i // rows * tokens + jnp.minimum(i % rows, tokens - 1)
    query_spot = jnp.sum(jnp.where(source == j, spots[z], 0.0), axis=1, keepdims=True)
    visible = (key_spot <= query_spot) | (key_spot < prefix[0].astype(F32))
    bias = jnp.where(visible, 0.0, HIDE)
    scale = 1.0 / math.sqrt(HEAD_SIZE)
    done = []
    for h in range(heads):
        at = slice((h + 2) * HEAD_SIZE, (h + 3) * HEAD_SIZE)
        gate_at = slice((heads + h + 2) * HEAD_SIZE, (heads + h + 3) * HEAD_SIZE)
        q = jnp.concatenate([qg[b ^ r, :, at] for b in range(group)])
        gate = jnp.concatenate([qg[b ^ r, :, gate_at] for b in range(group)]).astype(F32)
        s = lax.dot_general(q, keys, NT, preferred_element_type=F32) * scale + bias
        e = jnp.exp(s - jnp.max(s, axis=-1, keepdims=True))
        denom = jnp.sum(e, axis=-1, keepdims=True)
        attended = dot(e.astype(BF16), values) / denom
        done.append((attended / (1.0 + jnp.exp(-gate))).astype(BF16))
    out[...] = dot(pick[...], jnp.concatenate(done, axis=1)).astype(BF16)


def project_kernel(planes, idx, *refs):
    parts = refs[:planes]
    weights, (pick, keep, send, held, wide) = refs[planes:-5], refs[-5:]
    z, q = idx[0], idx[2]
    for k in range(planes):
        held[z ^ k] = parts[k][...]
    rows, width = parts[0].shape
    x = dot(pick[...], held[...].reshape(planes * rows, width)).astype(BF16)
    lanes = weights[0].shape[1]
    for c, weight in enumerate(weights):
        wide[:, pl.ds(pl.multiple_of((q ^ c) * lanes, lanes), lanes)] = weight[...]
    y = dot(x, wide[...]).astype(BF16)
    half = y.shape[0] // 2
    keep[...] = y[:half]
    send[...] = y[half:]


def core_sum_kernel(keep, got, *outs):
    rows = outs[0].shape[0]
    for i, out in enumerate(outs):
        at = slice(i * rows, (i + 1) * rows)
        out[...] = (keep[at].astype(F32) + got[at].astype(F32)).astype(out.dtype)


def hidden_kernel(planes, tokens, idx, *refs):
    parts, messages, out = refs[:-planes - 1], refs[-planes - 1:-1], refs[-1]
    total = parts[0][...]
    for part in parts[1:]:
        total = total + part[...].astype(F32)
    width = out.shape[1]
    pair = messages[0].shape[1]
    pieces = width // pair
    rows = -(-tokens // ROW_TILE) * ROW_TILE
    for k, message in enumerate(messages):
        i = lax.broadcasted_iota(jnp.int32, (out.shape[0], rows), 0)
        j = lax.broadcasted_iota(jnp.int32, (out.shape[0], rows), 1)
        place = jnp.where((i == j + (idx[0] ^ k) * tokens) & (j < tokens), 1.0, 0.0).astype(BF16)
        lot = message.shape[0] - pieces * rows
        held = [message[lot + c * rows:lot + (c + 1) * rows] for c in range(pieces)]
        total = total + dot(place, jnp.concatenate(held, axis=1))
    out[...] = total.astype(BF16)


def stack_kernel(*refs):
    *parts, out = refs
    for k, part in enumerate(parts):
        out[k] = part[...]


def split_gate_up_kernel(planes, sides, idx, gate, up, *outs):
    units = outs[0].shape[1] // (2 * planes)
    for c, out in enumerate(outs):
        for k in range(planes):
            chip = (idx[0] ^ k) * sides + (idx[3] ^ c)
            at = pl.ds(pl.multiple_of(chip * units, units), units)
            out[:, 2 * k * units:(2 * k + 1) * units] = gate[:, at]
            out[:, (2 * k + 1) * units:(2 * k + 2) * units] = up[:, at]


def split_rows_kernel(planes, per, idx, down, heads, message, own, own_heads, core_heads):
    sides = per // 2
    units, head_rows = own.shape[1], own_heads.shape[0]
    for k in range(planes):
        for c in range(sides):
            chip = (idx[0] ^ k) * sides + (idx[3] ^ c)
            start = pl.multiple_of(chip * units, units)
            rows = down[pl.ds(start, units), :]
            if c:
                message[k * units:(k + 1) * units] = rows
            else:
                own[k] = rows
    for c in range(per):
        rows = heads[pl.ds(pl.multiple_of((idx[2] ^ c) * head_rows, head_rows), head_rows), :]
        if c == 0:
            own_heads[...] = rows
        elif c == 1:
            core_heads[...] = rows
        else:
            start = planes * units + (c - 2) * head_rows
            message[start:start + head_rows] = rows


def regroup_kernel(own, message, *outs):
    *downs, near_heads, far_heads = outs
    units, head_rows = own.shape[1], near_heads.shape[0]
    for k, out in enumerate(downs):
        out[0] = own[k]
        out[1] = message[k * units:(k + 1) * units]
    start = len(downs) * units
    near_heads[...] = message[start:start + head_rows]
    far_heads[...] = message[start + head_rows:start + 2 * head_rows]


def gate_up_kernel(blocks, per, planes, idx, *refs):
    parts, pieces = refs[:blocks], refs[blocks:blocks + per]
    gain, same, *outs, held = refs[blocks + per:]
    x = jnp.concatenate([part[...] for part in parts]).astype(F32)
    rows, width = x.shape
    lanes = width // per
    square = jnp.sum(x * x, axis=1, keepdims=True)
    held[...] = (x * gain[idx[0]]).astype(BF16)
    x = [held[:, pl.ds(pl.multiple_of((idx[2] ^ c) * lanes, lanes), lanes)] for c in range(per)]
    x = jnp.concatenate(x, axis=1)
    columns = pieces[0].shape[1] // planes
    lane = lax.broadcasted_iota(jnp.int32, (rows, HEAD_SIZE), 1)
    high = square.astype(BF16).astype(F32)
    terms = jnp.where(lane == 0, high, jnp.where(lane == 1, square - high, 0.0)).astype(BF16)
    terms = lax.dot_general(terms, same[...], (((0,), (0,)), ((), ())), preferred_element_type=F32)
    keep, near, *fars = outs
    terms = terms[:ROW_TILE]
    split = rows // 2
    for k in range(planes):
        at = slice(k * columns, (k + 1) * columns)
        total = dot(x, jnp.concatenate([piece[:, at] for piece in pieces]))
        if k < 2:
            places = [(outs[k], 0, rows)]
        else:
            places = [(fars[2 * k - 4], split, rows), (fars[2 * k - 3], 0, split)]
        for out, start, end in places:
            many = end - start
            out[:many] = total[start:end].astype(out.dtype)
            if out.shape[0] > many:
                out[many:] = jnp.zeros((ROW_TILE, columns), out.dtype)
                out[many:, :rows] = terms.astype(out.dtype)


def far_sum_kernel(rows, kept, got, out):
    total = kept[...] + got[...].astype(F32)
    out[:rows] = total[:rows].astype(BF16)
    if out.shape[0] > rows:
        square = jnp.sum(total[rows:], axis=0, keepdims=True)
        high = square.astype(BF16).astype(F32)
        row = lax.broadcasted_iota(jnp.int32, (out.shape[0] - rows, total.shape[1]), 0)
        terms = jnp.where(row == 0, high, jnp.where(row == 1, square - high, 0.0))
        out[rows:] = terms.astype(BF16)


def down_kernel(start, planes, per, features, idx, keep, got, far_head, far_part, near, far, same, *outs):
    many = same.shape[0]
    half = many // 2
    at = slice(start, start + half)
    total = keep[at] + got[at].astype(F32) + far_part[:half].astype(F32)
    terms = [keep[many:, :many], got[many:, :many].astype(F32), far_head[half:, :many].astype(F32)]
    units = total.shape[1] // 2
    square = jnp.concatenate(terms).astype(BF16)
    square = lax.dot_general(same[at], square, NT, preferred_element_type=F32)
    square = jnp.sum(square, axis=1, keepdims=True)
    factor = lax.rsqrt(square / features + 1e-06)
    gate, up = total[:, :units] * factor, total[:, units:] * factor
    activated = (gate / (1.0 + jnp.exp(-gate)) * up).astype(BF16)
    z, q = idx[0], idx[2]
    rows = outs[0].shape[1]
    for k in range(planes):
        w = [(far if c % 2 else near)[k, c // 2] for c in range(per)]
        y = dot(activated, jnp.concatenate(w, axis=1))
        lanes = w[0].shape[1]
        for c in range(per):
            at = pl.ds(pl.multiple_of((q ^ c) * lanes, lanes), lanes)
            block = y[:, c * lanes:(c + 1) * lanes]
            for i, out in enumerate(outs):
                out[z ^ k, :, at] = block[i * rows:(i + 1) * rows].astype(out.dtype)


def plane_sum_kernel(planes, tokens, idx, hidden, *refs):
    parts, outs = refs[:-planes], refs[-planes:]
    total = parts[0][...]
    for part in parts[1:]:
        total = total + part[...].astype(F32)
    total = total.astype(BF16)
    share = hidden.shape[0]
    source = jnp.concatenate([total[p] for p in range(planes)] + [hidden[...]])
    for k, out in enumerate(outs):
        i = lax.broadcasted_iota(jnp.int32, (out.shape[0], source.shape[0]), 0)
        j = lax.broadcasted_iota(jnp.int32, (out.shape[0], source.shape[0]), 1)
        spot = i // tokens * share + (idx[0] ^ k) * tokens + i % tokens
        pick = jnp.where((spot == j) & (i < (planes + 1) * tokens), 1.0, 0.0).astype(BF16)
        out[...] = dot(pick, source).astype(BF16)


def last_kernel(planes, tokens, idx, *refs):
    *parts, out, held = refs
    width = parts[0].shape[1]
    total = parts[0][...].astype(F32)
    for part in parts[1:]:
        total = total + part[...].astype(F32)
    end = planes * tokens
    for k, part in enumerate(parts):
        held[idx[0] ^ k, :tokens] = part[...].astype(F32)[end:end + tokens]
    for p in range(planes):
        value = held[p, :tokens] + total[p * tokens:(p + 1) * tokens]
        out[:, p * width:(p + 1) * width] = value.astype(BF16)


def call(kernel, outs, *args, scratch=(), place=VMEM, limit=16):
    single = not isinstance(outs, list)
    shapes = [outs] if single else outs
    got = pl.pallas_call(
        kernel,
        out_shape=shapes,
        in_specs=[SMEM if a.dtype == jnp.int32 else place for a in args],
        out_specs=[VMEM] * len(shapes),
        scratch_shapes=list(scratch),
        compiler_params=pltpu.CompilerParams(vmem_limit_bytes=limit * 2**20),
    )(*args)
    return got[0] if single else list(got)


def like(*shape, dtype=BF16):
    return jax.ShapeDtypeStruct(shape, dtype)


def move_tokens(
    n_blk,
    n_uly,
    residual,
    query_projection,
    key_projection,
    value_projection,
    gate_proj,
    positions,
    prefix_len,
    out_weight,
    norm_gain,
    gate_weight,
    up_weight,
    down_weight,
):
    axes = ("blk", "uly")
    kv_heads = key_projection.shape[1] // HEAD_SIZE
    heads = query_projection.shape[1] // key_projection.shape[1]
    tokens, features = residual.shape
    rows = -(-tokens // ROW_TILE) * ROW_TILE
    group = kv_heads
    per = group // n_uly
    planes = n_blk // per
    devices = n_blk * n_uly
    me = lax.axis_index("blk") * n_uly + lax.axis_index("uly")
    z, r = me // group, me % group
    idx = jnp.stack([z, r, r // n_uly, r // (2 * n_uly)]).astype(jnp.int32)
    core = n_uly
    near = [b for b in range(group) if not b & core]
    order = near + [b ^ core for b in near]
    steps = near[1:]

    def swap(x, mask):
        return lax.ppermute(x, axes, [(i, i ^ mask) for i in range(devices)])

    def swap_planes(x):
        return [swap(x, k * group) for k in range(1, planes)]

    head_of = [(i % n_uly) * per + i // n_uly for i in range(group)]
    plane_groups = [[p * group + i for i in range(group)] for p in range(planes)]

    def plane_exchange(x):
        return lax.all_to_all(x, axes, 0, 0, axis_index_groups=plane_groups, tiled=True)

    def after(*xs):
        return lax.optimization_barrier(xs)

    width = features // planes
    sides = per // 2
    units = gate_weight.shape[1] // (planes * sides)

    def across_planes(parts):
        return [x if not k else swap(x, k * group) for k, x in enumerate(parts)]

    pair = 2 * HEAD_SIZE
    tokens_in = (key_projection, value_projection, query_projection, gate_proj)
    head_groups = call(
        functools.partial(pack_heads_kernel, head_of),
        like(group, rows, 2 * heads * HEAD_SIZE + pair),
        *tokens_in,
        scratch=[pltpu.VMEM(x.shape, x.dtype) for x in tokens_in]
        + [pltpu.SemaphoreType.DMA((len(tokens_in),))],
        place=pl.BlockSpec(memory_space=pl.ANY),
        limit=60,
    )
    head_groups, gate_weight, up_weight, down_weight, out_weight, positions = after(
        head_groups, gate_weight, up_weight, down_weight, out_weight, positions
    )
    side = 2 * n_uly
    gate_up = call(
        functools.partial(split_gate_up_kernel, planes, sides),
        [like(gate_weight.shape[0], 2 * planes * units)] * sides,
        idx, gate_weight, up_weight,
    )
    head_rows = out_weight.shape[0] // per
    lanes = out_weight.shape[1]
    message, own_down, wo_own, wo_core = call(
        functools.partial(split_rows_kernel, planes, per),
        [
            like(planes * units + 2 * head_rows, lanes),
            like(planes, units, lanes),
            like(head_rows, lanes),
            like(head_rows, lanes),
        ],
        idx, down_weight, out_weight,
    )
    spots = positions.astype(F32).reshape(planes, 1, group * tokens)
    own_heads = plane_exchange(head_groups)
    wo_core = swap(wo_core, core)
    own_heads, message, gate_up, wo_core, spots = after(
        own_heads, message, gate_up, wo_core, spots
    )
    pick = np.zeros((group, tokens, group, rows), np.float32)
    for b in range(group):
        for t in range(tokens):
            pick[b, t, b, t] = 1
    pick = jnp.asarray(pick.reshape(group * tokens, group * rows), BF16)
    messages = across_planes(
        call(
            functools.partial(message_kernel, planes),
            [like(group * tokens + rows * width // pair, pair)] * planes,
            idx, own_heads, residual, pick,
        )
    )
    message = swap(message, side)
    twin = [swap(gate_up[0], core), None]
    *messages, gate_up[1], twin[0] = after(*messages, gate_up[1], twin[0])
    gate_up[1] = swap(gate_up[1], side)
    gated = call(
        functools.partial(attention_kernel, heads, planes),
        like(group * tokens, heads * HEAD_SIZE),
        idx, prefix_len, own_heads, *messages, spots, pick,
    )
    gated, message = after(gated, message)
    *down_parts, wo_near, wo_far = call(
        regroup_kernel,
        [like(sides, units, lanes)] * planes + [like(head_rows, lanes)] * 2,
        own_down, message,
    )
    gateds = [gated] + swap_planes(gated)
    wo = [wo_own, wo_core, wo_near, swap(wo_far, core)]
    down_parts[1] = swap(down_parts[1], group)
    gateds, wo, down_parts = after(gateds, wo, down_parts)
    for k in (2, 3):
        down_parts[k] = swap(down_parts[k], k * group)

    turn = np.zeros((group, planes, tokens, planes, group, tokens), np.float32)
    for i, b in enumerate(order):
        for p in range(planes):
            for t in range(tokens):
                turn[i, p, t, p, b, t] = 1
    total = devices * tokens
    turn = jnp.asarray(turn.reshape(total, total), BF16)
    keep, send = call(
        functools.partial(project_kernel, planes),
        [like(total // 2, width)] * 2,
        idx, *gateds, *wo, turn,
        scratch=[
            pltpu.VMEM((planes,) + gated.shape, BF16),
            pltpu.VMEM((wo[0].shape[0], width), BF16),
        ],
    )
    share = total // group
    own, *rest = call(
        core_sum_kernel,
        [like(share, width, dtype=F32)] + [like(share, width)] * len(steps),
        keep, swap(send, core),
    )
    rest, gate_up[1] = after(rest, gate_up[1])
    hidden = call(
        functools.partial(hidden_kernel, planes, tokens),
        like(share, width),
        idx, own, *[swap(x, b) for x, b in zip(rest, steps)], *messages,
    )
    hidden, gate_up[1], down_parts[2] = after(hidden, gate_up[1], down_parts[2])
    twin[1] = swap(gate_up[1], core)
    blocks = [hidden] + [swap(hidden, b) for b in steps]
    same = jnp.eye(len(blocks) * share, dtype=BF16)
    pieces = [x for both in zip(gate_up, twin) for x in both]
    many = len(blocks) * share
    group_far = planes // 2 * group
    split = many // 2
    ends = (split + ROW_TILE, split)
    keep, near_send, *fars = call(
        functools.partial(gate_up_kernel, len(blocks), per, planes),
        [like(many + ROW_TILE, 2 * units, dtype=F32), like(many + ROW_TILE, 2 * units)]
        + [like(rows_, 2 * units, dtype=F32) for rows_ in ends]
        + [like(rows_, 2 * units) for rows_ in ends],
        idx, *blocks, *pieces, norm_gain.reshape(planes, 1, width), same,
        scratch=[pltpu.VMEM((many, width), BF16)],
    )
    far_keeps, far_sends = fars[:2], fars[2:]
    far_sends[0], down_parts = after(far_sends[0], down_parts)

    def far_sum(i, got):
        return call(
            functools.partial(far_sum_kernel, split), like(ends[i], 2 * units), far_keeps[i], got
        )

    got = swap(far_sends[0], group)
    far_head = swap(far_sum(0, got), group_far)
    got, near_send = after(swap(far_sends[1], group), near_send)
    far_rest = swap(far_sum(1, got), group_far)
    near_got = swap(near_send, group)
    downs = call(stack_kernel, like(planes, *down_parts[0].shape), *down_parts)
    weights = [downs, swap(downs, core), same]

    def ffn_out(start, part, dtypes):
        return call(
            functools.partial(down_kernel, start, planes, per, features),
            [like(planes, share, width, dtype=dtype) for dtype in dtypes],
            idx, keep, near_got, far_head, part, *weights,
        )

    late = ffn_out(split, far_head, [BF16, BF16])
    own, early = ffn_out(0, far_rest, [F32, BF16])
    rest = [early] + late
    parts = call(
        functools.partial(plane_sum_kernel, planes, tokens),
        [like(-(-(planes + 1) * tokens // ROW_TILE) * ROW_TILE, width)] * planes,
        idx, hidden, own, *[swap(x, b) for x, b in zip(rest, steps)],
    )
    return call(
        functools.partial(last_kernel, planes, tokens),
        like(tokens, features),
        idx, *across_planes(parts),
        scratch=[pltpu.VMEM((planes, rows, width), F32)],
    )


def tokens_can_travel(n_blk, n_uly, kv_heads, token_count, unit_count):
    def power(n):
        return n > 0 and not n & (n - 1)

    per = kv_heads // n_uly
    return (
        power(n_blk)
        and power(n_uly)
        and power(kv_heads)
        and per > 1
        and n_blk == 4 * per
        and token_count < unit_count // n_uly
    )


def solution(mesh):
    n_blk, n_uly = mesh.shape["blk"], mesh.shape["uly"]

    def per_device(*args):
        residual, key_projection, gate_weight = args[0], args[2], args[9]
        travel = tokens_can_travel(
            n_blk,
            n_uly,
            key_projection.shape[1] // HEAD_SIZE,
            residual.shape[0] * n_blk * n_uly,
            gate_weight.shape[1] * n_uly,
        )
        if travel:
            return move_tokens(n_blk, n_uly, *args)
        return move_weights(*args)

    return jax.shard_map(
        per_device,
        mesh=mesh,
        in_specs=(
            P(("blk", "uly"), None),
            P(("blk", "uly"), None),
            P(("blk", "uly"), None),
            P(("blk", "uly"), None),
            P(("blk", "uly"), None),
            P(),
            P(),
            P("uly", "blk"),
            P(),
            P("blk", "uly"),
            P("blk", "uly"),
            P("uly", "blk"),
        ),
        out_specs=P(("blk", "uly"), None),
        check_vma=False,
    )
```

```python
import functools
import math

import jax
import jax.numpy as jnp
import numpy as np
from jax import lax
from jax.experimental import pallas as pl
from jax.experimental.pallas import tpu as pltpu
from jax.sharding import PartitionSpec as P

HEAD_SIZE = 128
ROW_TILE = 16
HIDE = -1e30
F32 = jnp.float32
BF16 = jnp.bfloat16
VMEM = pl.BlockSpec(memory_space=pltpu.VMEM)
SMEM = pl.BlockSpec(memory_space=pltpu.SMEM)
NT = (((1,), (1,)), ((), ()))


def move_weights(
    residual,
    query_projection,
    key_projection,
    value_projection,
    gate_proj,
    positions,
    prefix_len,
    out_weight,
    norm_gain,
    gate_weight,
    up_weight,
    down_weight,
):
    q_loc, k_loc, v_loc, g_loc = (
        lax.all_to_all(query_projection, "uly", split_axis=1, concat_axis=0, tiled=True),
        lax.all_to_all(key_projection, "uly", split_axis=1, concat_axis=0, tiled=True),
        lax.all_to_all(value_projection, "uly", split_axis=1, concat_axis=0, tiled=True),
        lax.all_to_all(gate_proj, "uly", split_axis=1, concat_axis=0, tiled=True),
    )
    row_count = q_loc.shape[0]
    kv_heads = k_loc.shape[1] // HEAD_SIZE
    q_heads = q_loc.shape[1] // HEAD_SIZE
    heads_per_group = q_heads // kv_heads
    score_scale = 1.0 / math.sqrt(HEAD_SIZE)
    blk_index = lax.axis_index("blk")
    query_pos = lax.dynamic_slice_in_dim(positions, blk_index * row_count, row_count)
    prefix = prefix_len[0]
    query_heads = q_loc.reshape(row_count, kv_heads, heads_per_group, HEAD_SIZE)
    wo_full, wg_full, wu_full, wd_full = (
        lax.all_gather(out_weight, "blk", axis=1, tiled=True),
        lax.all_gather(gate_weight, "blk", axis=0, tiled=True),
        lax.all_gather(up_weight, "blk", axis=0, tiled=True),
        lax.all_gather(down_weight, "blk", axis=1, tiled=True),
    )
    key_part = lax.all_gather(k_loc, "blk", axis=0, tiled=True)
    value_part = lax.all_gather(v_loc, "blk", axis=0, tiled=True)
    key_count = key_part.shape[0]
    scores = (
        jnp.einsum(
            "bkgd,skd->bkgs",
            query_heads,
            key_part.reshape(key_count, kv_heads, HEAD_SIZE),
            preferred_element_type=F32,
        )
        * score_scale
    )
    visible = (positions[None, :] <= query_pos[:, None]) | (positions[None, :] < prefix)
    scores = jnp.where(visible[:, None, None, :], scores, -jnp.inf)
    row_max = jnp.max(scores, axis=-1)
    exp_scores = jnp.exp(scores - row_max[..., None])
    denom = jnp.sum(exp_scores, axis=-1)
    probs = exp_scores.astype(BF16)
    weighted = jnp.einsum(
        "bkgs,skd->bkgd",
        probs,
        value_part.reshape(key_count, kv_heads, HEAD_SIZE),
        preferred_element_type=F32,
    )
    attended = (weighted / denom[..., None]).reshape(row_count, q_heads * HEAD_SIZE)
    gated_out = (attended * jax.nn.sigmoid(g_loc.astype(F32))).astype(BF16)
    head_partial = jnp.dot(gated_out, wo_full, preferred_element_type=F32)
    projected = lax.psum_scatter(
        head_partial.astype(BF16), "uly", scatter_dimension=0, tiled=True
    ).astype(F32)
    hidden_f = (residual.astype(F32) + projected).astype(BF16).astype(F32)
    mean_sq = jnp.mean(hidden_f * hidden_f, axis=-1, keepdims=True)
    normed = (hidden_f * lax.rsqrt(mean_sq + 1e-06) * norm_gain).astype(BF16)
    group_rows = lax.all_gather(normed, "uly", axis=0, tiled=True)
    gate_sum = jnp.dot(group_rows, wg_full, preferred_element_type=F32)
    up_sum = jnp.dot(group_rows, wu_full, preferred_element_type=F32)
    activated = (jax.nn.silu(gate_sum) * up_sum).astype(BF16)
    ffn_partial = jnp.dot(activated, wd_full, preferred_element_type=F32)
    ffn_out = lax.psum_scatter(
        ffn_partial.astype(BF16), "uly", scatter_dimension=0, tiled=True
    ).astype(F32)
    return (hidden_f + ffn_out).astype(BF16)


def dot(a, b):
    return jnp.dot(a, b, preferred_element_type=F32)


def pack_heads_kernel(head_of, *refs):
    many = (len(refs) - 2) // 2
    parts, out, held, sems = refs[:many], refs[many], refs[many + 1:-1], refs[-1]
    copies = [
        pltpu.make_async_copy(part, spot, sems.at[i])
        for i, (part, spot) in enumerate(zip(parts, held))
    ]
    for copy in copies:
        copy.start()
    out[...] = jnp.zeros_like(out)
    tokens = parts[0].shape[0]
    start = 0
    for copy, spot in zip(copies, held):
        copy.wait()
        width = spot.shape[1] // len(head_of)
        for r, j in enumerate(head_of):
            out[r, :tokens, start:start + width] = spot[:, j * width:(j + 1) * width]
        start += width


def message_kernel(planes, idx, heads, residual, pick, *outs):
    group, rows, _ = heads.shape
    tokens, features = residual.shape
    pair = 2 * HEAD_SIZE
    width = features // planes
    z = idx[0]
    keys = dot(pick[...], heads[:, :, :pair].reshape(group * rows, pair)).astype(BF16)
    lot = keys.shape[0]
    for k, out in enumerate(outs):
        out[:lot] = keys
        out[lot:] = jnp.zeros((out.shape[0] - lot, pair), BF16)
        for c in range(width // pair):
            at = pl.ds(pl.multiple_of((z ^ k) * width + c * pair, pair), pair)
            out[lot + c * rows:lot + c * rows + tokens] = residual[:, at]


def attention_kernel(heads, planes, idx, prefix, qg, *refs):
    messages, (spots, pick, out) = refs[:planes], refs[planes:]
    group, rows, _ = qg.shape
    z, r = idx[0], idx[1]
    lot, held = group * rows, pick.shape[0]
    tokens = held // group
    keys, values, key_spot = [], [], []
    for k in range(planes):
        keys.append(messages[k][:held, :HEAD_SIZE])
        values.append(messages[k][:held, HEAD_SIZE:])
        key_spot.append(spots[z ^ k])
    keys, values = jnp.concatenate(keys), jnp.concatenate(values)
    key_spot = jnp.concatenate(key_spot, axis=1)
    i = lax.broadcasted_iota(jnp.int32, (lot, held), 0) ^ (r * rows)
    j = lax.broadcasted_iota(jnp.int32, (lot, held), 1)
    source = i // rows * tokens + jnp.minimum(i % rows, tokens - 1)
    query_spot = jnp.sum(jnp.where(source == j, spots[z], 0.0), axis=1, keepdims=True)
    visible = (key_spot <= query_spot) | (key_spot < prefix[0].astype(F32))
    bias = jnp.where(visible, 0.0, HIDE)
    scale = 1.0 / math.sqrt(HEAD_SIZE)
    done = []
    for h in range(heads):
        at = slice((h + 2) * HEAD_SIZE, (h + 3) * HEAD_SIZE)
        gate_at = slice((heads + h + 2) * HEAD_SIZE, (heads + h + 3) * HEAD_SIZE)
        q = jnp.concatenate([qg[b ^ r, :, at] for b in range(group)])
        gate = jnp.concatenate([qg[b ^ r, :, gate_at] for b in range(group)]).astype(F32)
        s = lax.dot_general(q, keys, NT, preferred_element_type=F32) * scale + bias
        e = jnp.exp(s - jnp.max(s, axis=-1, keepdims=True))
        denom = jnp.sum(e, axis=-1, keepdims=True)
        attended = dot(e.astype(BF16), values) / denom
        done.append((attended / (1.0 + jnp.exp(-gate))).astype(BF16))
    out[...] = dot(pick[...], jnp.concatenate(done, axis=1)).astype(BF16)


def project_kernel(planes, idx, *refs):
    parts = refs[:planes]
    weights, (pick, keep, send, held, wide) = refs[planes:-5], refs[-5:]
    z, q = idx[0], idx[2]
    for k in range(planes):
        held[z ^ k] = parts[k][...]
    rows, width = parts[0].shape
    x = dot(pick[...], held[...].reshape(planes * rows, width)).astype(BF16)
    lanes = weights[0].shape[1]
    for c, weight in enumerate(weights):
        wide[:, pl.ds(pl.multiple_of((q ^ c) * lanes, lanes), lanes)] = weight[...]
    y = dot(x, wide[...]).astype(BF16)
    half = y.shape[0] // 2
    keep[...] = y[:half]
    send[...] = y[half:]


def core_sum_kernel(keep, got, *outs):
    rows = outs[0].shape[0]
    for i, out in enumerate(outs):
        at = slice(i * rows, (i + 1) * rows)
        out[...] = (keep[at].astype(F32) + got[at].astype(F32)).astype(out.dtype)


def hidden_kernel(planes, tokens, idx, *refs):
    parts, messages, out = refs[:-planes - 1], refs[-planes - 1:-1], refs[-1]
    total = parts[0][...]
    for part in parts[1:]:
        total = total + part[...].astype(F32)
    width = out.shape[1]
    pair = messages[0].shape[1]
    pieces = width // pair
    rows = -(-tokens // ROW_TILE) * ROW_TILE
    for k, message in enumerate(messages):
        i = lax.broadcasted_iota(jnp.int32, (out.shape[0], rows), 0)
        j = lax.broadcasted_iota(jnp.int32, (out.shape[0], rows), 1)
        place = jnp.where((i == j + (idx[0] ^ k) * tokens) & (j < tokens), 1.0, 0.0).astype(BF16)
        lot = message.shape[0] - pieces * rows
        held = [message[lot + c * rows:lot + (c + 1) * rows] for c in range(pieces)]
        total = total + dot(place, jnp.concatenate(held, axis=1))
    out[...] = total.astype(BF16)


def stack_kernel(*refs):
    *parts, out = refs
    for k, part in enumerate(parts):
        out[k] = part[...]


def split_gate_up_kernel(planes, sides, idx, gate, up, *outs):
    units = outs[0].shape[1] // (2 * planes)
    for c, out in enumerate(outs):
        for k in range(planes):
            chip = (idx[0] ^ k) * sides + (idx[3] ^ c)
            at = pl.ds(pl.multiple_of(chip * units, units), units)
            out[:, 2 * k * units:(2 * k + 1) * units] = gate[:, at]
            out[:, (2 * k + 1) * units:(2 * k + 2) * units] = up[:, at]


def split_rows_kernel(planes, per, idx, down, heads, message, own, own_heads, core_heads):
    sides = per // 2
    units, head_rows = own.shape[1], own_heads.shape[0]
    for k in range(planes):
        for c in range(sides):
            chip = (idx[0] ^ k) * sides + (idx[3] ^ c)
            start = pl.multiple_of(chip * units, units)
            rows = down[pl.ds(start, units), :]
            if c:
                message[k * units:(k + 1) * units] = rows
            else:
                own[k] = rows
    for c in range(per):
        rows = heads[pl.ds(pl.multiple_of((idx[2] ^ c) * head_rows, head_rows), head_rows), :]
        if c == 0:
            own_heads[...] = rows
        elif c == 1:
            core_heads[...] = rows
        else:
            start = planes * units + (c - 2) * head_rows
            message[start:start + head_rows] = rows


def regroup_kernel(own, message, *outs):
    *downs, near_heads, far_heads = outs
    units, head_rows = own.shape[1], near_heads.shape[0]
    for k, out in enumerate(downs):
        out[0] = own[k]
        out[1] = message[k * units:(k + 1) * units]
    start = len(downs) * units
    near_heads[...] = message[start:start + head_rows]
    far_heads[...] = message[start + head_rows:start + 2 * head_rows]


def gate_up_kernel(blocks, per, planes, idx, *refs):
    parts, pieces = refs[:blocks], refs[blocks:blocks + per]
    gain, same, *outs, held = refs[blocks + per:]
    x = jnp.concatenate([part[...] for part in parts]).astype(F32)
    rows, width = x.shape
    lanes = width // per
    square = jnp.sum(x * x, axis=1, keepdims=True)
    held[...] = (x * gain[idx[0]]).astype(BF16)
    x = [held[:, pl.ds(pl.multiple_of((idx[2] ^ c) * lanes, lanes), lanes)] for c in range(per)]
    x = jnp.concatenate(x, axis=1)
    columns = pieces[0].shape[1] // planes
    lane = lax.broadcasted_iota(jnp.int32, (rows, HEAD_SIZE), 1)
    high = square.astype(BF16).astype(F32)
    terms = jnp.where(lane == 0, high, jnp.where(lane == 1, square - high, 0.0)).astype(BF16)
    terms = lax.dot_general(terms, same[...], (((0,), (0,)), ((), ())), preferred_element_type=F32)
    keep, near, *fars = outs
    terms = terms[:ROW_TILE]
    split = rows // 2
    for k in range(planes):
        at = slice(k * columns, (k + 1) * columns)
        total = dot(x, jnp.concatenate([piece[:, at] for piece in pieces]))
        if k < 2:
            places = [(outs[k], 0, rows)]
        else:
            places = [(fars[2 * k - 4], split, rows), (fars[2 * k - 3], 0, split)]
        for out, start, end in places:
            many = end - start
            out[:many] = total[start:end].astype(out.dtype)
            if out.shape[0] > many:
                out[many:] = jnp.zeros((ROW_TILE, columns), out.dtype)
                out[many:, :rows] = terms.astype(out.dtype)


def far_sum_kernel(rows, kept, got, out):
    total = kept[...] + got[...].astype(F32)
    out[:rows] = total[:rows].astype(BF16)
    if out.shape[0] > rows:
        square = jnp.sum(total[rows:], axis=0, keepdims=True)
        high = square.astype(BF16).astype(F32)
        row = lax.broadcasted_iota(jnp.int32, (out.shape[0] - rows, total.shape[1]), 0)
        terms = jnp.where(row == 0, high, jnp.where(row == 1, square - high, 0.0))
        out[rows:] = terms.astype(BF16)


def down_kernel(start, planes, per, features, idx, keep, got, far_head, far_part, near, far, same, *outs):
    many = same.shape[0]
    half = many // 2
    at = slice(start, start + half)
    total = keep[at] + got[at].astype(F32) + far_part[:half].astype(F32)
    terms = [keep[many:, :many], got[many:, :many].astype(F32), far_head[half:, :many].astype(F32)]
    units = total.shape[1] // 2
    square = jnp.concatenate(terms).astype(BF16)
    square = lax.dot_general(same[at], square, NT, preferred_element_type=F32)
    square = jnp.sum(square, axis=1, keepdims=True)
    factor = lax.rsqrt(square / features + 1e-06)
    gate, up = total[:, :units] * factor, total[:, units:] * factor
    activated = (gate / (1.0 + jnp.exp(-gate)) * up).astype(BF16)
    z, q = idx[0], idx[2]
    rows = outs[0].shape[1]
    for k in range(planes):
        w = [(far if c % 2 else near)[k, c // 2] for c in range(per)]
        y = dot(activated, jnp.concatenate(w, axis=1))
        lanes = w[0].shape[1]
        for c in range(per):
            at = pl.ds(pl.multiple_of((q ^ c) * lanes, lanes), lanes)
            block = y[:, c * lanes:(c + 1) * lanes]
            for i, out in enumerate(outs):
                out[z ^ k, :, at] = block[i * rows:(i + 1) * rows].astype(out.dtype)


def plane_sum_kernel(planes, tokens, idx, hidden, *refs):
    parts, outs = refs[:-planes], refs[-planes:]
    total = parts[0][...]
    for part in parts[1:]:
        total = total + part[...].astype(F32)
    total = total.astype(BF16)
    share = hidden.shape[0]
    source = jnp.concatenate([total[p] for p in range(planes)] + [hidden[...]])
    for k, out in enumerate(outs):
        i = lax.broadcasted_iota(jnp.int32, (out.shape[0], source.shape[0]), 0)
        j = lax.broadcasted_iota(jnp.int32, (out.shape[0], source.shape[0]), 1)
        spot = i // tokens * share + (idx[0] ^ k) * tokens + i % tokens
        pick = jnp.where((spot == j) & (i < (planes + 1) * tokens), 1.0, 0.0).astype(BF16)
        out[...] = dot(pick, source).astype(BF16)


def last_kernel(planes, tokens, idx, *refs):
    *parts, out, held = refs
    width = parts[0].shape[1]
    total = parts[0][...].astype(F32)
    for part in parts[1:]:
        total = total + part[...].astype(F32)
    end = planes * tokens
    for k, part in enumerate(parts):
        held[idx[0] ^ k, :tokens] = part[...].astype(F32)[end:end + tokens]
    for p in range(planes):
        value = held[p, :tokens] + total[p * tokens:(p + 1) * tokens]
        out[:, p * width:(p + 1) * width] = value.astype(BF16)


def call(kernel, outs, *args, scratch=(), place=VMEM, limit=16):
    single = not isinstance(outs, list)
    shapes = [outs] if single else outs
    got = pl.pallas_call(
        kernel,
        out_shape=shapes,
        in_specs=[SMEM if a.dtype == jnp.int32 else place for a in args],
        out_specs=[VMEM] * len(shapes),
        scratch_shapes=list(scratch),
        compiler_params=pltpu.CompilerParams(vmem_limit_bytes=limit * 2**20),
    )(*args)
    return got[0] if single else list(got)


def like(*shape, dtype=BF16):
    return jax.ShapeDtypeStruct(shape, dtype)


def move_tokens(
    n_blk,
    n_uly,
    residual,
    query_projection,
    key_projection,
    value_projection,
    gate_proj,
    positions,
    prefix_len,
    out_weight,
    norm_gain,
    gate_weight,
    up_weight,
    down_weight,
):
    axes = ("blk", "uly")
    kv_heads = key_projection.shape[1] // HEAD_SIZE
    heads = query_projection.shape[1] // key_projection.shape[1]
    tokens, features = residual.shape
    rows = -(-tokens // ROW_TILE) * ROW_TILE
    group = kv_heads
    per = group // n_uly
    planes = n_blk // per
    devices = n_blk * n_uly
    me = lax.axis_index("blk") * n_uly + lax.axis_index("uly")
    z, r = me // group, me % group
    idx = jnp.stack([z, r, r // n_uly, r // (2 * n_uly)]).astype(jnp.int32)
    core = n_uly
    near = [b for b in range(group) if not b & core]
    order = near + [b ^ core for b in near]
    steps = near[1:]

    def swap(x, mask):
        return lax.ppermute(x, axes, [(i, i ^ mask) for i in range(devices)])

    def swap_planes(x):
        return [swap(x, k * group) for k in range(1, planes)]

    head_of = [(i % n_uly) * per + i // n_uly for i in range(group)]
    plane_groups = [[p * group + i for i in range(group)] for p in range(planes)]

    def plane_exchange(x):
        return lax.all_to_all(x, axes, 0, 0, axis_index_groups=plane_groups, tiled=True)

    def after(*xs):
        return lax.optimization_barrier(xs)

    width = features // planes
    sides = per // 2
    units = gate_weight.shape[1] // (planes * sides)

    def across_planes(parts):
        return [x if not k else swap(x, k * group) for k, x in enumerate(parts)]

    pair = 2 * HEAD_SIZE
    tokens_in = (key_projection, value_projection, query_projection, gate_proj)
    head_groups = call(
        functools.partial(pack_heads_kernel, head_of),
        like(group, rows, 2 * heads * HEAD_SIZE + pair),
        *tokens_in,
        scratch=[pltpu.VMEM(x.shape, x.dtype) for x in tokens_in]
        + [pltpu.SemaphoreType.DMA((len(tokens_in),))],
        place=pl.BlockSpec(memory_space=pl.ANY),
        limit=60,
    )
    head_groups, gate_weight, up_weight, down_weight, out_weight, positions = after(
        head_groups, gate_weight, up_weight, down_weight, out_weight, positions
    )
    side = 2 * n_uly
    gate_up = call(
        functools.partial(split_gate_up_kernel, planes, sides),
        [like(gate_weight.shape[0], 2 * planes * units)] * sides,
        idx, gate_weight, up_weight,
    )
    head_rows = out_weight.shape[0] // per
    lanes = out_weight.shape[1]
    message, own_down, wo_own, wo_core = call(
        functools.partial(split_rows_kernel, planes, per),
        [
            like(planes * units + 2 * head_rows, lanes),
            like(planes, units, lanes),
            like(head_rows, lanes),
            like(head_rows, lanes),
        ],
        idx, down_weight, out_weight,
    )
    spots = positions.astype(F32).reshape(planes, 1, group * tokens)
    own_heads = plane_exchange(head_groups)
    wo_core = swap(wo_core, core)
    own_heads, message, gate_up, wo_core, spots = after(
        own_heads, message, gate_up, wo_core, spots
    )
    pick = np.zeros((group, tokens, group, rows), np.float32)
    for b in range(group):
        for t in range(tokens):
            pick[b, t, b, t] = 1
    pick = jnp.asarray(pick.reshape(group * tokens, group * rows), BF16)
    messages = across_planes(
        call(
            functools.partial(message_kernel, planes),
            [like(group * tokens + rows * width // pair, pair)] * planes,
            idx, own_heads, residual, pick,
        )
    )
    message = swap(message, side)
    twin = [swap(gate_up[0], core), None]
    *messages, gate_up[1], twin[0] = after(*messages, gate_up[1], twin[0])
    gate_up[1] = swap(gate_up[1], side)
    gated = call(
        functools.partial(attention_kernel, heads, planes),
        like(group * tokens, heads * HEAD_SIZE),
        idx, prefix_len, own_heads, *messages, spots, pick,
    )
    gated, message = after(gated, message)
    *down_parts, wo_near, wo_far = call(
        regroup_kernel,
        [like(sides, units, lanes)] * planes + [like(head_rows, lanes)] * 2,
        own_down, message,
    )
    gateds = [gated] + swap_planes(gated)
    wo = [wo_own, wo_core, wo_near, swap(wo_far, core)]
    gateds, wo, down_parts = after(gateds, wo, down_parts)
    for k in (1, 2):
        down_parts[k] = swap(down_parts[k], k * group)

    turn = np.zeros((group, planes, tokens, planes, group, tokens), np.float32)
    for i, b in enumerate(order):
        for p in range(planes):
            for t in range(tokens):
                turn[i, p, t, p, b, t] = 1
    total = devices * tokens
    turn = jnp.asarray(turn.reshape(total, total), BF16)
    keep, send = call(
        functools.partial(project_kernel, planes),
        [like(total // 2, width)] * 2,
        idx, *gateds, *wo, turn,
        scratch=[
            pltpu.VMEM((planes,) + gated.shape, BF16),
            pltpu.VMEM((wo[0].shape[0], width), BF16),
        ],
    )
    share = total // group
    own, *rest = call(
        core_sum_kernel,
        [like(share, width, dtype=F32)] + [like(share, width)] * len(steps),
        keep, swap(send, core),
    )
    rest, gate_up[1] = after(rest, gate_up[1])
    hidden = call(
        functools.partial(hidden_kernel, planes, tokens),
        like(share, width),
        idx, own, *[swap(x, b) for x, b in zip(rest, steps)], *messages,
    )
    hidden, gate_up[1], down_parts = after(hidden, gate_up[1], down_parts)
    down_parts[3] = swap(down_parts[3], 3 * group)
    twin[1] = swap(gate_up[1], core)
    blocks = [hidden] + [swap(hidden, b) for b in steps]
    same = jnp.eye(len(blocks) * share, dtype=BF16)
    pieces = [x for both in zip(gate_up, twin) for x in both]
    many = len(blocks) * share
    group_far = planes // 2 * group
    split = many // 2
    ends = (split + ROW_TILE, split)
    keep, near_send, *fars = call(
        functools.partial(gate_up_kernel, len(blocks), per, planes),
        [like(many + ROW_TILE, 2 * units, dtype=F32), like(many + ROW_TILE, 2 * units)]
        + [like(rows_, 2 * units, dtype=F32) for rows_ in ends]
        + [like(rows_, 2 * units) for rows_ in ends],
        idx, *blocks, *pieces, norm_gain.reshape(planes, 1, width), same,
        scratch=[pltpu.VMEM((many, width), BF16)],
    )
    far_keeps, far_sends = fars[:2], fars[2:]
    far_sends[0], down_parts = after(far_sends[0], down_parts)

    def far_sum(i, got):
        return call(
            functools.partial(far_sum_kernel, split), like(ends[i], 2 * units), far_keeps[i], got
        )

    got = swap(far_sends[0], group)
    far_head = swap(far_sum(0, got), group_far)
    got, near_send = after(swap(far_sends[1], group), near_send)
    far_rest = swap(far_sum(1, got), group_far)
    near_got = swap(near_send, group)
    downs = call(stack_kernel, like(planes, *down_parts[0].shape), *down_parts)
    weights = [downs, swap(downs, core), same]

    def ffn_out(start, part, dtypes):
        return call(
            functools.partial(down_kernel, start, planes, per, features),
            [like(planes, share, width, dtype=dtype) for dtype in dtypes],
            idx, keep, near_got, far_head, part, *weights,
        )

    late = ffn_out(split, far_head, [BF16, BF16])
    own, early = ffn_out(0, far_rest, [F32, BF16])
    rest = [early] + late
    parts = call(
        functools.partial(plane_sum_kernel, planes, tokens),
        [like(-(-(planes + 1) * tokens // ROW_TILE) * ROW_TILE, width)] * planes,
        idx, hidden, own, *[swap(x, b) for x, b in zip(rest, steps)],
    )
    return call(
        functools.partial(last_kernel, planes, tokens),
        like(tokens, features),
        idx, *across_planes(parts),
        scratch=[pltpu.VMEM((planes, rows, width), F32)],
    )


def tokens_can_travel(n_blk, n_uly, kv_heads, token_count, unit_count):
    def power(n):
        return n > 0 and not n & (n - 1)

    per = kv_heads // n_uly
    return (
        power(n_blk)
        and power(n_uly)
        and power(kv_heads)
        and per > 1
        and n_blk == 4 * per
        and token_count < unit_count // n_uly
    )


def solution(mesh):
    n_blk, n_uly = mesh.shape["blk"], mesh.shape["uly"]

    def per_device(*args):
        residual, key_projection, gate_weight = args[0], args[2], args[9]
        travel = tokens_can_travel(
            n_blk,
            n_uly,
            key_projection.shape[1] // HEAD_SIZE,
            residual.shape[0] * n_blk * n_uly,
            gate_weight.shape[1] * n_uly,
        )
        if travel:
            return move_tokens(n_blk, n_uly, *args)
        return move_weights(*args)

    return jax.shard_map(
        per_device,
        mesh=mesh,
        in_specs=(
            P(("blk", "uly"), None),
            P(("blk", "uly"), None),
            P(("blk", "uly"), None),
            P(("blk", "uly"), None),
            P(("blk", "uly"), None),
            P(),
            P(),
            P("uly", "blk"),
            P(),
            P("blk", "uly"),
            P("blk", "uly"),
            P("uly", "blk"),
        ),
        out_specs=P(("blk", "uly"), None),
        check_vma=False,
    )
```

```python
import functools
import math

import jax
import jax.numpy as jnp
import numpy as np
from jax import lax
from jax.experimental import pallas as pl
from jax.experimental.pallas import tpu as pltpu
from jax.sharding import PartitionSpec as P

HEAD_SIZE = 128
ROW_TILE = 16
HIDE = -1e30
F32 = jnp.float32
BF16 = jnp.bfloat16
VMEM = pl.BlockSpec(memory_space=pltpu.VMEM)
SMEM = pl.BlockSpec(memory_space=pltpu.SMEM)
NT = (((1,), (1,)), ((), ()))


def move_weights(
    residual,
    query_projection,
    key_projection,
    value_projection,
    gate_proj,
    positions,
    prefix_len,
    out_weight,
    norm_gain,
    gate_weight,
    up_weight,
    down_weight,
):
    q_loc, k_loc, v_loc, g_loc = (
        lax.all_to_all(query_projection, "uly", split_axis=1, concat_axis=0, tiled=True),
        lax.all_to_all(key_projection, "uly", split_axis=1, concat_axis=0, tiled=True),
        lax.all_to_all(value_projection, "uly", split_axis=1, concat_axis=0, tiled=True),
        lax.all_to_all(gate_proj, "uly", split_axis=1, concat_axis=0, tiled=True),
    )
    row_count = q_loc.shape[0]
    kv_heads = k_loc.shape[1] // HEAD_SIZE
    q_heads = q_loc.shape[1] // HEAD_SIZE
    heads_per_group = q_heads // kv_heads
    score_scale = 1.0 / math.sqrt(HEAD_SIZE)
    blk_index = lax.axis_index("blk")
    query_pos = lax.dynamic_slice_in_dim(positions, blk_index * row_count, row_count)
    prefix = prefix_len[0]
    query_heads = q_loc.reshape(row_count, kv_heads, heads_per_group, HEAD_SIZE)
    wo_full, wg_full, wu_full, wd_full = (
        lax.all_gather(out_weight, "blk", axis=1, tiled=True),
        lax.all_gather(gate_weight, "blk", axis=0, tiled=True),
        lax.all_gather(up_weight, "blk", axis=0, tiled=True),
        lax.all_gather(down_weight, "blk", axis=1, tiled=True),
    )
    key_part = lax.all_gather(k_loc, "blk", axis=0, tiled=True)
    value_part = lax.all_gather(v_loc, "blk", axis=0, tiled=True)
    key_count = key_part.shape[0]
    scores = (
        jnp.einsum(
            "bkgd,skd->bkgs",
            query_heads,
            key_part.reshape(key_count, kv_heads, HEAD_SIZE),
            preferred_element_type=F32,
        )
        * score_scale
    )
    visible = (positions[None, :] <= query_pos[:, None]) | (positions[None, :] < prefix)
    scores = jnp.where(visible[:, None, None, :], scores, -jnp.inf)
    row_max = jnp.max(scores, axis=-1)
    exp_scores = jnp.exp(scores - row_max[..., None])
    denom = jnp.sum(exp_scores, axis=-1)
    probs = exp_scores.astype(BF16)
    weighted = jnp.einsum(
        "bkgs,skd->bkgd",
        probs,
        value_part.reshape(key_count, kv_heads, HEAD_SIZE),
        preferred_element_type=F32,
    )
    attended = (weighted / denom[..., None]).reshape(row_count, q_heads * HEAD_SIZE)
    gated_out = (attended * jax.nn.sigmoid(g_loc.astype(F32))).astype(BF16)
    head_partial = jnp.dot(gated_out, wo_full, preferred_element_type=F32)
    projected = lax.psum_scatter(
        head_partial.astype(BF16), "uly", scatter_dimension=0, tiled=True
    ).astype(F32)
    hidden_f = (residual.astype(F32) + projected).astype(BF16).astype(F32)
    mean_sq = jnp.mean(hidden_f * hidden_f, axis=-1, keepdims=True)
    normed = (hidden_f * lax.rsqrt(mean_sq + 1e-06) * norm_gain).astype(BF16)
    group_rows = lax.all_gather(normed, "uly", axis=0, tiled=True)
    gate_sum = jnp.dot(group_rows, wg_full, preferred_element_type=F32)
    up_sum = jnp.dot(group_rows, wu_full, preferred_element_type=F32)
    activated = (jax.nn.silu(gate_sum) * up_sum).astype(BF16)
    ffn_partial = jnp.dot(activated, wd_full, preferred_element_type=F32)
    ffn_out = lax.psum_scatter(
        ffn_partial.astype(BF16), "uly", scatter_dimension=0, tiled=True
    ).astype(F32)
    return (hidden_f + ffn_out).astype(BF16)


def dot(a, b):
    return jnp.dot(a, b, preferred_element_type=F32)


def pack_heads_kernel(head_of, *refs):
    *parts, out = refs
    out[...] = jnp.zeros_like(out)
    tokens = parts[0].shape[0]
    start = 0
    for part in parts:
        width = part.shape[1] // len(head_of)
        for r, j in enumerate(head_of):
            out[r, :tokens, start:start + width] = part[:, j * width:(j + 1) * width]
        start += width


def message_kernel(planes, idx, heads, residual, pick, *outs):
    group, rows, _ = heads.shape
    tokens, features = residual.shape
    pair = 2 * HEAD_SIZE
    width = features // planes
    z = idx[0]
    keys = dot(pick[...], heads[:, :, :pair].reshape(group * rows, pair)).astype(BF16)
    lot = keys.shape[0]
    for k, out in enumerate(outs):
        out[:lot] = keys
        out[lot:] = jnp.zeros((out.shape[0] - lot, pair), BF16)
        for c in range(width // pair):
            at = pl.ds(pl.multiple_of((z ^ k) * width + c * pair, pair), pair)
            out[lot + c * rows:lot + c * rows + tokens] = residual[:, at]


def attention_kernel(heads, planes, idx, prefix, qg, *refs):
    messages, (spots, pick, out) = refs[:planes], refs[planes:]
    group, rows, _ = qg.shape
    z, r = idx[0], idx[1]
    lot, held = group * rows, pick.shape[0]
    tokens = held // group
    keys, values, key_spot = [], [], []
    for k in range(planes):
        keys.append(messages[k][:held, :HEAD_SIZE])
        values.append(messages[k][:held, HEAD_SIZE:])
        key_spot.append(spots[z ^ k])
    keys, values = jnp.concatenate(keys), jnp.concatenate(values)
    key_spot = jnp.concatenate(key_spot, axis=1)
    i = lax.broadcasted_iota(jnp.int32, (lot, held), 0) ^ (r * rows)
    j = lax.broadcasted_iota(jnp.int32, (lot, held), 1)
    source = i // rows * tokens + jnp.minimum(i % rows, tokens - 1)
    query_spot = jnp.sum(jnp.where(source == j, spots[z], 0.0), axis=1, keepdims=True)
    visible = (key_spot <= query_spot) | (key_spot < prefix[0].astype(F32))
    bias = jnp.where(visible, 0.0, HIDE)
    scale = 1.0 / math.sqrt(HEAD_SIZE)
    wide = jnp.concatenate([qg[b ^ r, :, 2 * HEAD_SIZE:] for b in range(group)])

    def by_head(start):
        return jnp.concatenate(
            [wide[:, (start + h) * HEAD_SIZE:(start + h + 1) * HEAD_SIZE] for h in range(heads)]
        )

    gate = by_head(heads).astype(F32)
    s = lax.dot_general(by_head(0), keys, NT, preferred_element_type=F32) * scale
    s = s + jnp.concatenate([bias] * heads)
    e = jnp.exp(s - jnp.max(s, axis=-1, keepdims=True))
    denom = jnp.sum(e, axis=-1, keepdims=True)
    attended = dot(e.astype(BF16), values) / denom
    gated = (attended / (1.0 + jnp.exp(-gate))).astype(BF16)
    done = [gated[h * lot:(h + 1) * lot] for h in range(heads)]
    out[...] = dot(pick[...], jnp.concatenate(done, axis=1)).astype(BF16)


def project_kernel(planes, idx, *refs):
    parts = refs[:planes]
    weights, (pick, keep, send, held, wide) = refs[planes:-5], refs[-5:]
    z, q = idx[0], idx[2]
    for k in range(planes):
        held[z ^ k] = parts[k][...]
    rows, width = parts[0].shape
    x = dot(pick[...], held[...].reshape(planes * rows, width)).astype(BF16)
    lanes = weights[0].shape[1]
    for c, weight in enumerate(weights):
        wide[:, pl.ds(pl.multiple_of((q ^ c) * lanes, lanes), lanes)] = weight[...]
    y = dot(x, wide[...]).astype(BF16)
    half = y.shape[0] // 2
    keep[...] = y[:half]
    send[...] = y[half:]


def core_sum_kernel(keep, got, *outs):
    rows = outs[0].shape[0]
    for i, out in enumerate(outs):
        at = slice(i * rows, (i + 1) * rows)
        out[...] = (keep[at].astype(F32) + got[at].astype(F32)).astype(out.dtype)


def hidden_kernel(planes, tokens, idx, *refs):
    parts, messages, out = refs[:-planes - 1], refs[-planes - 1:-1], refs[-1]
    total = parts[0][...]
    for part in parts[1:]:
        total = total + part[...].astype(F32)
    width = out.shape[1]
    pair = messages[0].shape[1]
    pieces = width // pair
    rows = -(-tokens // ROW_TILE) * ROW_TILE
    for k, message in enumerate(messages):
        i = lax.broadcasted_iota(jnp.int32, (out.shape[0], rows), 0)
        j = lax.broadcasted_iota(jnp.int32, (out.shape[0], rows), 1)
        place = jnp.where((i == j + (idx[0] ^ k) * tokens) & (j < tokens), 1.0, 0.0).astype(BF16)
        lot = message.shape[0] - pieces * rows
        held = [message[lot + c * rows:lot + (c + 1) * rows] for c in range(pieces)]
        total = total + dot(place, jnp.concatenate(held, axis=1))
    out[...] = total.astype(BF16)


def stack_kernel(*refs):
    *parts, out = refs
    for k, part in enumerate(parts):
        out[k] = part[...]


def split_gate_up_kernel(planes, sides, idx, gate, up, *outs):
    units = outs[0].shape[1] // (2 * planes)
    for c, out in enumerate(outs):
        for k in range(planes):
            chip = (idx[0] ^ k) * sides + (idx[3] ^ c)
            at = pl.ds(pl.multiple_of(chip * units, units), units)
            out[:, 2 * k * units:(2 * k + 1) * units] = gate[:, at]
            out[:, (2 * k + 1) * units:(2 * k + 2) * units] = up[:, at]


def split_rows_kernel(planes, per, idx, down, heads, message, own, own_heads, core_heads):
    sides = per // 2
    units, head_rows = own.shape[1], own_heads.shape[0]
    for k in range(planes):
        for c in range(sides):
            chip = (idx[0] ^ k) * sides + (idx[3] ^ c)
            start = pl.multiple_of(chip * units, units)
            rows = down[pl.ds(start, units), :]
            if c:
                message[k * units:(k + 1) * units] = rows
            else:
                own[k] = rows
    for c in range(per):
        rows = heads[pl.ds(pl.multiple_of((idx[2] ^ c) * head_rows, head_rows), head_rows), :]
        if c == 0:
            own_heads[...] = rows
        elif c == 1:
            core_heads[...] = rows
        else:
            start = planes * units + (c - 2) * head_rows
            message[start:start + head_rows] = rows


def regroup_kernel(own, message, *outs):
    *downs, near_heads, far_heads = outs
    units, head_rows = own.shape[1], near_heads.shape[0]
    for k, out in enumerate(downs):
        out[0] = own[k]
        out[1] = message[k * units:(k + 1) * units]
    start = len(downs) * units
    near_heads[...] = message[start:start + head_rows]
    far_heads[...] = message[start + head_rows:start + 2 * head_rows]


def gate_up_kernel(blocks, per, planes, idx, *refs):
    parts, pieces = refs[:blocks], refs[blocks:blocks + per]
    gain, same, *outs, held = refs[blocks + per:]
    x = jnp.concatenate([part[...] for part in parts]).astype(F32)
    rows, width = x.shape
    lanes = width // per
    square = jnp.sum(x * x, axis=1, keepdims=True)
    held[...] = (x * gain[idx[0]]).astype(BF16)
    x = [held[:, pl.ds(pl.multiple_of((idx[2] ^ c) * lanes, lanes), lanes)] for c in range(per)]
    x = jnp.concatenate(x, axis=1)
    columns = pieces[0].shape[1] // planes
    lane = lax.broadcasted_iota(jnp.int32, (rows, HEAD_SIZE), 1)
    high = square.astype(BF16).astype(F32)
    terms = jnp.where(lane == 0, high, jnp.where(lane == 1, square - high, 0.0)).astype(BF16)
    terms = lax.dot_general(terms, same[...], (((0,), (0,)), ((), ())), preferred_element_type=F32)
    keep, near, *fars = outs
    terms = terms[:ROW_TILE]
    split = rows // 2
    for k in range(planes):
        at = slice(k * columns, (k + 1) * columns)
        total = dot(x, jnp.concatenate([piece[:, at] for piece in pieces]))
        if k < 2:
            places = [(outs[k], 0, rows)]
        else:
            places = [(fars[2 * k - 4], split, rows), (fars[2 * k - 3], 0, split)]
        for out, start, end in places:
            many = end - start
            out[:many] = total[start:end].astype(out.dtype)
            if out.shape[0] > many:
                out[many:] = jnp.zeros((ROW_TILE, columns), out.dtype)
                out[many:, :rows] = terms.astype(out.dtype)


def far_sum_kernel(rows, kept, got, out):
    total = kept[...] + got[...].astype(F32)
    out[:rows] = total[:rows].astype(BF16)
    if out.shape[0] > rows:
        square = jnp.sum(total[rows:], axis=0, keepdims=True)
        high = square.astype(BF16).astype(F32)
        row = lax.broadcasted_iota(jnp.int32, (out.shape[0] - rows, total.shape[1]), 0)
        terms = jnp.where(row == 0, high, jnp.where(row == 1, square - high, 0.0))
        out[rows:] = terms.astype(BF16)


def down_kernel(start, planes, per, features, idx, keep, got, far_head, far_part, near, far, same, *outs):
    many = same.shape[0]
    half = many // 2
    at = slice(start, start + half)
    total = keep[at] + got[at].astype(F32) + far_part[:half].astype(F32)
    terms = [keep[many:, :many], got[many:, :many].astype(F32), far_head[half:, :many].astype(F32)]
    units = total.shape[1] // 2
    square = jnp.concatenate(terms).astype(BF16)
    square = lax.dot_general(same[at], square, NT, preferred_element_type=F32)
    square = jnp.sum(square, axis=1, keepdims=True)
    factor = lax.rsqrt(square / features + 1e-06)
    gate, up = total[:, :units] * factor, total[:, units:] * factor
    activated = (gate / (1.0 + jnp.exp(-gate)) * up).astype(BF16)
    z, q = idx[0], idx[2]
    rows = outs[0].shape[1]
    for k in range(planes):
        w = [(far if c % 2 else near)[k, c // 2] for c in range(per)]
        y = dot(activated, jnp.concatenate(w, axis=1))
        lanes = w[0].shape[1]
        for c in range(per):
            at = pl.ds(pl.multiple_of((q ^ c) * lanes, lanes), lanes)
            block = y[:, c * lanes:(c + 1) * lanes]
            for i, out in enumerate(outs):
                out[z ^ k, :, at] = block[i * rows:(i + 1) * rows].astype(out.dtype)


def plane_sum_kernel(planes, tokens, idx, hidden, *refs):
    parts, outs = refs[:-planes], refs[-planes:]
    total = parts[0][...]
    for part in parts[1:]:
        total = total + part[...].astype(F32)
    total = total.astype(BF16)
    share = hidden.shape[0]
    source = jnp.concatenate([total[p] for p in range(planes)] + [hidden[...]])
    for k, out in enumerate(outs):
        i = lax.broadcasted_iota(jnp.int32, (out.shape[0], source.shape[0]), 0)
        j = lax.broadcasted_iota(jnp.int32, (out.shape[0], source.shape[0]), 1)
        spot = i // tokens * share + (idx[0] ^ k) * tokens + i % tokens
        pick = jnp.where((spot == j) & (i < (planes + 1) * tokens), 1.0, 0.0).astype(BF16)
        out[...] = dot(pick, source).astype(BF16)


def last_kernel(planes, tokens, idx, *refs):
    *parts, out, held = refs
    width = parts[0].shape[1]
    total = parts[0][...].astype(F32)
    for part in parts[1:]:
        total = total + part[...].astype(F32)
    end = planes * tokens
    for k, part in enumerate(parts):
        held[idx[0] ^ k, :tokens] = part[...].astype(F32)[end:end + tokens]
    for p in range(planes):
        value = held[p, :tokens] + total[p * tokens:(p + 1) * tokens]
        out[:, p * width:(p + 1) * width] = value.astype(BF16)


def call(kernel, outs, *args, scratch=(), limit=16):
    single = not isinstance(outs, list)
    shapes = [outs] if single else outs
    got = pl.pallas_call(
        kernel,
        out_shape=shapes,
        in_specs=[SMEM if a.dtype == jnp.int32 else VMEM for a in args],
        out_specs=[VMEM] * len(shapes),
        scratch_shapes=list(scratch),
        compiler_params=pltpu.CompilerParams(vmem_limit_bytes=limit * 2**20),
    )(*args)
    return got[0] if single else list(got)


def like(*shape, dtype=BF16):
    return jax.ShapeDtypeStruct(shape, dtype)


def move_tokens(
    n_blk,
    n_uly,
    residual,
    query_projection,
    key_projection,
    value_projection,
    gate_proj,
    positions,
    prefix_len,
    out_weight,
    norm_gain,
    gate_weight,
    up_weight,
    down_weight,
):
    axes = ("blk", "uly")
    kv_heads = key_projection.shape[1] // HEAD_SIZE
    heads = query_projection.shape[1] // key_projection.shape[1]
    tokens, features = residual.shape
    rows = -(-tokens // ROW_TILE) * ROW_TILE
    group = kv_heads
    per = group // n_uly
    planes = n_blk // per
    devices = n_blk * n_uly
    me = lax.axis_index("blk") * n_uly + lax.axis_index("uly")
    z, r = me // group, me % group
    idx = jnp.stack([z, r, r // n_uly, r // (2 * n_uly)]).astype(jnp.int32)
    core = n_uly
    near = [b for b in range(group) if not b & core]
    order = near + [b ^ core for b in near]
    steps = near[1:]

    def swap(x, mask):
        return lax.ppermute(x, axes, [(i, i ^ mask) for i in range(devices)])

    def swap_planes(x):
        return [swap(x, k * group) for k in range(1, planes)]

    head_of = [(i % n_uly) * per + i // n_uly for i in range(group)]
    plane_groups = [[p * group + i for i in range(group)] for p in range(planes)]

    def plane_exchange(x):
        return lax.all_to_all(x, axes, 0, 0, axis_index_groups=plane_groups, tiled=True)

    def after(*xs):
        return lax.optimization_barrier(xs)

    width = features // planes
    sides = per // 2
    units = gate_weight.shape[1] // (planes * sides)

    def across_planes(parts):
        return [x if not k else swap(x, k * group) for k, x in enumerate(parts)]

    pair = 2 * HEAD_SIZE
    tokens_in = (key_projection, value_projection, query_projection, gate_proj)
    head_groups = call(
        functools.partial(pack_heads_kernel, head_of),
        like(group, rows, 2 * heads * HEAD_SIZE + pair),
        *tokens_in,
        limit=60,
    )
    head_groups, gate_weight, up_weight, down_weight, out_weight, positions = after(
        head_groups, gate_weight, up_weight, down_weight, out_weight, positions
    )
    side = 2 * n_uly
    gate_up = call(
        functools.partial(split_gate_up_kernel, planes, sides),
        [like(gate_weight.shape[0], 2 * planes * units)] * sides,
        idx, gate_weight, up_weight,
    )
    head_rows = out_weight.shape[0] // per
    lanes = out_weight.shape[1]
    message, own_down, wo_own, wo_core = call(
        functools.partial(split_rows_kernel, planes, per),
        [
            like(planes * units + 2 * head_rows, lanes),
            like(planes, units, lanes),
            like(head_rows, lanes),
            like(head_rows, lanes),
        ],
        idx, down_weight, out_weight,
    )
    spots = positions.astype(F32).reshape(planes, 1, group * tokens)
    own_heads = plane_exchange(head_groups)
    wo_core = swap(wo_core, core)
    own_heads, message, gate_up, wo_core, spots = after(
        own_heads, message, gate_up, wo_core, spots
    )
    pick = np.zeros((group, tokens, group, rows), np.float32)
    for b in range(group):
        for t in range(tokens):
            pick[b, t, b, t] = 1
    pick = jnp.asarray(pick.reshape(group * tokens, group * rows), BF16)
    messages = across_planes(
        call(
            functools.partial(message_kernel, planes),
            [like(group * tokens + rows * width // pair, pair)] * planes,
            idx, own_heads, residual, pick,
        )
    )
    message = swap(message, side)
    twin = [swap(gate_up[0], core), None]
    *messages, gate_up[1], twin[0] = after(*messages, gate_up[1], twin[0])
    gate_up[1] = swap(gate_up[1], side)
    gated = call(
        functools.partial(attention_kernel, heads, planes),
        like(group * tokens, heads * HEAD_SIZE),
        idx, prefix_len, own_heads, *messages, spots, pick,
    )
    gated, message = after(gated, message)
    *down_parts, wo_near, wo_far = call(
        regroup_kernel,
        [like(sides, units, lanes)] * planes + [like(head_rows, lanes)] * 2,
        own_down, message,
    )
    gateds = [gated] + swap_planes(gated)
    wo = [wo_own, wo_core, wo_near, swap(wo_far, core)]
    gateds, wo, down_parts = after(gateds, wo, down_parts)
    for k in (1, 2):
        down_parts[k] = swap(down_parts[k], k * group)

    turn = np.zeros((group, planes, tokens, planes, group, tokens), np.float32)
    for i, b in enumerate(order):
        for p in range(planes):
            for t in range(tokens):
                turn[i, p, t, p, b, t] = 1
    total = devices * tokens
    turn = jnp.asarray(turn.reshape(total, total), BF16)
    keep, send = call(
        functools.partial(project_kernel, planes),
        [like(total // 2, width)] * 2,
        idx, *gateds, *wo, turn,
        scratch=[
            pltpu.VMEM((planes,) + gated.shape, BF16),
            pltpu.VMEM((wo[0].shape[0], width), BF16),
        ],
    )
    share = total // group
    own, *rest = call(
        core_sum_kernel,
        [like(share, width, dtype=F32)] + [like(share, width)] * len(steps),
        keep, swap(send, core),
    )
    rest, gate_up[1] = after(rest, gate_up[1])
    hidden = call(
        functools.partial(hidden_kernel, planes, tokens),
        like(share, width),
        idx, own, *[swap(x, b) for x, b in zip(rest, steps)], *messages,
    )
    hidden, gate_up[1], down_parts = after(hidden, gate_up[1], down_parts)
    down_parts[3] = swap(down_parts[3], 3 * group)
    twin[1] = swap(gate_up[1], core)
    blocks = [hidden] + [swap(hidden, b) for b in steps]
    same = jnp.eye(len(blocks) * share, dtype=BF16)
    pieces = [x for both in zip(gate_up, twin) for x in both]
    many = len(blocks) * share
    group_far = planes // 2 * group
    split = many // 2
    ends = (split + ROW_TILE, split)
    keep, near_send, *fars = call(
        functools.partial(gate_up_kernel, len(blocks), per, planes),
        [like(many + ROW_TILE, 2 * units, dtype=F32), like(many + ROW_TILE, 2 * units)]
        + [like(rows_, 2 * units, dtype=F32) for rows_ in ends]
        + [like(rows_, 2 * units) for rows_ in ends],
        idx, *blocks, *pieces, norm_gain.reshape(planes, 1, width), same,
        scratch=[pltpu.VMEM((many, width), BF16)],
    )
    far_keeps, far_sends = fars[:2], fars[2:]
    far_sends[0], down_parts = after(far_sends[0], down_parts)

    def far_sum(i, got):
        return call(
            functools.partial(far_sum_kernel, split), like(ends[i], 2 * units), far_keeps[i], got
        )

    got = swap(far_sends[0], group)
    far_head = swap(far_sum(0, got), group_far)
    got, near_send = after(swap(far_sends[1], group), near_send)
    far_rest = swap(far_sum(1, got), group_far)
    near_got = swap(near_send, group)
    downs = call(stack_kernel, like(planes, *down_parts[0].shape), *down_parts)
    weights = [downs, swap(downs, core), same]

    def ffn_out(start, part, dtypes):
        return call(
            functools.partial(down_kernel, start, planes, per, features),
            [like(planes, share, width, dtype=dtype) for dtype in dtypes],
            idx, keep, near_got, far_head, part, *weights,
        )

    late = ffn_out(split, far_head, [BF16, BF16])
    own, early = ffn_out(0, far_rest, [F32, BF16])
    rest = [early] + late
    parts = call(
        functools.partial(plane_sum_kernel, planes, tokens),
        [like(-(-(planes + 1) * tokens // ROW_TILE) * ROW_TILE, width)] * planes,
        idx, hidden, own, *[swap(x, b) for x, b in zip(rest, steps)],
    )
    return call(
        functools.partial(last_kernel, planes, tokens),
        like(tokens, features),
        idx, *across_planes(parts),
        scratch=[pltpu.VMEM((planes, rows, width), F32)],
    )


def tokens_can_travel(n_blk, n_uly, kv_heads, token_count, unit_count):
    def power(n):
        return n > 0 and not n & (n - 1)

    per = kv_heads // n_uly
    return (
        power(n_blk)
        and power(n_uly)
        and power(kv_heads)
        and per == 4
        and n_blk == 4 * per
        and token_count < unit_count // n_uly
    )


def solution(mesh):
    n_blk, n_uly = mesh.shape["blk"], mesh.shape["uly"]

    def per_device(*args):
        residual, key_projection, gate_weight = args[0], args[2], args[9]
        travel = tokens_can_travel(
            n_blk,
            n_uly,
            key_projection.shape[1] // HEAD_SIZE,
            residual.shape[0] * n_blk * n_uly,
            gate_weight.shape[1] * n_uly,
        )
        if travel:
            return move_tokens(n_blk, n_uly, *args)
        return move_weights(*args)

    return jax.shard_map(
        per_device,
        mesh=mesh,
        in_specs=(
            P(("blk", "uly"), None),
            P(("blk", "uly"), None),
            P(("blk", "uly"), None),
            P(("blk", "uly"), None),
            P(("blk", "uly"), None),
            P(),
            P(),
            P("uly", "blk"),
            P(),
            P("blk", "uly"),
            P("blk", "uly"),
            P("uly", "blk"),
        ),
        out_specs=P(("blk", "uly"), None),
        check_vma=False,
    )
```

```python
import functools
import math

import jax
import jax.numpy as jnp
import numpy as np
from jax import lax
from jax.experimental import pallas as pl
from jax.experimental.pallas import tpu as pltpu
from jax.sharding import PartitionSpec as P

HEAD_SIZE = 128
ROW_TILE = 16
HIDE = -1e30
F32 = jnp.float32
BF16 = jnp.bfloat16
VMEM = pl.BlockSpec(memory_space=pltpu.VMEM)
SMEM = pl.BlockSpec(memory_space=pltpu.SMEM)
NT = (((1,), (1,)), ((), ()))


def move_weights(
    residual,
    query_projection,
    key_projection,
    value_projection,
    gate_proj,
    positions,
    prefix_len,
    out_weight,
    norm_gain,
    gate_weight,
    up_weight,
    down_weight,
):
    q_loc, k_loc, v_loc, g_loc = (
        lax.all_to_all(query_projection, "uly", split_axis=1, concat_axis=0, tiled=True),
        lax.all_to_all(key_projection, "uly", split_axis=1, concat_axis=0, tiled=True),
        lax.all_to_all(value_projection, "uly", split_axis=1, concat_axis=0, tiled=True),
        lax.all_to_all(gate_proj, "uly", split_axis=1, concat_axis=0, tiled=True),
    )
    row_count = q_loc.shape[0]
    kv_heads = k_loc.shape[1] // HEAD_SIZE
    q_heads = q_loc.shape[1] // HEAD_SIZE
    heads_per_group = q_heads // kv_heads
    score_scale = 1.0 / math.sqrt(HEAD_SIZE)
    blk_index = lax.axis_index("blk")
    query_pos = lax.dynamic_slice_in_dim(positions, blk_index * row_count, row_count)
    prefix = prefix_len[0]
    query_heads = q_loc.reshape(row_count, kv_heads, heads_per_group, HEAD_SIZE)
    wo_full, wg_full, wu_full, wd_full = (
        lax.all_gather(out_weight, "blk", axis=1, tiled=True),
        lax.all_gather(gate_weight, "blk", axis=0, tiled=True),
        lax.all_gather(up_weight, "blk", axis=0, tiled=True),
        lax.all_gather(down_weight, "blk", axis=1, tiled=True),
    )
    key_part = lax.all_gather(k_loc, "blk", axis=0, tiled=True)
    value_part = lax.all_gather(v_loc, "blk", axis=0, tiled=True)
    key_count = key_part.shape[0]
    scores = (
        jnp.einsum(
            "bkgd,skd->bkgs",
            query_heads,
            key_part.reshape(key_count, kv_heads, HEAD_SIZE),
            preferred_element_type=F32,
        )
        * score_scale
    )
    visible = (positions[None, :] <= query_pos[:, None]) | (positions[None, :] < prefix)
    scores = jnp.where(visible[:, None, None, :], scores, -jnp.inf)
    row_max = jnp.max(scores, axis=-1)
    exp_scores = jnp.exp(scores - row_max[..., None])
    denom = jnp.sum(exp_scores, axis=-1)
    probs = exp_scores.astype(BF16)
    weighted = jnp.einsum(
        "bkgs,skd->bkgd",
        probs,
        value_part.reshape(key_count, kv_heads, HEAD_SIZE),
        preferred_element_type=F32,
    )
    attended = (weighted / denom[..., None]).reshape(row_count, q_heads * HEAD_SIZE)
    gated_out = (attended * jax.nn.sigmoid(g_loc.astype(F32))).astype(BF16)
    head_partial = jnp.dot(gated_out, wo_full, preferred_element_type=F32)
    projected = lax.psum_scatter(
        head_partial.astype(BF16), "uly", scatter_dimension=0, tiled=True
    ).astype(F32)
    hidden_f = (residual.astype(F32) + projected).astype(BF16).astype(F32)
    mean_sq = jnp.mean(hidden_f * hidden_f, axis=-1, keepdims=True)
    normed = (hidden_f * lax.rsqrt(mean_sq + 1e-06) * norm_gain).astype(BF16)
    group_rows = lax.all_gather(normed, "uly", axis=0, tiled=True)
    gate_sum = jnp.dot(group_rows, wg_full, preferred_element_type=F32)
    up_sum = jnp.dot(group_rows, wu_full, preferred_element_type=F32)
    activated = (jax.nn.silu(gate_sum) * up_sum).astype(BF16)
    ffn_partial = jnp.dot(activated, wd_full, preferred_element_type=F32)
    ffn_out = lax.psum_scatter(
        ffn_partial.astype(BF16), "uly", scatter_dimension=0, tiled=True
    ).astype(F32)
    return (hidden_f + ffn_out).astype(BF16)


def dot(a, b):
    return jnp.dot(a, b, preferred_element_type=F32)


def pack_heads_kernel(head_of, *refs):
    *parts, out = refs
    out[...] = jnp.zeros_like(out)
    tokens = parts[0].shape[0]
    start = 0
    for part in parts:
        width = part.shape[1] // len(head_of)
        for r, j in enumerate(head_of):
            out[r, :tokens, start:start + width] = part[:, j * width:(j + 1) * width]
        start += width


def message_kernel(planes, idx, heads, residual, pick, *outs):
    group, rows, _ = heads.shape
    tokens, features = residual.shape
    pair = 2 * HEAD_SIZE
    width = features // planes
    z = idx[0]
    keys = dot(pick[...], heads[:, :, :pair].reshape(group * rows, pair)).astype(BF16)
    lot = keys.shape[0]
    for k, out in enumerate(outs):
        out[:lot] = keys
        out[lot:] = jnp.zeros((out.shape[0] - lot, pair), BF16)
        for c in range(width // pair):
            at = pl.ds(pl.multiple_of((z ^ k) * width + c * pair, pair), pair)
            out[lot + c * rows:lot + c * rows + tokens] = residual[:, at]


def attention_kernel(heads, planes, idx, prefix, qg, *refs):
    messages, (spots, pick, out) = refs[:planes], refs[planes:]
    group, rows, _ = qg.shape
    z, r = idx[0], idx[1]
    lot, held = group * rows, pick.shape[0]
    tokens = held // group
    keys, values, key_spot = [], [], []
    for k in range(planes):
        keys.append(messages[k][:held, :HEAD_SIZE])
        values.append(messages[k][:held, HEAD_SIZE:])
        key_spot.append(spots[z ^ k])
    keys, values = jnp.concatenate(keys), jnp.concatenate(values)
    key_spot = jnp.concatenate(key_spot, axis=1)
    i = lax.broadcasted_iota(jnp.int32, (lot, held), 0) ^ (r * rows)
    j = lax.broadcasted_iota(jnp.int32, (lot, held), 1)
    source = i // rows * tokens + jnp.minimum(i % rows, tokens - 1)
    query_spot = jnp.sum(jnp.where(source == j, spots[z], 0.0), axis=1, keepdims=True)
    visible = (key_spot <= query_spot) | (key_spot < prefix[0].astype(F32))
    bias = jnp.where(visible, 0.0, HIDE)
    scale = 1.0 / math.sqrt(HEAD_SIZE)
    wide = jnp.concatenate([qg[b ^ r, :, 2 * HEAD_SIZE:] for b in range(group)])

    def by_head(start):
        return jnp.concatenate(
            [wide[:, (start + h) * HEAD_SIZE:(start + h + 1) * HEAD_SIZE] for h in range(heads)]
        )

    gate = by_head(heads).astype(F32)
    s = lax.dot_general(by_head(0), keys, NT, preferred_element_type=F32) * scale
    s = s + jnp.concatenate([bias] * heads)
    e = jnp.exp(s - jnp.max(s, axis=-1, keepdims=True))
    denom = jnp.sum(e, axis=-1, keepdims=True)
    attended = dot(e.astype(BF16), values) / denom
    gated = (attended / (1.0 + jnp.exp(-gate))).astype(BF16)
    done = [gated[h * lot:(h + 1) * lot] for h in range(heads)]
    out[...] = dot(pick[...], jnp.concatenate(done, axis=1)).astype(BF16)


def project_kernel(planes, idx, *refs):
    parts = refs[:planes]
    weights, (pick, keep, send, held, wide) = refs[planes:-5], refs[-5:]
    z, q = idx[0], idx[2]
    for k in range(planes):
        held[z ^ k] = parts[k][...]
    rows, width = parts[0].shape
    x = dot(pick[...], held[...].reshape(planes * rows, width)).astype(BF16)
    lanes = weights[0].shape[1]
    for c, weight in enumerate(weights):
        wide[:, pl.ds(pl.multiple_of((q ^ c) * lanes, lanes), lanes)] = weight[...]
    y = dot(x, wide[...]).astype(BF16)
    half = y.shape[0] // 2
    keep[...] = y[:half]
    send[...] = y[half:]


def core_sum_kernel(keep, got, *outs):
    rows = outs[0].shape[0]
    for i, out in enumerate(outs):
        at = slice(i * rows, (i + 1) * rows)
        out[...] = (keep[at].astype(F32) + got[at].astype(F32)).astype(out.dtype)


def hidden_kernel(planes, tokens, idx, *refs):
    parts, messages, out = refs[:-planes - 1], refs[-planes - 1:-1], refs[-1]
    total = parts[0][...]
    for part in parts[1:]:
        total = total + part[...].astype(F32)
    width = out.shape[1]
    pair = messages[0].shape[1]
    pieces = width // pair
    rows = -(-tokens // ROW_TILE) * ROW_TILE
    for k, message in enumerate(messages):
        i = lax.broadcasted_iota(jnp.int32, (out.shape[0], rows), 0)
        j = lax.broadcasted_iota(jnp.int32, (out.shape[0], rows), 1)
        place = jnp.where((i == j + (idx[0] ^ k) * tokens) & (j < tokens), 1.0, 0.0).astype(BF16)
        lot = message.shape[0] - pieces * rows
        held = [message[lot + c * rows:lot + (c + 1) * rows] for c in range(pieces)]
        total = total + dot(place, jnp.concatenate(held, axis=1))
    out[...] = total.astype(BF16)


def stack_kernel(*refs):
    *parts, out = refs
    for k, part in enumerate(parts):
        out[k] = part[...]


def split_gate_up_kernel(planes, sides, idx, gate, up, *outs):
    units = outs[0].shape[1] // (2 * planes)
    for c, out in enumerate(outs):
        for k in range(planes):
            chip = (idx[0] ^ k) * sides + (idx[3] ^ c)
            at = pl.ds(pl.multiple_of(chip * units, units), units)
            out[:, 2 * k * units:(2 * k + 1) * units] = gate[:, at]
            out[:, (2 * k + 1) * units:(2 * k + 2) * units] = up[:, at]


def split_rows_kernel(planes, per, idx, down, heads, message, own, own_heads, core_heads):
    sides = per // 2
    units, head_rows = own.shape[1], own_heads.shape[0]
    for k in range(planes):
        for c in range(sides):
            chip = (idx[0] ^ k) * sides + (idx[3] ^ c)
            start = pl.multiple_of(chip * units, units)
            rows = down[pl.ds(start, units), :]
            if c:
                message[k * units:(k + 1) * units] = rows
            else:
                own[k] = rows
    for c in range(per):
        rows = heads[pl.ds(pl.multiple_of((idx[2] ^ c) * head_rows, head_rows), head_rows), :]
        if c == 0:
            own_heads[...] = rows
        elif c == 1:
            core_heads[...] = rows
        else:
            start = planes * units + (c - 2) * head_rows
            message[start:start + head_rows] = rows


def regroup_kernel(own, message, *outs):
    *downs, near_heads, far_heads = outs
    units, head_rows = own.shape[1], near_heads.shape[0]
    for k, out in enumerate(downs):
        out[0] = own[k]
        out[1] = message[k * units:(k + 1) * units]
    start = len(downs) * units
    near_heads[...] = message[start:start + head_rows]
    far_heads[...] = message[start + head_rows:start + 2 * head_rows]


def gate_up_kernel(blocks, per, planes, idx, *refs):
    parts, pieces = refs[:blocks], refs[blocks:blocks + per]
    gain, same, *outs, held = refs[blocks + per:]
    x = jnp.concatenate([part[...] for part in parts]).astype(F32)
    rows, width = x.shape
    lanes = width // per
    square = jnp.sum(x * x, axis=1, keepdims=True)
    held[...] = (x * gain[idx[0]]).astype(BF16)
    x = [held[:, pl.ds(pl.multiple_of((idx[2] ^ c) * lanes, lanes), lanes)] for c in range(per)]
    x = jnp.concatenate(x, axis=1)
    columns = pieces[0].shape[1] // planes
    lane = lax.broadcasted_iota(jnp.int32, (rows, HEAD_SIZE), 1)
    high = square.astype(BF16).astype(F32)
    terms = jnp.where(lane == 0, high, jnp.where(lane == 1, square - high, 0.0)).astype(BF16)
    terms = lax.dot_general(terms, same[...], (((0,), (0,)), ((), ())), preferred_element_type=F32)
    keep, near, *fars = outs
    terms = terms[:ROW_TILE]
    split = rows // 2
    for k in range(planes):
        at = slice(k * columns, (k + 1) * columns)
        total = dot(x, jnp.concatenate([piece[:, at] for piece in pieces]))
        if k < 2:
            places = [(outs[k], 0, rows)]
        else:
            places = [(fars[2 * k - 4], split, rows), (fars[2 * k - 3], 0, split)]
        for out, start, end in places:
            many = end - start
            out[:many] = total[start:end].astype(out.dtype)
            if out.shape[0] > many:
                out[many:] = jnp.zeros((ROW_TILE, columns), out.dtype)
                out[many:, :rows] = terms.astype(out.dtype)


def far_sum_kernel(rows, kept, got, out):
    total = kept[...] + got[...].astype(F32)
    out[:rows] = total[:rows].astype(BF16)
    if out.shape[0] > rows:
        square = jnp.sum(total[rows:], axis=0, keepdims=True)
        high = square.astype(BF16).astype(F32)
        row = lax.broadcasted_iota(jnp.int32, (out.shape[0] - rows, total.shape[1]), 0)
        terms = jnp.where(row == 0, high, jnp.where(row == 1, square - high, 0.0))
        out[rows:] = terms.astype(BF16)


def down_kernel(start, planes, per, features, idx, keep, got, far_head, far_part, near, far, same, *outs):
    many = same.shape[0]
    half = many // 2
    at = slice(start, start + half)
    total = keep[at] + got[at].astype(F32) + far_part[:half].astype(F32)
    terms = [keep[many:, :many], got[many:, :many].astype(F32), far_head[half:, :many].astype(F32)]
    units = total.shape[1] // 2
    square = jnp.concatenate(terms).astype(BF16)
    square = lax.dot_general(same[at], square, NT, preferred_element_type=F32)
    square = jnp.sum(square, axis=1, keepdims=True)
    factor = lax.rsqrt(square / features + 1e-06)
    gate, up = total[:, :units] * factor, total[:, units:] * factor
    activated = (gate / (1.0 + jnp.exp(-gate)) * up).astype(BF16)
    z, q = idx[0], idx[2]
    rows = outs[0].shape[1]
    for k in range(planes):
        w = [(far if c % 2 else near)[k, c // 2] for c in range(per)]
        y = dot(activated, jnp.concatenate(w, axis=1))
        lanes = w[0].shape[1]
        for c in range(per):
            at = pl.ds(pl.multiple_of((q ^ c) * lanes, lanes), lanes)
            block = y[:, c * lanes:(c + 1) * lanes]
            for i, out in enumerate(outs):
                out[z ^ k, :, at] = block[i * rows:(i + 1) * rows].astype(out.dtype)


def plane_sum_kernel(planes, tokens, idx, hidden, *refs):
    parts, outs = refs[:-planes], refs[-planes:]
    total = parts[0][...]
    for part in parts[1:]:
        total = total + part[...].astype(F32)
    total = total.astype(BF16)
    share = hidden.shape[0]
    source = jnp.concatenate([total[p] for p in range(planes)] + [hidden[...]])
    for k, out in enumerate(outs):
        i = lax.broadcasted_iota(jnp.int32, (out.shape[0], source.shape[0]), 0)
        j = lax.broadcasted_iota(jnp.int32, (out.shape[0], source.shape[0]), 1)
        spot = i // tokens * share + (idx[0] ^ k) * tokens + i % tokens
        pick = jnp.where((spot == j) & (i < (planes + 1) * tokens), 1.0, 0.0).astype(BF16)
        out[...] = dot(pick, source).astype(BF16)


def last_kernel(planes, tokens, idx, *refs):
    *parts, out, held = refs
    width = parts[0].shape[1]
    total = parts[0][...].astype(F32)
    for part in parts[1:]:
        total = total + part[...].astype(F32)
    end = planes * tokens
    for k, part in enumerate(parts):
        held[idx[0] ^ k, :tokens] = part[...].astype(F32)[end:end + tokens]
    for p in range(planes):
        value = held[p, :tokens] + total[p * tokens:(p + 1) * tokens]
        out[:, p * width:(p + 1) * width] = value.astype(BF16)


def call(kernel, outs, *args, scratch=(), limit=16):
    single = not isinstance(outs, list)
    shapes = [outs] if single else outs
    got = pl.pallas_call(
        kernel,
        out_shape=shapes,
        in_specs=[SMEM if a.dtype == jnp.int32 else VMEM for a in args],
        out_specs=[VMEM] * len(shapes),
        scratch_shapes=list(scratch),
        compiler_params=pltpu.CompilerParams(vmem_limit_bytes=limit * 2**20),
    )(*args)
    return got[0] if single else list(got)


def like(*shape, dtype=BF16):
    return jax.ShapeDtypeStruct(shape, dtype)


def move_tokens(
    n_blk,
    n_uly,
    residual,
    query_projection,
    key_projection,
    value_projection,
    gate_proj,
    positions,
    prefix_len,
    out_weight,
    norm_gain,
    gate_weight,
    up_weight,
    down_weight,
):
    axes = ("blk", "uly")
    kv_heads = key_projection.shape[1] // HEAD_SIZE
    heads = query_projection.shape[1] // key_projection.shape[1]
    tokens, features = residual.shape
    rows = -(-tokens // ROW_TILE) * ROW_TILE
    group = kv_heads
    per = group // n_uly
    planes = n_blk // per
    devices = n_blk * n_uly
    me = lax.axis_index("blk") * n_uly + lax.axis_index("uly")
    z, r = me // group, me % group
    idx = jnp.stack([z, r, r // n_uly, r // (2 * n_uly)]).astype(jnp.int32)
    core = n_uly
    near = [b for b in range(group) if not b & core]
    order = near + [b ^ core for b in near]
    steps = near[1:]

    def swap(x, mask):
        return lax.ppermute(x, axes, [(i, i ^ mask) for i in range(devices)])

    def swap_planes(x):
        return [swap(x, k * group) for k in range(1, planes)]

    head_of = [(i % n_uly) * per + i // n_uly for i in range(group)]
    plane_groups = [[p * group + i for i in range(group)] for p in range(planes)]

    def plane_exchange(x):
        return lax.all_to_all(x, axes, 0, 0, axis_index_groups=plane_groups, tiled=True)

    def after(*xs):
        return lax.optimization_barrier(xs)

    width = features // planes
    sides = per // 2
    units = gate_weight.shape[1] // (planes * sides)

    def across_planes(parts):
        return [x if not k else swap(x, k * group) for k, x in enumerate(parts)]

    pair = 2 * HEAD_SIZE
    tokens_in = (key_projection, value_projection, query_projection, gate_proj)
    head_groups = call(
        functools.partial(pack_heads_kernel, head_of),
        like(group, rows, 2 * heads * HEAD_SIZE + pair),
        *tokens_in,
        limit=60,
    )
    head_groups, gate_weight, up_weight, down_weight, out_weight, positions = after(
        head_groups, gate_weight, up_weight, down_weight, out_weight, positions
    )
    side = 2 * n_uly
    gate_up = call(
        functools.partial(split_gate_up_kernel, planes, sides),
        [like(gate_weight.shape[0], 2 * planes * units)] * sides,
        idx, gate_weight, up_weight,
    )
    head_rows = out_weight.shape[0] // per
    lanes = out_weight.shape[1]
    message, own_down, wo_own, wo_core = call(
        functools.partial(split_rows_kernel, planes, per),
        [
            like(planes * units + 2 * head_rows, lanes),
            like(planes, units, lanes),
            like(head_rows, lanes),
            like(head_rows, lanes),
        ],
        idx, down_weight, out_weight,
    )
    spots = positions.astype(F32).reshape(planes, 1, group * tokens)
    own_heads = plane_exchange(head_groups)
    wo_core = swap(wo_core, core)
    own_heads, message, gate_up, wo_core, spots = after(
        own_heads, message, gate_up, wo_core, spots
    )
    pick = np.zeros((group, tokens, group, rows), np.float32)
    for b in range(group):
        for t in range(tokens):
            pick[b, t, b, t] = 1
    pick = jnp.asarray(pick.reshape(group * tokens, group * rows), BF16)
    messages = across_planes(
        call(
            functools.partial(message_kernel, planes),
            [like(group * tokens + rows * width // pair, pair)] * planes,
            idx, own_heads, residual, pick,
        )
    )
    message = swap(message, side)
    twin = [swap(gate_up[0], core), None]
    *messages, gate_up[1], twin[0] = after(*messages[::-1], gate_up[1], twin[0])
    messages = messages[::-1]
    gate_up[1] = swap(gate_up[1], side)
    gated = call(
        functools.partial(attention_kernel, heads, planes),
        like(group * tokens, heads * HEAD_SIZE),
        idx, prefix_len, own_heads, *messages, spots, pick,
    )
    gated, message = after(gated, message)
    *down_parts, wo_near, wo_far = call(
        regroup_kernel,
        [like(sides, units, lanes)] * planes + [like(head_rows, lanes)] * 2,
        own_down, message,
    )
    gateds = [gated] + swap_planes(gated)
    wo = [wo_own, wo_core, wo_near, swap(wo_far, core)]
    gateds, wo, down_parts = after(gateds, wo, down_parts)
    for k in (1, 2):
        down_parts[k] = swap(down_parts[k], k * group)

    turn = np.zeros((group, planes, tokens, planes, group, tokens), np.float32)
    for i, b in enumerate(order):
        for p in range(planes):
            for t in range(tokens):
                turn[i, p, t, p, b, t] = 1
    total = devices * tokens
    turn = jnp.asarray(turn.reshape(total, total), BF16)
    keep, send = call(
        functools.partial(project_kernel, planes),
        [like(total // 2, width)] * 2,
        idx, *gateds, *wo, turn,
        scratch=[
            pltpu.VMEM((planes,) + gated.shape, BF16),
            pltpu.VMEM((wo[0].shape[0], width), BF16),
        ],
    )
    share = total // group
    own, *rest = call(
        core_sum_kernel,
        [like(share, width, dtype=F32)] + [like(share, width)] * len(steps),
        keep, swap(send, core),
    )
    rest, gate_up[1] = after(rest, gate_up[1])
    hidden = call(
        functools.partial(hidden_kernel, planes, tokens),
        like(share, width),
        idx, own, *[swap(x, b) for x, b in zip(rest, steps)], *messages,
    )
    hidden, gate_up[1], down_parts = after(hidden, gate_up[1], down_parts)
    down_parts[3] = swap(down_parts[3], 3 * group)
    twin[1] = swap(gate_up[1], core)
    blocks = [hidden] + [swap(hidden, b) for b in steps]
    same = jnp.eye(len(blocks) * share, dtype=BF16)
    pieces = [x for both in zip(gate_up, twin) for x in both]
    many = len(blocks) * share
    group_far = planes // 2 * group
    split = many // 2
    ends = (split + ROW_TILE, split)
    keep, near_send, *fars = call(
        functools.partial(gate_up_kernel, len(blocks), per, planes),
        [like(many + ROW_TILE, 2 * units, dtype=F32), like(many + ROW_TILE, 2 * units)]
        + [like(rows_, 2 * units, dtype=F32) for rows_ in ends]
        + [like(rows_, 2 * units) for rows_ in ends],
        idx, *blocks, *pieces, norm_gain.reshape(planes, 1, width), same,
        scratch=[pltpu.VMEM((many, width), BF16)],
    )
    far_keeps, far_sends = fars[:2], fars[2:]
    far_sends[0], down_parts = after(far_sends[0], down_parts)

    def far_sum(i, got):
        return call(
            functools.partial(far_sum_kernel, split), like(ends[i], 2 * units), far_keeps[i], got
        )

    got = swap(far_sends[0], group)
    far_head = swap(far_sum(0, got), group_far)
    got, near_send = after(swap(far_sends[1], group), near_send)
    far_rest = swap(far_sum(1, got), group_far)
    near_got = swap(near_send, group)
    downs = call(stack_kernel, like(planes, *down_parts[0].shape), *down_parts)
    weights = [downs, swap(downs, core), same]

    def ffn_out(start, part, dtypes):
        return call(
            functools.partial(down_kernel, start, planes, per, features),
            [like(planes, share, width, dtype=dtype) for dtype in dtypes],
            idx, keep, near_got, far_head, part, *weights,
        )

    late = ffn_out(split, far_head, [BF16, BF16])
    own, early = ffn_out(0, far_rest, [F32, BF16])
    rest = [early] + late
    parts = call(
        functools.partial(plane_sum_kernel, planes, tokens),
        [like(-(-(planes + 1) * tokens // ROW_TILE) * ROW_TILE, width)] * planes,
        idx, hidden, own, *[swap(x, b) for x, b in zip(rest, steps)],
    )
    return call(
        functools.partial(last_kernel, planes, tokens),
        like(tokens, features),
        idx, *after(*across_planes(parts)[::-1])[::-1],
        scratch=[pltpu.VMEM((planes, rows, width), F32)],
    )


def tokens_can_travel(n_blk, n_uly, kv_heads, token_count, unit_count):
    def power(n):
        return n > 0 and not n & (n - 1)

    per = kv_heads // n_uly
    return (
        power(n_blk)
        and power(n_uly)
        and power(kv_heads)
        and per == 4
        and n_blk == 4 * per
        and token_count < unit_count // n_uly
    )


def solution(mesh):
    n_blk, n_uly = mesh.shape["blk"], mesh.shape["uly"]

    def per_device(*args):
        residual, key_projection, gate_weight = args[0], args[2], args[9]
        travel = tokens_can_travel(
            n_blk,
            n_uly,
            key_projection.shape[1] // HEAD_SIZE,
            residual.shape[0] * n_blk * n_uly,
            gate_weight.shape[1] * n_uly,
        )
        if travel:
            return move_tokens(n_blk, n_uly, *args)
        return move_weights(*args)

    return jax.shard_map(
        per_device,
        mesh=mesh,
        in_specs=(
            P(("blk", "uly"), None),
            P(("blk", "uly"), None),
            P(("blk", "uly"), None),
            P(("blk", "uly"), None),
            P(("blk", "uly"), None),
            P(),
            P(),
            P("uly", "blk"),
            P(),
            P("blk", "uly"),
            P("blk", "uly"),
            P("uly", "blk"),
        ),
        out_specs=P(("blk", "uly"), None),
        check_vma=False,
    )
```

```python
import functools
import math

import jax
import jax.numpy as jnp
import numpy as np
from jax import lax
from jax.experimental import pallas as pl
from jax.experimental.pallas import tpu as pltpu
from jax.sharding import PartitionSpec as P

HEAD_SIZE = 128
ROW_TILE = 16
HIDE = -1e30
F32 = jnp.float32
BF16 = jnp.bfloat16
VMEM = pl.BlockSpec(memory_space=pltpu.VMEM)
SMEM = pl.BlockSpec(memory_space=pltpu.SMEM)
NT = (((1,), (1,)), ((), ()))


def move_weights(
    residual,
    query_projection,
    key_projection,
    value_projection,
    gate_proj,
    positions,
    prefix_len,
    out_weight,
    norm_gain,
    gate_weight,
    up_weight,
    down_weight,
):
    q_loc, k_loc, v_loc, g_loc = (
        lax.all_to_all(query_projection, "uly", split_axis=1, concat_axis=0, tiled=True),
        lax.all_to_all(key_projection, "uly", split_axis=1, concat_axis=0, tiled=True),
        lax.all_to_all(value_projection, "uly", split_axis=1, concat_axis=0, tiled=True),
        lax.all_to_all(gate_proj, "uly", split_axis=1, concat_axis=0, tiled=True),
    )
    row_count = q_loc.shape[0]
    kv_heads = k_loc.shape[1] // HEAD_SIZE
    q_heads = q_loc.shape[1] // HEAD_SIZE
    heads_per_group = q_heads // kv_heads
    score_scale = 1.0 / math.sqrt(HEAD_SIZE)
    blk_index = lax.axis_index("blk")
    query_pos = lax.dynamic_slice_in_dim(positions, blk_index * row_count, row_count)
    prefix = prefix_len[0]
    query_heads = q_loc.reshape(row_count, kv_heads, heads_per_group, HEAD_SIZE)
    wo_full, wg_full, wu_full, wd_full = (
        lax.all_gather(out_weight, "blk", axis=1, tiled=True),
        lax.all_gather(gate_weight, "blk", axis=0, tiled=True),
        lax.all_gather(up_weight, "blk", axis=0, tiled=True),
        lax.all_gather(down_weight, "blk", axis=1, tiled=True),
    )
    key_part = lax.all_gather(k_loc, "blk", axis=0, tiled=True)
    value_part = lax.all_gather(v_loc, "blk", axis=0, tiled=True)
    key_count = key_part.shape[0]
    scores = (
        jnp.einsum(
            "bkgd,skd->bkgs",
            query_heads,
            key_part.reshape(key_count, kv_heads, HEAD_SIZE),
            preferred_element_type=F32,
        )
        * score_scale
    )
    visible = (positions[None, :] <= query_pos[:, None]) | (positions[None, :] < prefix)
    scores = jnp.where(visible[:, None, None, :], scores, -jnp.inf)
    row_max = jnp.max(scores, axis=-1)
    exp_scores = jnp.exp(scores - row_max[..., None])
    denom = jnp.sum(exp_scores, axis=-1)
    probs = exp_scores.astype(BF16)
    weighted = jnp.einsum(
        "bkgs,skd->bkgd",
        probs,
        value_part.reshape(key_count, kv_heads, HEAD_SIZE),
        preferred_element_type=F32,
    )
    attended = (weighted / denom[..., None]).reshape(row_count, q_heads * HEAD_SIZE)
    gated_out = (attended * jax.nn.sigmoid(g_loc.astype(F32))).astype(BF16)
    head_partial = jnp.dot(gated_out, wo_full, preferred_element_type=F32)
    projected = lax.psum_scatter(
        head_partial.astype(BF16), "uly", scatter_dimension=0, tiled=True
    ).astype(F32)
    hidden_f = (residual.astype(F32) + projected).astype(BF16).astype(F32)
    mean_sq = jnp.mean(hidden_f * hidden_f, axis=-1, keepdims=True)
    normed = (hidden_f * lax.rsqrt(mean_sq + 1e-06) * norm_gain).astype(BF16)
    group_rows = lax.all_gather(normed, "uly", axis=0, tiled=True)
    gate_sum = jnp.dot(group_rows, wg_full, preferred_element_type=F32)
    up_sum = jnp.dot(group_rows, wu_full, preferred_element_type=F32)
    activated = (jax.nn.silu(gate_sum) * up_sum).astype(BF16)
    ffn_partial = jnp.dot(activated, wd_full, preferred_element_type=F32)
    ffn_out = lax.psum_scatter(
        ffn_partial.astype(BF16), "uly", scatter_dimension=0, tiled=True
    ).astype(F32)
    return (hidden_f + ffn_out).astype(BF16)


def dot(a, b):
    return jnp.dot(a, b, preferred_element_type=F32)


def pack_heads_kernel(head_of, *refs):
    *parts, out = refs
    out[...] = jnp.zeros_like(out)
    tokens = parts[0].shape[0]
    start = 0
    for part in parts:
        width = part.shape[1] // len(head_of)
        for r, j in enumerate(head_of):
            out[r, :tokens, start:start + width] = part[:, j * width:(j + 1) * width]
        start += width


def message_kernel(planes, idx, heads, residual, pick, *outs):
    group, rows, _ = heads.shape
    tokens, features = residual.shape
    pair = 2 * HEAD_SIZE
    width = features // planes
    z = idx[0]
    keys = dot(pick[...], heads[:, :, :pair].reshape(group * rows, pair)).astype(BF16)
    lot = keys.shape[0]
    for k, out in enumerate(outs):
        out[:lot] = keys
        out[lot:] = jnp.zeros((out.shape[0] - lot, pair), BF16)
        for c in range(width // pair):
            at = pl.ds(pl.multiple_of((z ^ k) * width + c * pair, pair), pair)
            out[lot + c * rows:lot + c * rows + tokens] = residual[:, at]


def attention_kernel(heads, planes, idx, prefix, qg, *refs):
    messages, (spots, pick, out) = refs[:planes], refs[planes:]
    group, rows, _ = qg.shape
    z, r = idx[0], idx[1]
    lot, held = group * rows, pick.shape[0]
    tokens = held // group
    keys, values, key_spot = [], [], []
    for k in range(planes):
        keys.append(messages[k][:held, :HEAD_SIZE])
        values.append(messages[k][:held, HEAD_SIZE:])
        key_spot.append(spots[z ^ k])
    keys, values = jnp.concatenate(keys), jnp.concatenate(values)
    key_spot = jnp.concatenate(key_spot, axis=1)
    i = lax.broadcasted_iota(jnp.int32, (lot, held), 0) ^ (r * rows)
    j = lax.broadcasted_iota(jnp.int32, (lot, held), 1)
    source = i // rows * tokens + jnp.minimum(i % rows, tokens - 1)
    query_spot = jnp.sum(jnp.where(source == j, spots[z], 0.0), axis=1, keepdims=True)
    visible = (key_spot <= query_spot) | (key_spot < prefix[0].astype(F32))
    bias = jnp.where(visible, 0.0, HIDE)
    scale = 1.0 / math.sqrt(HEAD_SIZE)
    wide = jnp.concatenate([qg[b ^ r, :, 2 * HEAD_SIZE:] for b in range(group)])

    def by_head(start):
        return jnp.concatenate(
            [wide[:, (start + h) * HEAD_SIZE:(start + h + 1) * HEAD_SIZE] for h in range(heads)]
        )

    gate = by_head(heads).astype(F32)
    s = lax.dot_general(by_head(0), keys, NT, preferred_element_type=F32) * scale
    s = s + jnp.concatenate([bias] * heads)
    e = jnp.exp(s - jnp.max(s, axis=-1, keepdims=True))
    denom = jnp.sum(e, axis=-1, keepdims=True)
    attended = dot(e.astype(BF16), values) / denom
    gated = (attended / (1.0 + jnp.exp(-gate))).astype(BF16)
    done = [gated[h * lot:(h + 1) * lot] for h in range(heads)]
    out[...] = dot(pick[...], jnp.concatenate(done, axis=1)).astype(BF16)


def project_kernel(planes, idx, *refs):
    parts = refs[:planes]
    weights, (pick, keep, send, held, wide) = refs[planes:-5], refs[-5:]
    z, q = idx[0], idx[2]
    for k in range(planes):
        held[z ^ k] = parts[k][...]
    rows, width = parts[0].shape
    x = dot(pick[...], held[...].reshape(planes * rows, width)).astype(BF16)
    lanes = weights[0].shape[1]
    for c, weight in enumerate(weights):
        wide[:, pl.ds(pl.multiple_of((q ^ c) * lanes, lanes), lanes)] = weight[...]
    y = dot(x, wide[...]).astype(BF16)
    half = y.shape[0] // 2
    keep[...] = y[:half]
    send[...] = y[half:]


def core_sum_kernel(keep, got, *outs):
    rows = outs[0].shape[0]
    for i, out in enumerate(outs):
        at = slice(i * rows, (i + 1) * rows)
        out[...] = (keep[at].astype(F32) + got[at].astype(F32)).astype(out.dtype)


def hidden_kernel(planes, tokens, idx, *refs):
    parts, messages, out = refs[:-planes - 1], refs[-planes - 1:-1], refs[-1]
    total = parts[0][...]
    for part in parts[1:]:
        total = total + part[...].astype(F32)
    width = out.shape[1]
    pair = messages[0].shape[1]
    pieces = width // pair
    rows = -(-tokens // ROW_TILE) * ROW_TILE
    for k, message in enumerate(messages):
        i = lax.broadcasted_iota(jnp.int32, (out.shape[0], rows), 0)
        j = lax.broadcasted_iota(jnp.int32, (out.shape[0], rows), 1)
        place = jnp.where((i == j + (idx[0] ^ k) * tokens) & (j < tokens), 1.0, 0.0).astype(BF16)
        lot = message.shape[0] - pieces * rows
        held = [message[lot + c * rows:lot + (c + 1) * rows] for c in range(pieces)]
        total = total + dot(place, jnp.concatenate(held, axis=1))
    out[...] = total.astype(BF16)


def stack_kernel(*refs):
    *parts, out = refs
    for k, part in enumerate(parts):
        out[k] = part[...]


def split_gate_up_kernel(planes, sides, idx, gate, up, *outs):
    units = outs[0].shape[1] // (2 * planes)
    for c, out in enumerate(outs):
        for k in range(planes):
            chip = (idx[0] ^ k) * sides + (idx[3] ^ c)
            at = pl.ds(pl.multiple_of(chip * units, units), units)
            out[:, 2 * k * units:(2 * k + 1) * units] = gate[:, at]
            out[:, (2 * k + 1) * units:(2 * k + 2) * units] = up[:, at]


def split_rows_kernel(planes, per, idx, down, heads, message, own, own_heads, core_heads):
    sides = per // 2
    units, head_rows = own.shape[1], own_heads.shape[0]
    for k in range(planes):
        for c in range(sides):
            chip = (idx[0] ^ k) * sides + (idx[3] ^ c)
            start = pl.multiple_of(chip * units, units)
            rows = down[pl.ds(start, units), :]
            if c:
                message[k * units:(k + 1) * units] = rows
            else:
                own[k] = rows
    for c in range(per):
        rows = heads[pl.ds(pl.multiple_of((idx[2] ^ c) * head_rows, head_rows), head_rows), :]
        if c == 0:
            own_heads[...] = rows
        elif c == 1:
            core_heads[...] = rows
        else:
            start = planes * units + (c - 2) * head_rows
            message[start:start + head_rows] = rows


def regroup_kernel(own, message, *outs):
    *downs, near_heads, far_heads = outs
    units, head_rows = own.shape[1], near_heads.shape[0]
    for k, out in enumerate(downs):
        out[0] = own[k]
        out[1] = message[k * units:(k + 1) * units]
    start = len(downs) * units
    near_heads[...] = message[start:start + head_rows]
    far_heads[...] = message[start + head_rows:start + 2 * head_rows]


def gate_up_kernel(blocks, per, planes, idx, *refs):
    parts, pieces = refs[:blocks], refs[blocks:blocks + per]
    gain, same, *outs, held = refs[blocks + per:]
    x = jnp.concatenate([part[...] for part in parts]).astype(F32)
    rows, width = x.shape
    lanes = width // per
    square = jnp.sum(x * x, axis=1, keepdims=True)
    held[...] = (x * gain[idx[0]]).astype(BF16)
    x = [held[:, pl.ds(pl.multiple_of((idx[2] ^ c) * lanes, lanes), lanes)] for c in range(per)]
    x = jnp.concatenate(x, axis=1)
    columns = pieces[0].shape[1] // planes
    lane = lax.broadcasted_iota(jnp.int32, (rows, HEAD_SIZE), 1)
    high = square.astype(BF16).astype(F32)
    terms = jnp.where(lane == 0, high, jnp.where(lane == 1, square - high, 0.0)).astype(BF16)
    terms = lax.dot_general(terms, same[...], (((0,), (0,)), ((), ())), preferred_element_type=F32)
    keep, near, *fars = outs
    terms = terms[:ROW_TILE]
    split = rows // 2
    for k in range(planes):
        at = slice(k * columns, (k + 1) * columns)
        total = dot(x, jnp.concatenate([piece[:, at] for piece in pieces]))
        if k < 2:
            places = [(outs[k], 0, rows)]
        else:
            places = [(fars[2 * k - 4], split, rows), (fars[2 * k - 3], 0, split)]
        for out, start, end in places:
            many = end - start
            out[:many] = total[start:end].astype(out.dtype)
            if out.shape[0] > many:
                out[many:] = jnp.zeros((ROW_TILE, columns), out.dtype)
                out[many:, :rows] = terms.astype(out.dtype)


def far_sum_kernel(rows, kept, got, out):
    total = kept[...] + got[...].astype(F32)
    out[:rows] = total[:rows].astype(BF16)
    if out.shape[0] > rows:
        square = jnp.sum(total[rows:], axis=0, keepdims=True)
        high = square.astype(BF16).astype(F32)
        row = lax.broadcasted_iota(jnp.int32, (out.shape[0] - rows, total.shape[1]), 0)
        terms = jnp.where(row == 0, high, jnp.where(row == 1, square - high, 0.0))
        out[rows:] = terms.astype(BF16)


def down_kernel(start, planes, per, features, idx, keep, got, far_head, far_part, near, far, same, *outs):
    many = same.shape[0]
    half = many // 2
    at = slice(start, start + half)
    total = keep[at] + got[at].astype(F32) + far_part[:half].astype(F32)
    terms = [keep[many:, :many], got[many:, :many].astype(F32), far_head[half:, :many].astype(F32)]
    units = total.shape[1] // 2
    square = jnp.concatenate(terms).astype(BF16)
    square = lax.dot_general(same[at], square, NT, preferred_element_type=F32)
    square = jnp.sum(square, axis=1, keepdims=True)
    factor = lax.rsqrt(square / features + 1e-06)
    gate, up = total[:, :units] * factor, total[:, units:] * factor
    activated = (gate / (1.0 + jnp.exp(-gate)) * up).astype(BF16)
    z, q = idx[0], idx[2]
    rows = outs[0].shape[1]
    for k in range(planes):
        w = [(far if c % 2 else near)[k, c // 2] for c in range(per)]
        y = dot(activated, jnp.concatenate(w, axis=1))
        lanes = w[0].shape[1]
        for c in range(per):
            at = pl.ds(pl.multiple_of((q ^ c) * lanes, lanes), lanes)
            block = y[:, c * lanes:(c + 1) * lanes]
            for i, out in enumerate(outs):
                out[z ^ k, :, at] = block[i * rows:(i + 1) * rows].astype(out.dtype)


def plane_sum_kernel(planes, tokens, idx, hidden, *refs):
    parts, outs = refs[:-planes], refs[-planes:]
    total = parts[0][...]
    for part in parts[1:]:
        total = total + part[...].astype(F32)
    total = total.astype(BF16)
    share = hidden.shape[0]
    source = jnp.concatenate([total[p] for p in range(planes)] + [hidden[...]])
    for k, out in enumerate(outs):
        i = lax.broadcasted_iota(jnp.int32, (out.shape[0], source.shape[0]), 0)
        j = lax.broadcasted_iota(jnp.int32, (out.shape[0], source.shape[0]), 1)
        spot = i // tokens * share + (idx[0] ^ k) * tokens + i % tokens
        pick = jnp.where((spot == j) & (i < (planes + 1) * tokens), 1.0, 0.0).astype(BF16)
        out[...] = dot(pick, source).astype(BF16)


def last_kernel(planes, tokens, idx, *refs):
    *parts, out, held = refs
    width = parts[0].shape[1]
    total = parts[0][...].astype(F32)
    for part in parts[1:]:
        total = total + part[...].astype(F32)
    end = planes * tokens
    for k, part in enumerate(parts):
        held[idx[0] ^ k, :tokens] = part[...].astype(F32)[end:end + tokens]
    for p in range(planes):
        value = held[p, :tokens] + total[p * tokens:(p + 1) * tokens]
        out[:, p * width:(p + 1) * width] = value.astype(BF16)


def call(kernel, outs, *args, scratch=(), limit=16):
    single = not isinstance(outs, list)
    shapes = [outs] if single else outs
    got = pl.pallas_call(
        kernel,
        out_shape=shapes,
        in_specs=[SMEM if a.dtype == jnp.int32 else VMEM for a in args],
        out_specs=[VMEM] * len(shapes),
        scratch_shapes=list(scratch),
        compiler_params=pltpu.CompilerParams(vmem_limit_bytes=limit * 2**20),
    )(*args)
    return got[0] if single else list(got)


def like(*shape, dtype=BF16):
    return jax.ShapeDtypeStruct(shape, dtype)


def move_tokens(
    n_blk,
    n_uly,
    residual,
    query_projection,
    key_projection,
    value_projection,
    gate_proj,
    positions,
    prefix_len,
    out_weight,
    norm_gain,
    gate_weight,
    up_weight,
    down_weight,
):
    axes = ("blk", "uly")
    kv_heads = key_projection.shape[1] // HEAD_SIZE
    heads = query_projection.shape[1] // key_projection.shape[1]
    tokens, features = residual.shape
    rows = -(-tokens // ROW_TILE) * ROW_TILE
    group = kv_heads
    per = group // n_uly
    planes = n_blk // per
    devices = n_blk * n_uly
    me = lax.axis_index("blk") * n_uly + lax.axis_index("uly")
    z, r = me // group, me % group
    idx = jnp.stack([z, r, r // n_uly, r // (2 * n_uly)]).astype(jnp.int32)
    core = n_uly
    near = [b for b in range(group) if not b & core]
    order = near + [b ^ core for b in near]
    steps = near[1:]

    def swap(x, mask):
        return lax.ppermute(x, axes, [(i, i ^ mask) for i in range(devices)])

    def swap_planes(x):
        return [swap(x, k * group) for k in range(1, planes)]

    head_of = [(i % n_uly) * per + i // n_uly for i in range(group)]
    plane_groups = [[p * group + i for i in range(group)] for p in range(planes)]

    def plane_exchange(x):
        return lax.all_to_all(x, axes, 0, 0, axis_index_groups=plane_groups, tiled=True)

    def after(*xs):
        return lax.optimization_barrier(xs)

    width = features // planes
    sides = per // 2
    units = gate_weight.shape[1] // (planes * sides)

    def across_planes(parts):
        return [x if not k else swap(x, k * group) for k, x in enumerate(parts)]

    pair = 2 * HEAD_SIZE
    tokens_in = (key_projection, value_projection, query_projection, gate_proj)
    head_groups = call(
        functools.partial(pack_heads_kernel, head_of),
        like(group, rows, 2 * heads * HEAD_SIZE + pair),
        *tokens_in,
        limit=60,
    )
    head_groups, gate_weight, up_weight, down_weight, out_weight, positions = after(
        head_groups, gate_weight, up_weight, down_weight, out_weight, positions
    )
    side = 2 * n_uly
    gate_up = call(
        functools.partial(split_gate_up_kernel, planes, sides),
        [like(gate_weight.shape[0], 2 * planes * units)] * sides,
        idx, gate_weight, up_weight,
    )
    head_rows = out_weight.shape[0] // per
    lanes = out_weight.shape[1]
    message, own_down, wo_own, wo_core = call(
        functools.partial(split_rows_kernel, planes, per),
        [
            like(planes * units + 2 * head_rows, lanes),
            like(planes, units, lanes),
            like(head_rows, lanes),
            like(head_rows, lanes),
        ],
        idx, down_weight, out_weight,
    )
    spots = positions.astype(F32).reshape(planes, 1, group * tokens)
    own_heads = plane_exchange(head_groups)
    wo_core = swap(wo_core, core)
    own_heads, message, gate_up, wo_core, spots = after(
        own_heads, message, gate_up, wo_core, spots
    )
    pick = np.zeros((group, tokens, group, rows), np.float32)
    for b in range(group):
        for t in range(tokens):
            pick[b, t, b, t] = 1
    pick = jnp.asarray(pick.reshape(group * tokens, group * rows), BF16)
    messages = across_planes(
        call(
            functools.partial(message_kernel, planes),
            [like(group * tokens + rows * width // pair, pair)] * planes,
            idx, own_heads, residual, pick,
        )
    )
    message = swap(message, side)
    twin = [swap(gate_up[0], core), None]
    *messages, gate_up[1], twin[0] = after(*messages[::-1], gate_up[1], twin[0])
    messages = messages[::-1]
    gate_up[1] = swap(gate_up[1], side)
    gated = call(
        functools.partial(attention_kernel, heads, planes),
        like(group * tokens, heads * HEAD_SIZE),
        idx, prefix_len, own_heads, *messages, spots, pick,
    )
    gated, message = after(gated, message)
    *down_parts, wo_near, wo_far = call(
        regroup_kernel,
        [like(sides, units, lanes)] * planes + [like(head_rows, lanes)] * 2,
        own_down, message,
    )
    gateds = [gated] + swap_planes(gated)
    wo = [wo_own, wo_core, wo_near, swap(wo_far, core)]
    gateds, wo, down_parts = after(gateds, wo, down_parts)
    for k in (1, 2):
        down_parts[k] = swap(down_parts[k], k * group)

    turn = np.zeros((group, planes, tokens, planes, group, tokens), np.float32)
    for i, b in enumerate(order):
        for p in range(planes):
            for t in range(tokens):
                turn[i, p, t, p, b, t] = 1
    total = devices * tokens
    turn = jnp.asarray(turn.reshape(total, total), BF16)
    keep, send = call(
        functools.partial(project_kernel, planes),
        [like(total // 2, width)] * 2,
        idx, *gateds, *wo, turn,
        scratch=[
            pltpu.VMEM((planes,) + gated.shape, BF16),
            pltpu.VMEM((wo[0].shape[0], width), BF16),
        ],
    )
    share = total // group
    own, *rest = call(
        core_sum_kernel,
        [like(share, width, dtype=F32)] + [like(share, width)] * len(steps),
        keep, swap(send, core),
    )
    rest, gate_up[1] = after(rest, gate_up[1])
    hidden = call(
        functools.partial(hidden_kernel, planes, tokens),
        like(share, width),
        idx, own, *[swap(x, b) for x, b in zip(rest, steps)], *messages,
    )
    hidden, gate_up[1], down_parts = after(hidden, gate_up[1], down_parts)
    down_parts[3] = swap(down_parts[3], 3 * group)
    twin[1] = swap(gate_up[1], core)
    blocks = [hidden] + [swap(hidden, b) for b in steps]
    same = jnp.eye(len(blocks) * share, dtype=BF16)
    pieces = [x for both in zip(gate_up, twin) for x in both]
    many = len(blocks) * share
    group_far = planes // 2 * group
    split = many // 2
    ends = (split + ROW_TILE, split)
    keep, near_send, *fars = call(
        functools.partial(gate_up_kernel, len(blocks), per, planes),
        [like(many + ROW_TILE, 2 * units, dtype=F32), like(many + ROW_TILE, 2 * units)]
        + [like(rows_, 2 * units, dtype=F32) for rows_ in ends]
        + [like(rows_, 2 * units) for rows_ in ends],
        idx, *blocks, *pieces, norm_gain.reshape(planes, 1, width), same,
        scratch=[pltpu.VMEM((many, width), BF16)],
    )
    far_keeps, far_sends = fars[:2], fars[2:]
    far_sends[0], down_parts = after(far_sends[0], down_parts)

    def far_sum(i, got):
        return call(
            functools.partial(far_sum_kernel, split), like(ends[i], 2 * units), far_keeps[i], got
        )

    got = swap(far_sends[0], group)
    far_head = swap(far_sum(0, got), group_far)
    got, near_send = after(swap(far_sends[1], group), near_send)
    far_rest = swap(far_sum(1, got), group_far)
    near_got = swap(near_send, group)
    downs = call(stack_kernel, like(planes, *down_parts[0].shape), *down_parts)
    weights = [downs, swap(downs, core), same]

    def ffn_out(start, part, dtypes):
        return call(
            functools.partial(down_kernel, start, planes, per, features),
            [like(planes, share, width, dtype=dtype) for dtype in dtypes],
            idx, keep, near_got, far_head, part, *weights,
        )

    late = ffn_out(split, far_head, [BF16, BF16])
    own, early = ffn_out(0, far_rest, [F32, BF16])
    rest = [early] + late
    parts = call(
        functools.partial(plane_sum_kernel, planes, tokens),
        [like(-(-(planes + 1) * tokens // ROW_TILE) * ROW_TILE, width)] * planes,
        idx, hidden, own, *[swap(x, b) for x, b in zip(rest, steps)],
    )
    return call(
        functools.partial(last_kernel, planes, tokens),
        like(tokens, features),
        idx, *across_planes(parts),
        scratch=[pltpu.VMEM((planes, rows, width), F32)],
    )


def tokens_can_travel(n_blk, n_uly, kv_heads, token_count, unit_count):
    def power(n):
        return n > 0 and not n & (n - 1)

    per = kv_heads // n_uly
    return (
        power(n_blk)
        and power(n_uly)
        and power(kv_heads)
        and per == 4
        and n_blk == 4 * per
        and token_count < unit_count // n_uly
    )


def solution(mesh):
    n_blk, n_uly = mesh.shape["blk"], mesh.shape["uly"]

    def per_device(*args):
        residual, key_projection, gate_weight = args[0], args[2], args[9]
        travel = tokens_can_travel(
            n_blk,
            n_uly,
            key_projection.shape[1] // HEAD_SIZE,
            residual.shape[0] * n_blk * n_uly,
            gate_weight.shape[1] * n_uly,
        )
        if travel:
            return move_tokens(n_blk, n_uly, *args)
        return move_weights(*args)

    return jax.shard_map(
        per_device,
        mesh=mesh,
        in_specs=(
            P(("blk", "uly"), None),
            P(("blk", "uly"), None),
            P(("blk", "uly"), None),
            P(("blk", "uly"), None),
            P(("blk", "uly"), None),
            P(),
            P(),
            P("uly", "blk"),
            P(),
            P("blk", "uly"),
            P("blk", "uly"),
            P("uly", "blk"),
        ),
        out_specs=P(("blk", "uly"), None),
        check_vma=False,
    )
```
